32 devices in a mesh: slides: 2 (over y), row: 16 (over z, x, core), col: 1.
Axes of the slice: x: 2, y: 2, z: 4, core: 2. Of those that a mesh axis runs over, the one named last changes fastest.
Arguments:
- features: bfloat16 [128, 64, 2048], P(('slides', 'row'), 'col'), parts along dimension 0, may hold values from -6 to 6
- write_vecs: bfloat16 [128, 64, 128], P(('slides', 'row'), 'col'), parts along dimension 0, may hold values from -6 to 6
- read_vecs: bfloat16 [128, 64, 128], P(('slides', 'row'), 'col'), parts along dimension 0, may hold values from -0.119628906 to 0.119628906
- row_decay: bfloat16 [128, 64, 32], P(('slides', 'row'), 'col'), parts along dimension 0, may hold values from -1 to 0, as said below
- col_decay: bfloat16 [128, 64, 32], P(('slides', 'row'), 'col'), parts along dimension 0, may hold values from -1 to 0, as said below
- tile_mask: int32 [128, 1], P(('slides', 'row'), 'col'), parts along dimension 0, may hold values 0 or 1
- skip_gain: float32 [32], replicated, may hold values from 0.5 to 2
Outputs:
- mixed: bfloat16 [128, 64, 2048], P(('slides', 'row'), 'col'), parts along dimension 0
The draws below stay inside these ranges and needn't reach their ends.
There are 2 independent parts, one for each index of `slides`. The reference program is written for one: setup_inputs(seed, part) draws one part's arguments, and reference() takes and returns one part's arrays. A program takes and returns all parts, laid end to end along the dimension named above; an argument that names none is the same for every part. Nothing has to cross between parts.
Inputs may be any that keep to these rules, and one draw needn't show every extreme that they name: `row_decay`: log decays of each patch and head along rows, never positive. `col_decay`: log decays of each patch and head along columns, never positive.
All inputs are finite; a program needn't handle non-finite values. No bound on the sum of `tile_mask` on one device may be relied on, other than what follows from the above.
Results may differ from the reference program's by a relative error of at most 0.005.
Values may be sent and summed in bfloat16 or wider, within the bound.
A program may use at most 128 MiB of HBM per device.

```python
import math
import jax
import jax.numpy as jnp
from jax import lax

HEADS = 32
HEAD_DIM = 64
STATE = 128
D_INNER = 2048
STRETCH = 64
ROWS = 64
COLS = 64


def decay_law(key, sequence_length, chain_dim, slow_share, uniform_factor):
    split_random_keys = jax.random.split(key, 6)
    slow_heads = jax.random.uniform(split_random_keys[0], (HEADS,)) < slow_share
    slow_rate = jnp.exp(jax.random.uniform(split_random_keys[1], (HEADS,), minval=math.log(0.1), maxval=math.log(0.5))) / sequence_length
    fast_rate = jax.random.uniform(split_random_keys[2], (HEADS,), minval=0.07, maxval=0.1)
    head_rates = jnp.where(slow_heads, slow_rate, fast_rate)
    if uniform_factor:
        factor = jax.random.uniform(split_random_keys[3], (ROWS, COLS, HEADS), minval=0.5, maxval=2.0)
    else:
        factor = jnp.exp(jax.random.uniform(split_random_keys[3], (ROWS, COLS, HEADS), minval=-0.7, maxval=0.7))
    dropout_locations = jax.random.permutation(split_random_keys[4], sequence_length)[:3]
    dropout_fraction = jax.random.uniform(split_random_keys[5], (3,), minval=0.22, maxval=0.69)
    target_slots = jnp.arange(sequence_length)
    dropout_events = jnp.sum(jnp.where(target_slots[:, None] == dropout_locations[None, :], dropout_fraction[None, :], 0.0), axis=1)
    if chain_dim == 0:
        scattered_tiles = dropout_events[:, None, None]
    else:
        scattered_tiles = dropout_events[None, :, None]
    return (-(head_rates * factor + scattered_tiles)).astype(jnp.float32).astype(jnp.bfloat16)


def draw_row_decay(key, part):
    return decay_law(jax.random.fold_in(key, 11), COLS, 1, 0.5, False)


def draw_col_decay(key, part):
    return decay_law(jax.random.fold_in(key, 23), ROWS, 0, 0.5, False)


def place_ends(result, rng, least, largest):
    index_at = [jax.random.randint(jax.random.fold_in(rng, axis), (), 0, length) for axis, length in enumerate(result.shape)]
    widest = result.shape.index(max(result.shape))
    neighbour = index_at[:widest] + [(index_at[widest] + 1) % result.shape[widest]] + index_at[widest + 1:]
    return result.at[tuple(index_at)].set(least).at[tuple(neighbour)].set(largest)


def block_levels(own_key, dims, cuts, least, largest):
    loudness, own = 1.0, jax.random.fold_in(own_key, 6)
    for position, parts in cuts:
        draws = jnp.exp(jax.random.uniform(jax.random.fold_in(own, position), (parts,), jnp.float32, least / len(cuts), largest / len(cuts)))
        loudness = loudness * jnp.repeat(draws, dims[position] // parts).reshape([-1 if axis == position else 1 for axis in range(len(dims))])
    return loudness


def normal_values(rng, extent, scale, limit, pieces=(), kind=jnp.bfloat16):
    result = scale * jax.random.normal(rng, extent, jnp.float32)
    if pieces:
        result = result * block_levels(rng, extent, pieces, -0.22, 0.18)
    return jnp.clip(result, -limit, limit).astype(kind)


def setup_inputs(seed: int = 0, part: int = 0) -> dict:
    arg_keys = jax.random.split(jax.random.key(seed), 8)
    own_keys = jax.random.split(jax.random.fold_in(arg_keys[7], part), 8)
    features = normal_values(own_keys[0], (ROWS, COLS, D_INNER), 1.0, 6.0, ((0, 16),))
    write_vecs = normal_values(own_keys[1], (ROWS, COLS, STATE), 1.0, 6.0, ((0, 16),))
    read_vecs = normal_values(own_keys[2], (ROWS, COLS, STATE), 0.02, 0.119628906, ((0, 16),))
    row_decay = draw_row_decay(jax.random.fold_in(jax.random.fold_in(arg_keys[7], part), 71), part)
    col_decay = draw_col_decay(jax.random.fold_in(jax.random.fold_in(arg_keys[7], part), 71), part)
    tile_mask = place_ends((jax.random.randint(own_keys[5], (ROWS, COLS // STRETCH), 0, 4) < 3).astype(jnp.int32), jax.random.fold_in(own_keys[5], 1), 0, 1)
    skip_gain = jnp.clip(jnp.exp(jax.random.uniform(arg_keys[6], (HEADS,), jnp.float32, math.log(0.5), math.log(2.0))), 0.5, 2.0)
    return dict(features=features, write_vecs=write_vecs, read_vecs=read_vecs, row_decay=row_decay, col_decay=col_decay, tile_mask=tile_mask, skip_gain=skip_gain)


def block_local(masked, write_vecs, read_vecs, decays):
    blocks, length, span_width = masked.shape
    head_count = decays.shape[-1]
    head_width = span_width // head_count
    running = jnp.swapaxes(jnp.cumsum(decays.astype(jnp.float32), axis=1), 1, 2)
    scores = jnp.einsum('ktn,ksn->kts', read_vecs.astype(jnp.float32), write_vecs.astype(jnp.float32))
    target_slots = jnp.arange(length)
    causal = target_slots[:, None] >= target_slots[None, :]
    spread = jnp.where(causal, running[:, :, :, None] - running[:, :, None, :], jnp.float32(0.0))
    weights = jnp.where(causal, scores[:, None] * jnp.exp(spread), jnp.float32(0.0)).astype(jnp.bfloat16)
    values = masked.reshape(blocks, length, head_count, head_width).astype(jnp.float32)
    inside = jnp.einsum('khts,kshp->kthp', weights.astype(jnp.float32), values)
    closing = running[:, :, -1]
    scaled = (write_vecs.astype(jnp.float32)[:, None] * jnp.exp(closing[:, :, None] - running)[..., None]).astype(jnp.bfloat16)
    block_state = jnp.einsum('khsn,kshp->khnp', scaled.astype(jnp.float32), values)
    return inside, block_state, jnp.exp(closing), running


def chain_pass(masked, write_vecs, read_vecs, decays):
    inside, block_state, damping, running = block_local(masked, write_vecs, read_vecs, decays)

    def advance(carry_state, element):
        factor, fresh_term = element
        return factor[:, None, None] * carry_state + fresh_term, carry_state

    zero_state = jnp.zeros(block_state.shape[1:], jnp.float32)
    closing_state, entering = lax.scan(advance, zero_state, (damping, block_state))
    carried = jnp.einsum('ktn,khnp->kthp', read_vecs.astype(jnp.float32), entering, precision=lax.Precision.HIGHEST)
    carried = carried * jnp.swapaxes(jnp.exp(running), 1, 2)[..., None]
    total = inside + carried
    return total.reshape(total.shape[0] * total.shape[1], total.shape[2] * total.shape[3])


def chains(masked, write_vecs, read_vecs, decays):
    chain_count, sequence_length = masked.shape[0], masked.shape[1]

    def to_blocks(array):
        return array.reshape(chain_count, sequence_length // STRETCH, STRETCH, array.shape[-1])

    return jax.vmap(chain_pass)(to_blocks(masked), to_blocks(write_vecs), to_blocks(read_vecs), to_blocks(decays))


def grouped(function, arrays):
    chain_count = arrays[0].shape[0]
    packed = tuple(array.reshape((chain_count // 8, 8) + array.shape[1:]) for array in arrays)
    results = lax.map(lambda group: function(*group), packed)
    return results.reshape((chain_count,) + results.shape[2:])


def reference(features, write_vecs, read_vecs, row_decay, col_decay, tile_mask, skip_gain):
    patch_mask = jnp.repeat(tile_mask, STRETCH, axis=1)
    masked = jnp.where(patch_mask[..., None] > 0, features, jnp.zeros((), features.dtype))

    def column_work(masked_c, write_c, read_c, decay_c):
        return chains(masked_c, write_c, read_c, decay_c).astype(jnp.bfloat16)

    flipped = tuple(jnp.swapaxes(array, 0, 1) for array in (masked, write_vecs, read_vecs, col_decay))
    col_out = jnp.swapaxes(grouped(column_work, flipped), 0, 1)
    skip_vector = jnp.repeat(skip_gain, HEAD_DIM)

    def row_work(masked_r, write_r, read_r, decay_r, column_r, feature_r, mask_r):
        y_row = chains(masked_r, write_r, read_r, decay_r)
        total = y_row + column_r.astype(jnp.float32) + skip_vector * feature_r.astype(jnp.float32)
        return (mask_r[..., None].astype(jnp.float32) * total).astype(jnp.bfloat16)

    return grouped(row_work, (masked, write_vecs, read_vecs, row_decay, col_out, features, patch_mask))
```

```python
import functools

import jax
import jax.numpy as jnp
from jax import lax
from jax.experimental import pallas as pl
from jax.experimental.pallas import tpu as pltpu
from jax.sharding import PartitionSpec as P


def entering_2(array, axis, combine, identity):
    devices, here = (lax.axis_size(axis), lax.axis_index(axis))
    everything = jax.tree.map(
        lambda part, kind: lax.all_gather(part.astype(kind), axis),
        array,
        (jnp.bfloat16, jnp.bfloat16),
    )
    start = jax.tree.map(
        lambda part, zero: jnp.broadcast_to(jnp.asarray(zero, part.dtype), part.shape),
        array,
        identity,
    )

    def step(k, before):
        reached = k < here
        new = combine(
            before, jax.tree.map(lambda part, own: part[k].astype(own.dtype), everything, array)
        )
        return jax.tree.map(lambda a, b: jnp.where(reached, a, b), new, before)

    return lax.fori_loop(0, devices, step, start)


def block_local(masked, write_vecs, read_vecs, decays):
    blocks, length, span_width = masked.shape
    head_count = decays.shape[-1]
    head_width = span_width // head_count
    slots = jnp.arange(length)
    upto = (slots[:, None] >= slots[None, :]).astype(decays.dtype)
    running = jnp.einsum("ts,ksh->kht", upto, decays, preferred_element_type=jnp.float32)
    scores = jnp.einsum("ktn,ksn->kts", read_vecs, write_vecs, preferred_element_type=jnp.float32)
    target_slots = jnp.arange(length)
    causal = target_slots[:, None] >= target_slots[None, :]
    spread = jnp.where(causal, running[:, :, :, None] - running[:, :, None, :], jnp.float32(0.0))
    weights = jnp.where(causal, scores[:, None] * jnp.exp(spread), jnp.float32(0.0)).astype(
        jnp.bfloat16
    )
    values = masked.reshape(blocks, length, head_count, head_width)
    inside = jnp.einsum("khts,kshp->kthp", weights, values, preferred_element_type=jnp.float32)
    closing = running[:, :, -1]
    scaled = (
        write_vecs.astype(jnp.float32)[:, None] * jnp.exp(closing[:, :, None] - running)[..., None]
    ).astype(jnp.bfloat16)
    block_state = jnp.einsum("khsn,kshp->khnp", scaled, values, preferred_element_type=jnp.float32)
    return (inside, block_state, jnp.exp(closing), running)


def enter_states(damping, block_state, initial):

    def advance(carry_state, element):
        factor, fresh_term = element
        return (factor[:, None, None] * carry_state + fresh_term, carry_state)

    return lax.scan(advance, initial, (damping, block_state))


def combine_out(inside, entering, read_blocks, running):
    carried = jnp.einsum(
        "ktn,khnp->kthp", read_blocks.astype(jnp.float32), entering, precision=lax.Precision.HIGHEST
    )
    total = inside + carried * jnp.swapaxes(jnp.exp(running), 1, 2)[..., None]
    return total.reshape(total.shape[0] * total.shape[1], total.shape[2] * total.shape[3])


def to_blocks(array, block_len):
    return array.reshape(
        array.shape[:-2] + (array.shape[-2] // block_len, block_len, array.shape[-1])
    )


def column_chains(masked, write_vecs, read_vecs, decays, block_len):

    def one_column(masked_c, write_c, read_c, decay_c):
        read_blocks = to_blocks(read_c, block_len)
        inside, block_state, damping, running = block_local(
            to_blocks(masked_c, block_len),
            to_blocks(write_c, block_len),
            read_blocks,
            to_blocks(decay_c, block_len),
        )
        if read_blocks.shape[0] == 1:
            return inside.reshape(masked_c.shape)
        zero_state = jnp.zeros(block_state.shape[1:], jnp.float32)
        closing_state, entering = enter_states(damping, block_state, zero_state)
        return combine_out(inside, entering, read_blocks, running)

    results = jax.vmap(one_column, in_axes=1, out_axes=1)(masked, write_vecs, read_vecs, decays)
    return results.astype(jnp.bfloat16)


def row_terms(masked, write_vecs, read_vecs, decays, block_len):
    read_blocks = to_blocks(read_vecs, block_len)
    local_terms = jax.vmap(block_local)(
        to_blocks(masked, block_len),
        to_blocks(write_vecs, block_len),
        read_blocks,
        to_blocks(decays, block_len),
    )
    return (local_terms, read_blocks)


def row_finish(local_terms, read_blocks, incoming):
    inside, block_state, damping, running = local_terms
    closing_state, entering = jax.vmap(enter_states)(damping, block_state, incoming)
    return jax.vmap(combine_out)(inside, entering, read_blocks, running)


def link(earlier, later):
    return (earlier[0] * later[0], later[0][..., None, None] * earlier[1] + later[1])


MESH = pl.DeviceIdType.MESH
CHUNKS = 4


def fused_kernel(
    shape,
    mask_ref,
    skip_ref,
    x_hbm,
    write_hbm,
    read_hbm,
    row_hbm,
    col_hbm,
    out_ref,
    x_ref,
    write_ref,
    read_ref,
    row_ref,
    col_ref,
    aux_out,
    aux_in,
    sent,
    got,
    col_sent,
    col_got,
    total,
    grow,
    fade,
    load_sems,
    x_sems,
    aux_sems,
    there_sems,
    back_sems,
):
    devices, tile_rows, tile_cols, heads = shape
    per = tile_cols // devices
    block = tile_rows * per
    patches = tile_rows * tile_cols
    chunks, _, width = sent.shape
    head_width = chunks * width // heads
    state = write_ref.shape[-1]
    f32, bf16 = jnp.float32, jnp.bfloat16
    me = lax.axis_index("row")
    own = pl.ds(pl.multiple_of(me * block, block), block)

    def dot(a, b):
        return jnp.dot(a, b, preferred_element_type=f32)

    def peer(step):
        return lax.rem(me + 1 + step, devices)

    barrier = pltpu.get_barrier_semaphore()

    def greet(step, carry):
        pl.semaphore_signal(barrier, inc=1, device_id={"row": peer(step)}, device_id_type=MESH)
        return carry

    lax.fori_loop(0, devices - 1, greet, 0)
    loads = [
        pltpu.make_async_copy(source, target, load_sems.at[i])
        for i, (source, target) in enumerate(
            ((write_hbm, write_ref), (read_hbm, read_ref), (col_hbm, col_ref), (row_hbm, row_ref))
        )
    ]
    x_loads = [
        pltpu.make_async_copy(
            x_hbm.at[:, pl.ds(c * width, width)], x_ref.at[:, pl.ds(c * width, width)], x_sems.at[c]
        )
        for c in range(chunks)
    ]
    for load in loads[:3] + x_loads + loads[3:]:
        load.start()

    def scatter(source, target, sems):
        def send(step, carry):
            other = peer(step)
            pltpu.make_async_remote_copy(
                src_ref=source.at[pl.ds(pl.multiple_of(other * block, block), block)],
                dst_ref=target.at[own],
                send_sem=sems.at[0],
                recv_sem=sems.at[1],
                device_id={"row": other},
                device_id_type=MESH,
            ).start()
            return carry

        lax.fori_loop(0, devices - 1, send, 0)
        target[own, :] = source[own, :]

    def wait(buffer, sem):
        part = buffer.at[pl.ds(0, block * (devices - 1))]
        pltpu.make_async_copy(part, part, sem).wait()

    def shift(i, size):
        return lax.shift_right_logical(i, size.bit_length() - 1)

    down = lax.broadcasted_iota(jnp.int32, (patches, 1), 0)
    across = lax.broadcasted_iota(jnp.int32, (1, patches), 1)

    def home(i):
        row = shift(i, per) & (tile_rows - 1)
        return row * tile_cols + shift(i, block) * per + (i & (per - 1))

    def ones(where):
        return where.astype(f32).astype(bf16)

    from_home = home(down)
    order = ones(from_home == across)

    def turned(places, ref):
        lanes = lax.broadcasted_iota(jnp.int32, (1, tile_cols), 1)
        return sum(
            lax.dot_general(
                ones(places == lanes + r * tile_cols),
                ref[r],
                (((1,), (1,)), ((), ())),
                preferred_element_type=f32,
            )
            for r in range(tile_rows)
        ).astype(bf16)

    tile = [mask_ref[r].astype(f32) for r in range(tile_rows)]

    def keep(value):
        return jnp.concatenate(
            [value[r * tile_cols : (r + 1) * tile_cols] * tile[r] for r in range(tile_rows)]
        )

    aux_out[:, 2 * state :] = jnp.zeros((patches, aux_out.shape[1] - 2 * state), bf16)
    for load in loads[:3]:
        load.wait()
    aux_out[:, :state] = dot(order, write_ref[...]).astype(bf16)
    aux_out[:, state : 2 * state] = dot(order, read_ref[...]).astype(bf16)
    aux_out[:, 2 * state : 2 * state + heads] = turned(from_home, col_ref)
    pl.semaphore_wait(barrier, devices - 1)
    scatter(aux_out, aux_in, aux_sems)

    def masked(c):
        return keep(x_ref[:, c * width : (c + 1) * width].astype(f32)).astype(bf16)

    for c in range(chunks):
        x_loads[c].wait()
        sent[c] = dot(order, masked(c)).astype(bf16)
        scatter(sent.at[c], got.at[c], there_sems.at[c])

    def spread(c):
        head = lax.broadcasted_iota(jnp.int32, (heads, width), 0)
        lane = lax.broadcasted_iota(jnp.int32, (heads, width), 1)
        return (head == shift(lane + c * width, head_width)).astype(f32)

    def running(below, decays, c):
        return dot(below, dot(decays, spread(c).astype(bf16)).astype(bf16))

    def causal(reads, writes, allowed):
        scores = lax.dot_general(
            reads, writes, (((1,), (1,)), ((), ())), preferred_element_type=f32
        )
        return jnp.where(allowed, scores, 0.0).astype(bf16)

    restore = ones(down == home(across))
    in_row = (down >= across) & (shift(down, tile_cols) == shift(across, tile_cols))
    row_below = ones(in_row)
    loads[3].wait()
    row_decays = turned(down, row_ref)
    row_scores = causal(read_ref[...], write_ref[...], in_row)
    skip = jnp.broadcast_to(skip_ref[...], (8, heads))
    for c in range(chunks):
        cut = slice(c * width, (c + 1) * width)
        run = running(row_below, row_decays, c)
        faded = (masked(c).astype(f32) * jnp.exp(-run)).astype(bf16)
        gain = jnp.dot(
            skip, spread(c), precision=lax.Precision.HIGHEST, preferred_element_type=f32
        )[:1]
        total[:, cut] = jnp.exp(run) * dot(row_scores, faded) + gain * x_ref[:, cut].astype(f32)

    in_col = (down >= across) & ((down & (per - 1)) == (across & (per - 1)))
    col_below = ones(in_col)
    wait(aux_in, aux_sems.at[1])
    col_scores = causal(aux_in[:, state : 2 * state], aux_in[:, :state], in_col)
    for c in range(chunks):
        run = running(col_below, aux_in[:, 2 * state : 2 * state + heads], c)
        grow[c] = jnp.exp(run)
        fade[c] = jnp.exp(-run)

    for c in range(chunks):
        wait(got.at[c], there_sems.at[c, 1])
        faded = (got[c].astype(f32) * fade[c]).astype(bf16)
        col_sent[c] = (grow[c] * dot(col_scores, faded)).astype(bf16)
        scatter(col_sent.at[c], col_got.at[c], back_sems.at[c])

    for c in range(chunks):
        cut = slice(c * width, (c + 1) * width)
        wait(col_got.at[c], back_sems.at[c, 1])
        out_ref[:, cut] = keep(total[:, cut] + dot(restore, col_got[c])).astype(bf16)

    wait(aux_out, aux_sems.at[0])
    for c in range(chunks):
        wait(sent.at[c], there_sems.at[c, 0])
        wait(col_sent.at[c], back_sems.at[c, 0])


def fused(features, write_vecs, read_vecs, row_decay, col_decay, tile_mask, skip_gain):
    tile_rows, tile_cols, span_width = features.shape
    heads, state = row_decay.shape[-1], write_vecs.shape[-1]
    patches = tile_rows * tile_cols
    devices = lax.axis_size("row")
    width = span_width // CHUNKS

    def flat(array):
        return array.reshape(patches, array.shape[-1])

    vmem = pl.BlockSpec(memory_space=pltpu.VMEM)
    piece = (CHUNKS, patches, width)
    aux = pltpu.VMEM((patches, 2 * state + 128), jnp.bfloat16)
    result = pl.pallas_call(
        functools.partial(fused_kernel, (devices, tile_rows, tile_cols, heads)),
        out_shape=pltpu.VMEM((patches, span_width), jnp.bfloat16),
        in_specs=[pl.BlockSpec(memory_space=pltpu.SMEM), vmem]
        + [pl.BlockSpec(memory_space=pl.ANY)] * 5,
        out_specs=vmem,
        scratch_shapes=[
            pltpu.VMEM((patches, span_width), jnp.bfloat16),
            pltpu.VMEM((patches, state), jnp.bfloat16),
            pltpu.VMEM((patches, state), jnp.bfloat16),
            pltpu.VMEM((tile_rows, heads, tile_cols), jnp.bfloat16),
            pltpu.VMEM((tile_rows, heads, tile_cols), jnp.bfloat16),
            aux,
            aux,
            pltpu.VMEM(piece, jnp.bfloat16),
            pltpu.VMEM(piece, jnp.bfloat16),
            pltpu.VMEM(piece, jnp.bfloat16),
            pltpu.VMEM(piece, jnp.bfloat16),
            pltpu.VMEM((patches, span_width), jnp.float32),
            pltpu.VMEM(piece, jnp.float32),
            pltpu.VMEM(piece, jnp.float32),
            pltpu.SemaphoreType.DMA((4,)),
            pltpu.SemaphoreType.DMA((CHUNKS,)),
            pltpu.SemaphoreType.DMA((2,)),
            pltpu.SemaphoreType.DMA((CHUNKS, 2)),
            pltpu.SemaphoreType.DMA((CHUNKS, 2)),
        ],
        compiler_params=pltpu.CompilerParams(
            collective_id=0, has_side_effects=True, vmem_limit_bytes=60 * 2**20
        ),
    )(
        tile_mask.reshape(-1),
        skip_gain.reshape(1, heads),
        flat(features),
        flat(write_vecs),
        flat(read_vecs),
        jnp.swapaxes(row_decay, 1, 2),
        jnp.swapaxes(col_decay, 1, 2),
    )
    return result.reshape(features.shape)


def fits_fused(features, row_decay, tile_mask):
    tile_rows, tile_cols, span_width = features.shape
    devices = lax.axis_size("row")
    return (
        lax.axis_size("col") == 1
        and tile_mask.shape[1] == 1
        and tile_rows * devices == tile_cols
        and tile_cols <= 64
        and (tile_rows * (tile_cols // devices)) % 16 == 0
        and span_width % (CHUNKS * 128) == 0
        and row_decay.shape[-1] <= 128
        and all(
            size.bit_count() == 1
            for size in (tile_rows, tile_cols, devices, span_width // row_decay.shape[-1])
        )
    )


def per_device(features, write_vecs, read_vecs, row_decay, col_decay, tile_mask, skip_gain):
    tile_rows, tile_cols, span_width = features.shape
    if fits_fused(features, row_decay, tile_mask):
        return fused(features, write_vecs, read_vecs, row_decay, col_decay, tile_mask, skip_gain)
    head_count = row_decay.shape[-1]
    block_len = tile_cols // tile_mask.shape[1]
    patch_mask = jnp.repeat(tile_mask, block_len, axis=1)
    masked = jnp.where(patch_mask[..., None] > 0, features, jnp.zeros((), features.dtype))
    moved = (
        lax.all_to_all(masked, "row", split_axis=1, concat_axis=0, tiled=True),
        lax.all_to_all(write_vecs, "row", split_axis=1, concat_axis=0, tiled=True),
        lax.all_to_all(read_vecs, "row", split_axis=1, concat_axis=0, tiled=True),
        lax.all_to_all(col_decay, "row", split_axis=1, concat_axis=0, tiled=True),
    )
    result = column_chains(moved[0], moved[1], moved[2], moved[3], block_len)
    col_out = lax.all_to_all(result, "row", split_axis=0, concat_axis=1, tiled=True)
    local_terms, read_blocks = row_terms(masked, write_vecs, read_vecs, row_decay, block_len)
    if lax.axis_size("col") == 1 and tile_mask.shape[1] == 1:
        y_row = local_terms[0].reshape(features.shape)
    else:
        zero_states = jnp.zeros((tile_rows,) + local_terms[1].shape[2:], jnp.float32)
        closing_states, unused_states = jax.vmap(enter_states)(
            local_terms[2], local_terms[1], zero_states
        )
        device_decay = jnp.prod(local_terms[2], axis=1)
        identity = (jnp.ones_like(device_decay), jnp.zeros_like(closing_states))
        decay_before, state_before = entering_2((device_decay, closing_states), "col", link, identity)
        y_row = row_finish(local_terms, read_blocks, state_before)
    skip_vector = jnp.repeat(skip_gain, span_width // head_count)
    total = y_row + col_out.astype(jnp.float32) + skip_vector * features.astype(jnp.float32)
    return (patch_mask[..., None].astype(jnp.float32) * total).astype(jnp.bfloat16)


def solution(mesh):
    return jax.shard_map(
        per_device,
        mesh=mesh,
        in_specs=(
            P(("slides", "row"), "col", None),
            P(("slides", "row"), "col", None),
            P(("slides", "row"), "col", None),
            P(("slides", "row"), "col", None),
            P(("slides", "row"), "col", None),
            P(("slides", "row"), "col"),
            P(),
        ),
        out_specs=P(("slides", "row"), "col", None),
        check_vma=False,
    )
```

```python
import functools

import jax
import jax.numpy as jnp
from jax import lax
from jax.experimental import pallas as pl
from jax.experimental.pallas import tpu as pltpu
from jax.sharding import PartitionSpec as P


def entering_2(array, axis, combine, identity):
    devices, here = (lax.axis_size(axis), lax.axis_index(axis))
    everything = jax.tree.map(
        lambda part, kind: lax.all_gather(part.astype(kind), axis),
        array,
        (jnp.bfloat16, jnp.bfloat16),
    )
    start = jax.tree.map(
        lambda part, zero: jnp.broadcast_to(jnp.asarray(zero, part.dtype), part.shape),
        array,
        identity,
    )

    def step(k, before):
        reached = k < here
        new = combine(
            before, jax.tree.map(lambda part, own: part[k].astype(own.dtype), everything, array)
        )
        return jax.tree.map(lambda a, b: jnp.where(reached, a, b), new, before)

    return lax.fori_loop(0, devices, step, start)


def block_local(masked, write_vecs, read_vecs, decays):
    blocks, length, span_width = masked.shape
    head_count = decays.shape[-1]
    head_width = span_width // head_count
    slots = jnp.arange(length)
    upto = (slots[:, None] >= slots[None, :]).astype(decays.dtype)
    running = jnp.einsum("ts,ksh->kht", upto, decays, preferred_element_type=jnp.float32)
    scores = jnp.einsum("ktn,ksn->kts", read_vecs, write_vecs, preferred_element_type=jnp.float32)
    target_slots = jnp.arange(length)
    causal = target_slots[:, None] >= target_slots[None, :]
    spread = jnp.where(causal, running[:, :, :, None] - running[:, :, None, :], jnp.float32(0.0))
    weights = jnp.where(causal, scores[:, None] * jnp.exp(spread), jnp.float32(0.0)).astype(
        jnp.bfloat16
    )
    values = masked.reshape(blocks, length, head_count, head_width)
    inside = jnp.einsum("khts,kshp->kthp", weights, values, preferred_element_type=jnp.float32)
    closing = running[:, :, -1]
    scaled = (
        write_vecs.astype(jnp.float32)[:, None] * jnp.exp(closing[:, :, None] - running)[..., None]
    ).astype(jnp.bfloat16)
    block_state = jnp.einsum("khsn,kshp->khnp", scaled, values, preferred_element_type=jnp.float32)
    return (inside, block_state, jnp.exp(closing), running)


def enter_states(damping, block_state, initial):

    def advance(carry_state, element):
        factor, fresh_term = element
        return (factor[:, None, None] * carry_state + fresh_term, carry_state)

    return lax.scan(advance, initial, (damping, block_state))


def combine_out(inside, entering, read_blocks, running):
    carried = jnp.einsum(
        "ktn,khnp->kthp", read_blocks.astype(jnp.float32), entering, precision=lax.Precision.HIGHEST
    )
    total = inside + carried * jnp.swapaxes(jnp.exp(running), 1, 2)[..., None]
    return total.reshape(total.shape[0] * total.shape[1], total.shape[2] * total.shape[3])


def to_blocks(array, block_len):
    return array.reshape(
        array.shape[:-2] + (array.shape[-2] // block_len, block_len, array.shape[-1])
    )


def column_chains(masked, write_vecs, read_vecs, decays, block_len):

    def one_column(masked_c, write_c, read_c, decay_c):
        read_blocks = to_blocks(read_c, block_len)
        inside, block_state, damping, running = block_local(
            to_blocks(masked_c, block_len),
            to_blocks(write_c, block_len),
            read_blocks,
            to_blocks(decay_c, block_len),
        )
        if read_blocks.shape[0] == 1:
            return inside.reshape(masked_c.shape)
        zero_state = jnp.zeros(block_state.shape[1:], jnp.float32)
        closing_state, entering = enter_states(damping, block_state, zero_state)
        return combine_out(inside, entering, read_blocks, running)

    results = jax.vmap(one_column, in_axes=1, out_axes=1)(masked, write_vecs, read_vecs, decays)
    return results.astype(jnp.bfloat16)


def row_terms(masked, write_vecs, read_vecs, decays, block_len):
    read_blocks = to_blocks(read_vecs, block_len)
    local_terms = jax.vmap(block_local)(
        to_blocks(masked, block_len),
        to_blocks(write_vecs, block_len),
        read_blocks,
        to_blocks(decays, block_len),
    )
    return (local_terms, read_blocks)


def row_finish(local_terms, read_blocks, incoming):
    inside, block_state, damping, running = local_terms
    closing_state, entering = jax.vmap(enter_states)(damping, block_state, incoming)
    return jax.vmap(combine_out)(inside, entering, read_blocks, running)


def link(earlier, later):
    return (earlier[0] * later[0], later[0][..., None, None] * earlier[1] + later[1])


MESH = pl.DeviceIdType.MESH
CHUNKS = 4


def fused_kernel(
    shape,
    mask_hbm,
    skip_hbm,
    x_hbm,
    write_hbm,
    read_hbm,
    row_hbm,
    col_hbm,
    out_ref,
    mask_ref,
    skip_ref,
    x_ref,
    write_ref,
    read_ref,
    row_ref,
    col_ref,
    aux_out,
    aux_in,
    sent,
    got,
    col_sent,
    col_got,
    total,
    grow,
    fade,
    load_sems,
    x_sems,
    aux_sems,
    there_sems,
    back_sems,
):
    devices, tile_rows, tile_cols, heads = shape
    per = tile_cols // devices
    block = tile_rows * per
    patches = tile_rows * tile_cols
    chunks, _, width = sent.shape
    head_width = chunks * width // heads
    state = write_ref.shape[-1]
    f32, bf16 = jnp.float32, jnp.bfloat16
    me = lax.axis_index("row")
    own = pl.ds(pl.multiple_of(me * block, block), block)

    def dot(a, b):
        return jnp.dot(a, b, preferred_element_type=f32)

    def peer(step):
        return lax.rem(me + 1 + step, devices)

    barrier = pltpu.get_barrier_semaphore()

    def greet(step, carry):
        pl.semaphore_signal(barrier, inc=1, device_id={"row": peer(step)}, device_id_type=MESH)
        return carry

    lax.fori_loop(0, devices - 1, greet, 0)
    loads = [
        pltpu.make_async_copy(source, target, load_sems.at[i])
        for i, (source, target) in enumerate(
            (
                (mask_hbm, mask_ref),
                (write_hbm, write_ref),
                (read_hbm, read_ref),
                (col_hbm, col_ref),
                (row_hbm, row_ref),
                (skip_hbm, skip_ref),
            )
        )
    ]
    x_loads = [
        pltpu.make_async_copy(
            x_hbm.at[:, pl.ds(c * width, width)], x_ref.at[:, pl.ds(c * width, width)], x_sems.at[c]
        )
        for c in range(chunks)
    ]
    for load in loads[:4] + x_loads + loads[4:]:
        load.start()

    def scatter(source, target, sems):
        def send(step, carry):
            other = peer(step)
            pltpu.make_async_remote_copy(
                src_ref=source.at[pl.ds(pl.multiple_of(other * block, block), block)],
                dst_ref=target.at[own],
                send_sem=sems.at[0],
                recv_sem=sems.at[1],
                device_id={"row": other},
                device_id_type=MESH,
            ).start()
            return carry

        lax.fori_loop(0, devices - 1, send, 0)
        target[own, :] = source[own, :]

    def wait(buffer, sem):
        part = buffer.at[pl.ds(0, block * (devices - 1))]
        pltpu.make_async_copy(part, part, sem).wait()

    def shift(i, size):
        return lax.shift_right_logical(i, size.bit_length() - 1)

    down = lax.broadcasted_iota(jnp.int32, (patches, 1), 0)
    across = lax.broadcasted_iota(jnp.int32, (1, patches), 1)

    def home(i):
        row = shift(i, per) & (tile_rows - 1)
        return row * tile_cols + shift(i, block) * per + (i & (per - 1))

    def ones(where):
        return where.astype(f32).astype(bf16)

    from_home = home(down)
    order = ones(from_home == across)

    def turned(places, ref):
        lanes = lax.broadcasted_iota(jnp.int32, (1, tile_cols), 1)
        return sum(
            lax.dot_general(
                ones(places == lanes + r * tile_cols),
                ref[r],
                (((1,), (1,)), ((), ())),
                preferred_element_type=f32,
            )
            for r in range(tile_rows)
        ).astype(bf16)

    aux_out[:, 2 * state :] = jnp.zeros((patches, aux_out.shape[1] - 2 * state), bf16)
    for load in loads[:4]:
        load.wait()
    tile = [mask_ref[r].astype(f32) for r in range(tile_rows)]

    def keep(value):
        return jnp.concatenate(
            [value[r * tile_cols : (r + 1) * tile_cols] * tile[r] for r in range(tile_rows)]
        )

    aux_out[:, :state] = dot(order, keep(write_ref[...].astype(f32)).astype(bf16)).astype(bf16)
    aux_out[:, state : 2 * state] = dot(order, read_ref[...]).astype(bf16)
    aux_out[:, 2 * state : 2 * state + heads] = turned(from_home, col_ref)
    pl.semaphore_wait(barrier, devices - 1)
    scatter(aux_out, aux_in, aux_sems)

    for c in range(chunks):
        x_loads[c].wait()
        sent[c] = dot(order, x_ref[:, c * width : (c + 1) * width]).astype(bf16)
        scatter(sent.at[c], got.at[c], there_sems.at[c])

    def spread(c):
        head = lax.broadcasted_iota(jnp.int32, (heads, width), 0)
        lane = lax.broadcasted_iota(jnp.int32, (heads, width), 1)
        return (head == shift(lane + c * width, head_width)).astype(f32)

    def running(below, decays, c):
        return dot(below, dot(decays, spread(c).astype(bf16)).astype(bf16))

    def causal(reads, writes, allowed):
        scores = lax.dot_general(
            reads, writes, (((1,), (1,)), ((), ())), preferred_element_type=f32
        )
        return jnp.where(allowed, scores, 0.0).astype(bf16)

    restore = ones(down == home(across))
    in_row = (down >= across) & (shift(down, tile_cols) == shift(across, tile_cols))
    row_below = ones(in_row)
    for load in loads[4:]:
        load.wait()
    row_decays = turned(down, row_ref)
    row_scores = causal(read_ref[...], write_ref[...], in_row)
    skip = jnp.broadcast_to(skip_ref[...], (8, heads))
    for c in range(chunks):
        cut = slice(c * width, (c + 1) * width)
        run = running(row_below, row_decays, c)
        faded = (x_ref[:, cut].astype(f32) * jnp.exp(-run)).astype(bf16)
        gain = jnp.dot(
            skip, spread(c), precision=lax.Precision.HIGHEST, preferred_element_type=f32
        )[:1]
        total[:, cut] = jnp.exp(run) * dot(row_scores, faded) + gain * x_ref[:, cut].astype(f32)

    in_col = (down >= across) & ((down & (per - 1)) == (across & (per - 1)))
    col_below = ones(in_col)
    wait(aux_in, aux_sems.at[1])
    col_scores = causal(aux_in[:, state : 2 * state], aux_in[:, :state], in_col)
    for c in range(chunks):
        run = running(col_below, aux_in[:, 2 * state : 2 * state + heads], c)
        grow[c] = jnp.exp(run)
        fade[c] = jnp.exp(-run)

    for c in range(chunks):
        wait(got.at[c], there_sems.at[c, 1])
        faded = (got[c].astype(f32) * fade[c]).astype(bf16)
        col_sent[c] = (grow[c] * dot(col_scores, faded)).astype(bf16)
        scatter(col_sent.at[c], col_got.at[c], back_sems.at[c])

    for c in range(chunks):
        cut = slice(c * width, (c + 1) * width)
        wait(col_got.at[c], back_sems.at[c, 1])
        out_ref[:, cut] = keep(total[:, cut] + dot(restore, col_got[c])).astype(bf16)

    wait(aux_out, aux_sems.at[0])
    for c in range(chunks):
        wait(sent.at[c], there_sems.at[c, 0])
        wait(col_sent.at[c], back_sems.at[c, 0])


def fused(features, write_vecs, read_vecs, row_decay, col_decay, tile_mask, skip_gain):
    tile_rows, tile_cols, span_width = features.shape
    heads, state = row_decay.shape[-1], write_vecs.shape[-1]
    patches = tile_rows * tile_cols
    devices = lax.axis_size("row")
    width = span_width // CHUNKS

    def flat(array):
        return array.reshape(patches, array.shape[-1])

    vmem = pl.BlockSpec(memory_space=pltpu.VMEM)
    piece = (CHUNKS, patches, width)
    aux = pltpu.VMEM((patches, 2 * state + 128), jnp.bfloat16)
    result = pl.pallas_call(
        functools.partial(fused_kernel, (devices, tile_rows, tile_cols, heads)),
        out_shape=pltpu.VMEM((patches, span_width), jnp.bfloat16),
        in_specs=[pl.BlockSpec(memory_space=pl.ANY)] * 7,
        out_specs=vmem,
        scratch_shapes=[
            pltpu.SMEM((tile_rows,), jnp.int32),
            pltpu.VMEM((1, heads), jnp.float32),
            pltpu.VMEM((patches, span_width), jnp.bfloat16),
            pltpu.VMEM((patches, state), jnp.bfloat16),
            pltpu.VMEM((patches, state), jnp.bfloat16),
            pltpu.VMEM((tile_rows, heads, tile_cols), jnp.bfloat16),
            pltpu.VMEM((tile_rows, heads, tile_cols), jnp.bfloat16),
            aux,
            aux,
            pltpu.VMEM(piece, jnp.bfloat16),
            pltpu.VMEM(piece, jnp.bfloat16),
            pltpu.VMEM(piece, jnp.bfloat16),
            pltpu.VMEM(piece, jnp.bfloat16),
            pltpu.VMEM((patches, span_width), jnp.float32),
            pltpu.VMEM(piece, jnp.float32),
            pltpu.VMEM(piece, jnp.float32),
            pltpu.SemaphoreType.DMA((6,)),
            pltpu.SemaphoreType.DMA((CHUNKS,)),
            pltpu.SemaphoreType.DMA((2,)),
            pltpu.SemaphoreType.DMA((CHUNKS, 2)),
            pltpu.SemaphoreType.DMA((CHUNKS, 2)),
        ],
        compiler_params=pltpu.CompilerParams(
            collective_id=0, has_side_effects=True, vmem_limit_bytes=60 * 2**20
        ),
    )(
        tile_mask.reshape(-1),
        skip_gain.reshape(1, heads),
        flat(features),
        flat(write_vecs),
        flat(read_vecs),
        jnp.swapaxes(row_decay, 1, 2),
        jnp.swapaxes(col_decay, 1, 2),
    )
    return result.reshape(features.shape)


def fits_fused(features, row_decay, tile_mask):
    tile_rows, tile_cols, span_width = features.shape
    devices = lax.axis_size("row")
    return (
        lax.axis_size("col") == 1
        and tile_mask.shape[1] == 1
        and tile_rows * devices == tile_cols
        and tile_cols <= 64
        and (tile_rows * (tile_cols // devices)) % 16 == 0
        and span_width % (CHUNKS * 128) == 0
        and row_decay.shape[-1] <= 128
        and all(
            size.bit_count() == 1
            for size in (tile_rows, tile_cols, devices, span_width // row_decay.shape[-1])
        )
    )


def per_device(features, write_vecs, read_vecs, row_decay, col_decay, tile_mask, skip_gain):
    tile_rows, tile_cols, span_width = features.shape
    if fits_fused(features, row_decay, tile_mask):
        return fused(features, write_vecs, read_vecs, row_decay, col_decay, tile_mask, skip_gain)
    head_count = row_decay.shape[-1]
    block_len = tile_cols // tile_mask.shape[1]
    patch_mask = jnp.repeat(tile_mask, block_len, axis=1)
    masked = jnp.where(patch_mask[..., None] > 0, features, jnp.zeros((), features.dtype))
    moved = (
        lax.all_to_all(masked, "row", split_axis=1, concat_axis=0, tiled=True),
        lax.all_to_all(write_vecs, "row", split_axis=1, concat_axis=0, tiled=True),
        lax.all_to_all(read_vecs, "row", split_axis=1, concat_axis=0, tiled=True),
        lax.all_to_all(col_decay, "row", split_axis=1, concat_axis=0, tiled=True),
    )
    result = column_chains(moved[0], moved[1], moved[2], moved[3], block_len)
    col_out = lax.all_to_all(result, "row", split_axis=0, concat_axis=1, tiled=True)
    local_terms, read_blocks = row_terms(masked, write_vecs, read_vecs, row_decay, block_len)
    if lax.axis_size("col") == 1 and tile_mask.shape[1] == 1:
        y_row = local_terms[0].reshape(features.shape)
    else:
        zero_states = jnp.zeros((tile_rows,) + local_terms[1].shape[2:], jnp.float32)
        closing_states, unused_states = jax.vmap(enter_states)(
            local_terms[2], local_terms[1], zero_states
        )
        device_decay = jnp.prod(local_terms[2], axis=1)
        identity = (jnp.ones_like(device_decay), jnp.zeros_like(closing_states))
        decay_before, state_before = entering_2((device_decay, closing_states), "col", link, identity)
        y_row = row_finish(local_terms, read_blocks, state_before)
    skip_vector = jnp.repeat(skip_gain, span_width // head_count)
    total = y_row + col_out.astype(jnp.float32) + skip_vector * features.astype(jnp.float32)
    return (patch_mask[..., None].astype(jnp.float32) * total).astype(jnp.bfloat16)


def solution(mesh):
    return jax.shard_map(
        per_device,
        mesh=mesh,
        in_specs=(
            P(("slides", "row"), "col", None),
            P(("slides", "row"), "col", None),
            P(("slides", "row"), "col", None),
            P(("slides", "row"), "col", None),
            P(("slides", "row"), "col", None),
            P(("slides", "row"), "col"),
            P(),
        ),
        out_specs=P(("slides", "row"), "col", None),
        check_vma=False,
    )
```

```python
import functools

import jax
import jax.numpy as jnp
from jax import lax
from jax.experimental import pallas as pl
from jax.experimental.pallas import tpu as pltpu
from jax.sharding import PartitionSpec as P


def entering_2(array, axis, combine, identity):
    devices, here = (lax.axis_size(axis), lax.axis_index(axis))
    everything = jax.tree.map(
        lambda part, kind: lax.all_gather(part.astype(kind), axis),
        array,
        (jnp.bfloat16, jnp.bfloat16),
    )
    start = jax.tree.map(
        lambda part, zero: jnp.broadcast_to(jnp.asarray(zero, part.dtype), part.shape),
        array,
        identity,
    )

    def step(k, before):
        reached = k < here
        new = combine(
            before, jax.tree.map(lambda part, own: part[k].astype(own.dtype), everything, array)
        )
        return jax.tree.map(lambda a, b: jnp.where(reached, a, b), new, before)

    return lax.fori_loop(0, devices, step, start)


def block_local(masked, write_vecs, read_vecs, decays):
    blocks, length, span_width = masked.shape
    head_count = decays.shape[-1]
    head_width = span_width // head_count
    slots = jnp.arange(length)
    upto = (slots[:, None] >= slots[None, :]).astype(decays.dtype)
    running = jnp.einsum("ts,ksh->kht", upto, decays, preferred_element_type=jnp.float32)
    scores = jnp.einsum("ktn,ksn->kts", read_vecs, write_vecs, preferred_element_type=jnp.float32)
    target_slots = jnp.arange(length)
    causal = target_slots[:, None] >= target_slots[None, :]
    spread = jnp.where(causal, running[:, :, :, None] - running[:, :, None, :], jnp.float32(0.0))
    weights = jnp.where(causal, scores[:, None] * jnp.exp(spread), jnp.float32(0.0)).astype(
        jnp.bfloat16
    )
    values = masked.reshape(blocks, length, head_count, head_width)
    inside = jnp.einsum("khts,kshp->kthp", weights, values, preferred_element_type=jnp.float32)
    closing = running[:, :, -1]
    scaled = (
        write_vecs.astype(jnp.float32)[:, None] * jnp.exp(closing[:, :, None] - running)[..., None]
    ).astype(jnp.bfloat16)
    block_state = jnp.einsum("khsn,kshp->khnp", scaled, values, preferred_element_type=jnp.float32)
    return (inside, block_state, jnp.exp(closing), running)


def enter_states(damping, block_state, initial):

    def advance(carry_state, element):
        factor, fresh_term = element
        return (factor[:, None, None] * carry_state + fresh_term, carry_state)

    return lax.scan(advance, initial, (damping, block_state))


def combine_out(inside, entering, read_blocks, running):
    carried = jnp.einsum(
        "ktn,khnp->kthp", read_blocks.astype(jnp.float32), entering, precision=lax.Precision.HIGHEST
    )
    total = inside + carried * jnp.swapaxes(jnp.exp(running), 1, 2)[..., None]
    return total.reshape(total.shape[0] * total.shape[1], total.shape[2] * total.shape[3])


def to_blocks(array, block_len):
    return array.reshape(
        array.shape[:-2] + (array.shape[-2] // block_len, block_len, array.shape[-1])
    )


def column_chains(masked, write_vecs, read_vecs, decays, block_len):

    def one_column(masked_c, write_c, read_c, decay_c):
        read_blocks = to_blocks(read_c, block_len)
        inside, block_state, damping, running = block_local(
            to_blocks(masked_c, block_len),
            to_blocks(write_c, block_len),
            read_blocks,
            to_blocks(decay_c, block_len),
        )
        if read_blocks.shape[0] == 1:
            return inside.reshape(masked_c.shape)
        zero_state = jnp.zeros(block_state.shape[1:], jnp.float32)
        closing_state, entering = enter_states(damping, block_state, zero_state)
        return combine_out(inside, entering, read_blocks, running)

    results = jax.vmap(one_column, in_axes=1, out_axes=1)(masked, write_vecs, read_vecs, decays)
    return results.astype(jnp.bfloat16)


def row_terms(masked, write_vecs, read_vecs, decays, block_len):
    read_blocks = to_blocks(read_vecs, block_len)
    local_terms = jax.vmap(block_local)(
        to_blocks(masked, block_len),
        to_blocks(write_vecs, block_len),
        read_blocks,
        to_blocks(decays, block_len),
    )
    return (local_terms, read_blocks)


def row_finish(local_terms, read_blocks, incoming):
    inside, block_state, damping, running = local_terms
    closing_state, entering = jax.vmap(enter_states)(damping, block_state, incoming)
    return jax.vmap(combine_out)(inside, entering, read_blocks, running)


def link(earlier, later):
    return (earlier[0] * later[0], later[0][..., None, None] * earlier[1] + later[1])


MESH = pl.DeviceIdType.MESH
CHUNKS = 4


def fused_kernel(
    shape,
    mask_hbm,
    skip_hbm,
    x_hbm,
    write_hbm,
    read_hbm,
    row_hbm,
    col_hbm,
    out_ref,
    mask_ref,
    skip_ref,
    x_ref,
    write_ref,
    read_ref,
    row_ref,
    col_ref,
    aux_out,
    aux_in,
    sent,
    got,
    col_sent,
    col_got,
    total,
    grow,
    fade,
    load_sems,
    x_sems,
    aux_sems,
    there_sems,
    back_sems,
    late_sem,
):
    devices, tile_rows, tile_cols, heads = shape
    per = tile_cols // devices
    block = tile_rows * per
    patches = tile_rows * tile_cols
    chunks, _, width = sent.shape
    head_width = chunks * width // heads
    state = write_ref.shape[-1]
    f32, bf16 = jnp.float32, jnp.bfloat16
    me = lax.axis_index("row")
    own = pl.ds(pl.multiple_of(me * block, block), block)

    def dot(a, b):
        return jnp.dot(a, b, preferred_element_type=f32)

    quarter = devices // 4
    first = devices - quarter
    last = me >= first
    soon = jnp.where(last, devices - 1, first - 1)

    def peer(step):
        return lax.rem(me + 1 + step, devices)

    def soon_peer(step):
        return lax.rem(me + 1 + step, soon + 1)

    def late_peer(step):
        return first + lax.rem(me + step, quarter)

    barrier = pltpu.get_barrier_semaphore()

    def each(steps, act):
        def body(step, carry):
            act(step)
            return carry

        lax.fori_loop(0, steps, body, 0)

    def greet(other, semaphore=barrier):
        pl.semaphore_signal(semaphore, inc=1, device_id={"row": other}, device_id_type=MESH)

    @pl.when(last)
    def _():
        each(quarter - 1, lambda step: greet(first + lax.rem(me + 1 + step, quarter)))

    @pl.when(jnp.logical_not(last))
    def _():
        each(devices - 1, lambda step: greet(peer(step)))

    loads = [
        pltpu.make_async_copy(source, target, load_sems.at[i])
        for i, (source, target) in enumerate(
            (
                (mask_hbm, mask_ref),
                (write_hbm, write_ref),
                (read_hbm, read_ref),
                (col_hbm, col_ref),
                (row_hbm, row_ref),
                (skip_hbm, skip_ref),
            )
        )
    ]
    x_loads = [
        pltpu.make_async_copy(
            x_hbm.at[:, pl.ds(c * width, width)], x_ref.at[:, pl.ds(c * width, width)], x_sems.at[c]
        )
        for c in range(chunks)
    ]
    for load in loads[:4] + x_loads + loads[4:]:
        load.start()

    def send(source, target, sems, other):
        pltpu.make_async_remote_copy(
            src_ref=source.at[pl.ds(pl.multiple_of(other * block, block), block)],
            dst_ref=target.at[own],
            send_sem=sems.at[0],
            recv_sem=sems.at[1],
            device_id={"row": other},
            device_id_type=MESH,
        ).start()

    def scatter(source, target, sems):
        each(devices - 1, lambda step: send(source, target, sems, peer(step)))
        target[own, :] = source[own, :]

    def scatter_soon(source, target, sems):
        each(soon, lambda step: send(source, target, sems, soon_peer(step)))
        target[own, :] = source[own, :]

    def scatter_late(source, target, sems):
        each(quarter, lambda step: send(source, target, sems, late_peer(step)))

    def wait(buffer, sem):
        part = buffer.at[pl.ds(0, block * (devices - 1))]
        pltpu.make_async_copy(part, part, sem).wait()

    def shift(i, size):
        return lax.shift_right_logical(i, size.bit_length() - 1)

    down = lax.broadcasted_iota(jnp.int32, (patches, 1), 0)
    across = lax.broadcasted_iota(jnp.int32, (1, patches), 1)

    def home(i):
        row = shift(i, per) & (tile_rows - 1)
        return row * tile_cols + shift(i, block) * per + (i & (per - 1))

    def ones(where):
        return where.astype(f32).astype(bf16)

    from_home = home(down)
    order = ones(from_home == across)

    def turned(places, ref):
        lanes = lax.broadcasted_iota(jnp.int32, (1, tile_cols), 1)
        return sum(
            lax.dot_general(
                ones(places == lanes + r * tile_cols),
                ref[r],
                (((1,), (1,)), ((), ())),
                preferred_element_type=f32,
            )
            for r in range(tile_rows)
        ).astype(bf16)

    aux_out[:, 2 * state :] = jnp.zeros((patches, aux_out.shape[1] - 2 * state), bf16)
    for load in loads[:4]:
        load.wait()
    tile = [mask_ref[r].astype(f32) for r in range(tile_rows)]

    def keep(value):
        return jnp.concatenate(
            [value[r * tile_cols : (r + 1) * tile_cols] * tile[r] for r in range(tile_rows)]
        )

    aux_out[:, :state] = dot(order, keep(write_ref[...].astype(f32)).astype(bf16)).astype(bf16)
    aux_out[:, state : 2 * state] = dot(order, read_ref[...]).astype(bf16)
    aux_out[:, 2 * state : 2 * state + heads] = turned(from_home, col_ref)

    @pl.when(last)
    def _():
        pl.semaphore_wait(barrier, devices - 1)
        each(first, lambda step: greet(lax.rem(me + step, first), late_sem))

    @pl.when(jnp.logical_not(last))
    def _():
        pl.semaphore_wait(barrier, first - 1)

    scatter_soon(aux_out, aux_in, aux_sems)

    for c in range(chunks):
        x_loads[c].wait()
        sent[c] = dot(order, x_ref[:, c * width : (c + 1) * width]).astype(bf16)
        if c:
            scatter(sent.at[c], got.at[c], there_sems.at[c])
            continue
        scatter_soon(sent.at[c], got.at[c], there_sems.at[c])

        @pl.when(jnp.logical_not(last))
        def _():
            pl.semaphore_wait(late_sem, quarter)
            scatter_late(aux_out, aux_in, aux_sems)
            scatter_late(sent.at[c], got.at[c], there_sems.at[c])

    def spread(c):
        head = lax.broadcasted_iota(jnp.int32, (heads, width), 0)
        lane = lax.broadcasted_iota(jnp.int32, (heads, width), 1)
        return (head == shift(lane + c * width, head_width)).astype(f32)

    def running(below, decays, c):
        return dot(below, dot(decays, spread(c).astype(bf16)).astype(bf16))

    def causal(reads, writes, allowed):
        scores = lax.dot_general(
            reads, writes, (((1,), (1,)), ((), ())), preferred_element_type=f32
        )
        return jnp.where(allowed, scores, 0.0).astype(bf16)

    restore = ones(down == home(across))
    in_row = (down >= across) & (shift(down, tile_cols) == shift(across, tile_cols))
    row_below = ones(in_row)
    for load in loads[4:]:
        load.wait()
    row_decays = turned(down, row_ref)
    row_scores = causal(read_ref[...], write_ref[...], in_row)
    skip = jnp.broadcast_to(skip_ref[...], (8, heads))
    for c in range(chunks):
        cut = slice(c * width, (c + 1) * width)
        run = running(row_below, row_decays, c)
        faded = (x_ref[:, cut].astype(f32) * jnp.exp(-run)).astype(bf16)
        gain = jnp.dot(
            skip, spread(c), precision=lax.Precision.HIGHEST, preferred_element_type=f32
        )[:1]
        total[:, cut] = jnp.exp(run) * dot(row_scores, faded) + gain * x_ref[:, cut].astype(f32)

    in_col = (down >= across) & ((down & (per - 1)) == (across & (per - 1)))
    col_below = ones(in_col)
    wait(aux_in, aux_sems.at[1])
    col_scores = causal(aux_in[:, state : 2 * state], aux_in[:, :state], in_col)
    for c in range(chunks):
        run = running(col_below, aux_in[:, 2 * state : 2 * state + heads], c)
        grow[c] = jnp.exp(run)
        fade[c] = jnp.exp(-run)

    for c in range(chunks):
        wait(got.at[c], there_sems.at[c, 1])
        faded = (got[c].astype(f32) * fade[c]).astype(bf16)
        col_sent[c] = (grow[c] * dot(col_scores, faded)).astype(bf16)
        scatter(col_sent.at[c], col_got.at[c], back_sems.at[c])

    for c in range(chunks):
        cut = slice(c * width, (c + 1) * width)
        wait(col_got.at[c], back_sems.at[c, 1])
        out_ref[:, cut] = keep(total[:, cut] + dot(restore, col_got[c])).astype(bf16)

    wait(aux_out, aux_sems.at[0])
    for c in range(chunks):
        wait(sent.at[c], there_sems.at[c, 0])
        wait(col_sent.at[c], back_sems.at[c, 0])


def fused(features, write_vecs, read_vecs, row_decay, col_decay, tile_mask, skip_gain):
    tile_rows, tile_cols, span_width = features.shape
    heads, state = row_decay.shape[-1], write_vecs.shape[-1]
    patches = tile_rows * tile_cols
    devices = lax.axis_size("row")
    width = span_width // CHUNKS

    def flat(array):
        return array.reshape(patches, array.shape[-1])

    vmem = pl.BlockSpec(memory_space=pltpu.VMEM)
    piece = (CHUNKS, patches, width)
    aux = pltpu.VMEM((patches, 2 * state + 128), jnp.bfloat16)
    result = pl.pallas_call(
        functools.partial(fused_kernel, (devices, tile_rows, tile_cols, heads)),
        out_shape=pltpu.VMEM((patches, span_width), jnp.bfloat16),
        in_specs=[pl.BlockSpec(memory_space=pl.ANY)] * 7,
        out_specs=vmem,
        scratch_shapes=[
            pltpu.SMEM((tile_rows,), jnp.int32),
            pltpu.VMEM((1, heads), jnp.float32),
            pltpu.VMEM((patches, span_width), jnp.bfloat16),
            pltpu.VMEM((patches, state), jnp.bfloat16),
            pltpu.VMEM((patches, state), jnp.bfloat16),
            pltpu.VMEM((tile_rows, heads, tile_cols), jnp.bfloat16),
            pltpu.VMEM((tile_rows, heads, tile_cols), jnp.bfloat16),
            aux,
            aux,
            pltpu.VMEM(piece, jnp.bfloat16),
            pltpu.VMEM(piece, jnp.bfloat16),
            pltpu.VMEM(piece, jnp.bfloat16),
            pltpu.VMEM(piece, jnp.bfloat16),
            pltpu.VMEM((patches, span_width), jnp.float32),
            pltpu.VMEM(piece, jnp.float32),
            pltpu.VMEM(piece, jnp.float32),
            pltpu.SemaphoreType.DMA((6,)),
            pltpu.SemaphoreType.DMA((CHUNKS,)),
            pltpu.SemaphoreType.DMA((2,)),
            pltpu.SemaphoreType.DMA((CHUNKS, 2)),
            pltpu.SemaphoreType.DMA((CHUNKS, 2)),
            pltpu.SemaphoreType.REGULAR,
        ],
        compiler_params=pltpu.CompilerParams(
            collective_id=0, has_side_effects=True, vmem_limit_bytes=60 * 2**20
        ),
    )(
        tile_mask.reshape(-1),
        skip_gain.reshape(1, heads),
        flat(features),
        flat(write_vecs),
        flat(read_vecs),
        jnp.swapaxes(row_decay, 1, 2),
        jnp.swapaxes(col_decay, 1, 2),
    )
    return result.reshape(features.shape)


def fits_fused(features, row_decay, tile_mask):
    tile_rows, tile_cols, span_width = features.shape
    devices = lax.axis_size("row")
    return (
        lax.axis_size("col") == 1
        and tile_mask.shape[1] == 1
        and tile_rows * devices == tile_cols
        and devices % 4 == 0
        and tile_cols <= 64
        and (tile_rows * (tile_cols // devices)) % 16 == 0
        and span_width % (CHUNKS * 128) == 0
        and row_decay.shape[-1] <= 128
        and all(
            size.bit_count() == 1
            for size in (tile_rows, tile_cols, devices, span_width // row_decay.shape[-1])
        )
    )


def per_device(features, write_vecs, read_vecs, row_decay, col_decay, tile_mask, skip_gain):
    tile_rows, tile_cols, span_width = features.shape
    if fits_fused(features, row_decay, tile_mask):
        return fused(features, write_vecs, read_vecs, row_decay, col_decay, tile_mask, skip_gain)
    head_count = row_decay.shape[-1]
    block_len = tile_cols // tile_mask.shape[1]
    patch_mask = jnp.repeat(tile_mask, block_len, axis=1)
    masked = jnp.where(patch_mask[..., None] > 0, features, jnp.zeros((), features.dtype))
    moved = (
        lax.all_to_all(masked, "row", split_axis=1, concat_axis=0, tiled=True),
        lax.all_to_all(write_vecs, "row", split_axis=1, concat_axis=0, tiled=True),
        lax.all_to_all(read_vecs, "row", split_axis=1, concat_axis=0, tiled=True),
        lax.all_to_all(col_decay, "row", split_axis=1, concat_axis=0, tiled=True),
    )
    result = column_chains(moved[0], moved[1], moved[2], moved[3], block_len)
    col_out = lax.all_to_all(result, "row", split_axis=0, concat_axis=1, tiled=True)
    local_terms, read_blocks = row_terms(masked, write_vecs, read_vecs, row_decay, block_len)
    if lax.axis_size("col") == 1 and tile_mask.shape[1] == 1:
        y_row = local_terms[0].reshape(features.shape)
    else:
        zero_states = jnp.zeros((tile_rows,) + local_terms[1].shape[2:], jnp.float32)
        closing_states, unused_states = jax.vmap(enter_states)(
            local_terms[2], local_terms[1], zero_states
        )
        device_decay = jnp.prod(local_terms[2], axis=1)
        identity = (jnp.ones_like(device_decay), jnp.zeros_like(closing_states))
        decay_before, state_before = entering_2((device_decay, closing_states), "col", link, identity)
        y_row = row_finish(local_terms, read_blocks, state_before)
    skip_vector = jnp.repeat(skip_gain, span_width // head_count)
    total = y_row + col_out.astype(jnp.float32) + skip_vector * features.astype(jnp.float32)
    return (patch_mask[..., None].astype(jnp.float32) * total).astype(jnp.bfloat16)


def solution(mesh):
    return jax.shard_map(
        per_device,
        mesh=mesh,
        in_specs=(
            P(("slides", "row"), "col", None),
            P(("slides", "row"), "col", None),
            P(("slides", "row"), "col", None),
            P(("slides", "row"), "col", None),
            P(("slides", "row"), "col", None),
            P(("slides", "row"), "col"),
            P(),
        ),
        out_specs=P(("slides", "row"), "col", None),
        check_vma=False,
    )
```

```python
import functools

import jax
import jax.numpy as jnp
from jax import lax
from jax.experimental import pallas as pl
from jax.experimental.pallas import tpu as pltpu
from jax.sharding import PartitionSpec as P


def entering_2(array, axis, combine, identity):
    devices, here = (lax.axis_size(axis), lax.axis_index(axis))
    everything = jax.tree.map(
        lambda part, kind: lax.all_gather(part.astype(kind), axis),
        array,
        (jnp.bfloat16, jnp.bfloat16),
    )
    start = jax.tree.map(
        lambda part, zero: jnp.broadcast_to(jnp.asarray(zero, part.dtype), part.shape),
        array,
        identity,
    )

    def step(k, before):
        reached = k < here
        new = combine(
            before, jax.tree.map(lambda part, own: part[k].astype(own.dtype), everything, array)
        )
        return jax.tree.map(lambda a, b: jnp.where(reached, a, b), new, before)

    return lax.fori_loop(0, devices, step, start)


def block_local(masked, write_vecs, read_vecs, decays):
    blocks, length, span_width = masked.shape
    head_count = decays.shape[-1]
    head_width = span_width // head_count
    slots = jnp.arange(length)
    upto = (slots[:, None] >= slots[None, :]).astype(decays.dtype)
    running = jnp.einsum("ts,ksh->kht", upto, decays, preferred_element_type=jnp.float32)
    scores = jnp.einsum("ktn,ksn->kts", read_vecs, write_vecs, preferred_element_type=jnp.float32)
    target_slots = jnp.arange(length)
    causal = target_slots[:, None] >= target_slots[None, :]
    spread = jnp.where(causal, running[:, :, :, None] - running[:, :, None, :], jnp.float32(0.0))
    weights = jnp.where(causal, scores[:, None] * jnp.exp(spread), jnp.float32(0.0)).astype(
        jnp.bfloat16
    )
    values = masked.reshape(blocks, length, head_count, head_width)
    inside = jnp.einsum("khts,kshp->kthp", weights, values, preferred_element_type=jnp.float32)
    closing = running[:, :, -1]
    scaled = (
        write_vecs.astype(jnp.float32)[:, None] * jnp.exp(closing[:, :, None] - running)[..., None]
    ).astype(jnp.bfloat16)
    block_state = jnp.einsum("khsn,kshp->khnp", scaled, values, preferred_element_type=jnp.float32)
    return (inside, block_state, jnp.exp(closing), running)


def enter_states(damping, block_state, initial):

    def advance(carry_state, element):
        factor, fresh_term = element
        return (factor[:, None, None] * carry_state + fresh_term, carry_state)

    return lax.scan(advance, initial, (damping, block_state))


def combine_out(inside, entering, read_blocks, running):
    carried = jnp.einsum(
        "ktn,khnp->kthp", read_blocks.astype(jnp.float32), entering, precision=lax.Precision.HIGHEST
    )
    total = inside + carried * jnp.swapaxes(jnp.exp(running), 1, 2)[..., None]
    return total.reshape(total.shape[0] * total.shape[1], total.shape[2] * total.shape[3])


def to_blocks(array, block_len):
    return array.reshape(
        array.shape[:-2] + (array.shape[-2] // block_len, block_len, array.shape[-1])
    )


def column_chains(masked, write_vecs, read_vecs, decays, block_len):

    def one_column(masked_c, write_c, read_c, decay_c):
        read_blocks = to_blocks(read_c, block_len)
        inside, block_state, damping, running = block_local(
            to_blocks(masked_c, block_len),
            to_blocks(write_c, block_len),
            read_blocks,
            to_blocks(decay_c, block_len),
        )
        if read_blocks.shape[0] == 1:
            return inside.reshape(masked_c.shape)
        zero_state = jnp.zeros(block_state.shape[1:], jnp.float32)
        closing_state, entering = enter_states(damping, block_state, zero_state)
        return combine_out(inside, entering, read_blocks, running)

    results = jax.vmap(one_column, in_axes=1, out_axes=1)(masked, write_vecs, read_vecs, decays)
    return results.astype(jnp.bfloat16)


def row_terms(masked, write_vecs, read_vecs, decays, block_len):
    read_blocks = to_blocks(read_vecs, block_len)
    local_terms = jax.vmap(block_local)(
        to_blocks(masked, block_len),
        to_blocks(write_vecs, block_len),
        read_blocks,
        to_blocks(decays, block_len),
    )
    return (local_terms, read_blocks)


def row_finish(local_terms, read_blocks, incoming):
    inside, block_state, damping, running = local_terms
    closing_state, entering = jax.vmap(enter_states)(damping, block_state, incoming)
    return jax.vmap(combine_out)(inside, entering, read_blocks, running)


def link(earlier, later):
    return (earlier[0] * later[0], later[0][..., None, None] * earlier[1] + later[1])


MESH = pl.DeviceIdType.MESH
CHUNKS = 4


def fused_kernel(
    shape,
    mask_hbm,
    skip_hbm,
    x_hbm,
    write_hbm,
    read_hbm,
    row_hbm,
    col_hbm,
    out_ref,
    mask_ref,
    skip_ref,
    x_ref,
    write_ref,
    read_ref,
    row_ref,
    col_ref,
    aux_out,
    aux_in,
    sent,
    got,
    col_sent,
    col_got,
    total,
    grow,
    fade,
    load_sems,
    x_sems,
    aux_sems,
    there_sems,
    back_sems,
    late_sem,
):
    devices, tile_rows, tile_cols, heads = shape
    per = tile_cols // devices
    block = tile_rows * per
    patches = tile_rows * tile_cols
    chunks, _, width = sent.shape
    head_width = chunks * width // heads
    state = write_ref.shape[-1]
    f32, bf16 = jnp.float32, jnp.bfloat16
    me = lax.axis_index("row")
    own = pl.ds(pl.multiple_of(me * block, block), block)

    def dot(a, b):
        return jnp.dot(a, b, preferred_element_type=f32)

    quarter = devices // 4
    first = devices - quarter
    last = me >= first
    soon = jnp.where(last, devices - 1, first - 1)

    def peer(step):
        return lax.rem(me + 1 + step, devices)

    def soon_peer(step):
        return lax.rem(me + 1 + step, soon + 1)

    def late_peer(step):
        return first + lax.rem(me + step, quarter)

    barrier = pltpu.get_barrier_semaphore()

    def each(steps, act):
        def body(step, carry):
            act(step)
            return carry

        lax.fori_loop(0, steps, body, 0)

    def greet(other, semaphore=barrier):
        pl.semaphore_signal(semaphore, inc=1, device_id={"row": other}, device_id_type=MESH)

    @pl.when(last)
    def _():
        each(quarter - 1, lambda step: greet(first + lax.rem(me + 1 + step, quarter)))

    @pl.when(jnp.logical_not(last))
    def _():
        each(devices - 1, lambda step: greet(peer(step)))

    loads = [
        pltpu.make_async_copy(source, target, load_sems.at[i])
        for i, (source, target) in enumerate(
            (
                (mask_hbm, mask_ref),
                (write_hbm, write_ref),
                (read_hbm, read_ref),
                (col_hbm, col_ref),
                (row_hbm, row_ref),
                (skip_hbm, skip_ref),
            )
        )
    ]
    x_loads = [
        pltpu.make_async_copy(
            x_hbm.at[:, pl.ds(c * width, width)], x_ref.at[:, pl.ds(c * width, width)], x_sems.at[c]
        )
        for c in range(chunks)
    ]
    for load in loads[:4] + x_loads + loads[4:]:
        load.start()

    def send(source, target, sems, other):
        pltpu.make_async_remote_copy(
            src_ref=source.at[pl.ds(pl.multiple_of(other * block, block), block)],
            dst_ref=target.at[own],
            send_sem=sems.at[0],
            recv_sem=sems.at[1],
            device_id={"row": other},
            device_id_type=MESH,
        ).start()

    tail = me == devices - 1
    head = me == 0

    def scatter_soon(source, target, sems):
        each(soon, lambda step: send(source, target, sems, soon_peer(step)))

    def scatter_late(source, target, sems):
        each(quarter, lambda step: send(source, target, sems, late_peer(step)))

    def give_back(source, target, sems):
        def act(step):
            other = peer(step)

            @pl.when(other != 0)
            def _():
                send(source, target, sems, other)

        each(devices - 1, act)

    def wait(buffer, sem, count=devices - 1):
        part = buffer.at[pl.ds(0, block * count)]
        pltpu.make_async_copy(part, part, sem).wait()

    def wait_either(buffer, sem, all_of_them):
        @pl.when(all_of_them)
        def _():
            wait(buffer, sem)

        @pl.when(jnp.logical_not(all_of_them))
        def _():
            wait(buffer, sem, devices - 2)

    def shift(i, size):
        return lax.shift_right_logical(i, size.bit_length() - 1)

    down = lax.broadcasted_iota(jnp.int32, (patches, 1), 0)
    across = lax.broadcasted_iota(jnp.int32, (1, patches), 1)

    def home(i):
        row = shift(i, per) & (tile_rows - 1)
        return row * tile_cols + shift(i, block) * per + (i & (per - 1))

    def ones(where):
        return where.astype(f32).astype(bf16)

    from_home = home(down)
    order = ones(from_home == across)

    def turned(places, ref):
        lanes = lax.broadcasted_iota(jnp.int32, (1, tile_cols), 1)
        return sum(
            lax.dot_general(
                ones(places == lanes + r * tile_cols),
                ref[r],
                (((1,), (1,)), ((), ())),
                preferred_element_type=f32,
            )
            for r in range(tile_rows)
        ).astype(bf16)

    aux_out[:, 2 * state :] = jnp.zeros((patches, aux_out.shape[1] - 2 * state), bf16)
    for load in loads[:4]:
        load.wait()
    tile = [mask_ref[r].astype(f32) for r in range(tile_rows)]

    def keep(value):
        return jnp.concatenate(
            [value[r * tile_cols : (r + 1) * tile_cols] * tile[r] for r in range(tile_rows)]
        )

    aux_out[:, :state] = dot(order, keep(write_ref[...].astype(f32)).astype(bf16)).astype(bf16)
    aux_out[:, state : 2 * state] = dot(order, read_ref[...]).astype(bf16)
    aux_out[:, 2 * state : 2 * state + heads] = turned(from_home, col_ref)

    @pl.when(last)
    def _():
        pl.semaphore_wait(barrier, devices - 1)
        each(first, lambda step: greet(lax.rem(me + step, first), late_sem))

    @pl.when(jnp.logical_not(last))
    def _():
        pl.semaphore_wait(barrier, first - 1)

    scatter_soon(aux_out, aux_in, aux_sems)
    aux_in[own, :] = aux_out[own, :]

    for c in range(chunks):
        x_loads[c].wait()
        sent[c] = dot(order, x_ref[:, c * width : (c + 1) * width]).astype(bf16)
        got[c, block * (devices - 1) :, :] = jnp.zeros((block, width), bf16)
        got[c, own, :] = sent[c, own, :]

        @pl.when(jnp.logical_not(tail))
        def _():
            if c:
                each(devices - 1, lambda step: send(sent.at[c], got.at[c], there_sems.at[c], peer(step)))
            else:
                scatter_soon(sent.at[c], got.at[c], there_sems.at[c])

        if not c:

            @pl.when(jnp.logical_not(last))
            def _():
                pl.semaphore_wait(late_sem, quarter)
                scatter_late(aux_out, aux_in, aux_sems)
                scatter_late(sent.at[c], got.at[c], there_sems.at[c])

    def spread(c):
        head = lax.broadcasted_iota(jnp.int32, (heads, width), 0)
        lane = lax.broadcasted_iota(jnp.int32, (heads, width), 1)
        return (head == shift(lane + c * width, head_width)).astype(f32)

    def running(below, decays, c):
        return dot(below, dot(decays, spread(c).astype(bf16)).astype(bf16))

    def products(reads, writes):
        return lax.dot_general(
            reads, writes, (((1,), (1,)), ((), ())), preferred_element_type=f32
        )

    def causal(scores, allowed):
        return jnp.where(allowed, scores, 0.0).astype(bf16)

    restore = ones(down == home(across))
    in_row = (down >= across) & (shift(down, tile_cols) == shift(across, tile_cols))
    row_below = ones(in_row)
    for load in loads[4:]:
        load.wait()
    row_decays = turned(down, row_ref)
    own_scores = products(read_ref[...], write_ref[...])
    row_scores = causal(own_scores, in_row)
    in_home = (down >= across) & ((down & (tile_cols - 1)) == (across & (tile_cols - 1)))
    home_below = ones(in_home)
    home_decays = turned(down, col_ref)
    origin = shift(across, tile_cols)
    present = sum(jnp.where(origin == r, tile[r], 0.0) for r in range(tile_rows))
    home_scores = causal(own_scores * present, in_home)
    skip = jnp.broadcast_to(skip_ref[...], (8, heads))
    for c in range(chunks):
        cut = slice(c * width, (c + 1) * width)
        run = running(row_below, row_decays, c)
        faded = (x_ref[:, cut].astype(f32) * jnp.exp(-run)).astype(bf16)
        gain = jnp.dot(
            skip, spread(c), precision=lax.Precision.HIGHEST, preferred_element_type=f32
        )[:1]
        total[:, cut] = jnp.exp(run) * dot(row_scores, faded) + gain * x_ref[:, cut].astype(f32)

    same_col = (down & (per - 1)) == (across & (per - 1))
    col_below = ones((down >= across) & same_col)
    wait(aux_in, aux_sems.at[1])
    earlier = (shift(down, block) > shift(across, block)) & same_col
    col_scores = causal(products(aux_in[:, state : 2 * state], aux_in[:, :state]), earlier)
    for c in range(chunks):
        run = running(col_below, aux_in[:, 2 * state : 2 * state + heads], c)
        grow[c] = jnp.exp(run)
        fade[c] = jnp.exp(-run)

    for c in range(chunks):
        wait_either(got.at[c], there_sems.at[c, 1], tail)
        faded = (got[c].astype(f32) * fade[c]).astype(bf16)
        col_sent[c] = (grow[c] * dot(col_scores, faded)).astype(bf16)
        give_back(col_sent.at[c], col_got.at[c], back_sems.at[c])
        col_got[c, own, :] = col_sent[c, own, :]
        cut = slice(c * width, (c + 1) * width)
        run = running(home_below, home_decays, c)
        faded = (x_ref[:, cut].astype(f32) * jnp.exp(-run)).astype(bf16)
        total[:, cut] += jnp.exp(run) * dot(home_scores, faded)

    for c in range(chunks):
        cut = slice(c * width, (c + 1) * width)

        @pl.when(head)
        def _():
            col_got[c] = jnp.zeros((patches, width), bf16)

        @pl.when(jnp.logical_not(head))
        def _():
            wait(col_got.at[c], back_sems.at[c, 1])

        out_ref[:, cut] = keep(total[:, cut] + dot(restore, col_got[c])).astype(bf16)

    wait(aux_out, aux_sems.at[0])
    for c in range(chunks):
        wait_either(col_sent.at[c], back_sems.at[c, 0], head)

        @pl.when(jnp.logical_not(tail))
        def _():
            wait(sent.at[c], there_sems.at[c, 0])


def fused(features, write_vecs, read_vecs, row_decay, col_decay, tile_mask, skip_gain):
    tile_rows, tile_cols, span_width = features.shape
    heads, state = row_decay.shape[-1], write_vecs.shape[-1]
    patches = tile_rows * tile_cols
    devices = lax.axis_size("row")
    width = span_width // CHUNKS

    def flat(array):
        return array.reshape(patches, array.shape[-1])

    vmem = pl.BlockSpec(memory_space=pltpu.VMEM)
    piece = (CHUNKS, patches, width)
    aux = pltpu.VMEM((patches, 2 * state + 128), jnp.bfloat16)
    result = pl.pallas_call(
        functools.partial(fused_kernel, (devices, tile_rows, tile_cols, heads)),
        out_shape=pltpu.VMEM((patches, span_width), jnp.bfloat16),
        in_specs=[pl.BlockSpec(memory_space=pl.ANY)] * 7,
        out_specs=vmem,
        scratch_shapes=[
            pltpu.SMEM((tile_rows,), jnp.int32),
            pltpu.VMEM((1, heads), jnp.float32),
            pltpu.VMEM((patches, span_width), jnp.bfloat16),
            pltpu.VMEM((patches, state), jnp.bfloat16),
            pltpu.VMEM((patches, state), jnp.bfloat16),
            pltpu.VMEM((tile_rows, heads, tile_cols), jnp.bfloat16),
            pltpu.VMEM((tile_rows, heads, tile_cols), jnp.bfloat16),
            aux,
            aux,
            pltpu.VMEM(piece, jnp.bfloat16),
            pltpu.VMEM(piece, jnp.bfloat16),
            pltpu.VMEM(piece, jnp.bfloat16),
            pltpu.VMEM(piece, jnp.bfloat16),
            pltpu.VMEM((patches, span_width), jnp.float32),
            pltpu.VMEM(piece, jnp.float32),
            pltpu.VMEM(piece, jnp.float32),
            pltpu.SemaphoreType.DMA((6,)),
            pltpu.SemaphoreType.DMA((CHUNKS,)),
            pltpu.SemaphoreType.DMA((2,)),
            pltpu.SemaphoreType.DMA((CHUNKS, 2)),
            pltpu.SemaphoreType.DMA((CHUNKS, 2)),
            pltpu.SemaphoreType.REGULAR,
        ],
        compiler_params=pltpu.CompilerParams(
            collective_id=0, has_side_effects=True, vmem_limit_bytes=60 * 2**20
        ),
    )(
        tile_mask.reshape(-1),
        skip_gain.reshape(1, heads),
        flat(features),
        flat(write_vecs),
        flat(read_vecs),
        jnp.swapaxes(row_decay, 1, 2),
        jnp.swapaxes(col_decay, 1, 2),
    )
    return result.reshape(features.shape)


def fits_fused(features, row_decay, tile_mask):
    tile_rows, tile_cols, span_width = features.shape
    devices = lax.axis_size("row")
    return (
        lax.axis_size("col") == 1
        and tile_mask.shape[1] == 1
        and tile_rows * devices == tile_cols
        and devices % 4 == 0
        and tile_cols <= 64
        and (tile_rows * (tile_cols // devices)) % 16 == 0
        and span_width % (CHUNKS * 128) == 0
        and row_decay.shape[-1] <= 128
        and all(
            size.bit_count() == 1
            for size in (tile_rows, tile_cols, devices, span_width // row_decay.shape[-1])
        )
    )


def per_device(features, write_vecs, read_vecs, row_decay, col_decay, tile_mask, skip_gain):
    tile_rows, tile_cols, span_width = features.shape
    if fits_fused(features, row_decay, tile_mask):
        return fused(features, write_vecs, read_vecs, row_decay, col_decay, tile_mask, skip_gain)
    head_count = row_decay.shape[-1]
    block_len = tile_cols // tile_mask.shape[1]
    patch_mask = jnp.repeat(tile_mask, block_len, axis=1)
    masked = jnp.where(patch_mask[..., None] > 0, features, jnp.zeros((), features.dtype))
    moved = (
        lax.all_to_all(masked, "row", split_axis=1, concat_axis=0, tiled=True),
        lax.all_to_all(write_vecs, "row", split_axis=1, concat_axis=0, tiled=True),
        lax.all_to_all(read_vecs, "row", split_axis=1, concat_axis=0, tiled=True),
        lax.all_to_all(col_decay, "row", split_axis=1, concat_axis=0, tiled=True),
    )
    result = column_chains(moved[0], moved[1], moved[2], moved[3], block_len)
    col_out = lax.all_to_all(result, "row", split_axis=0, concat_axis=1, tiled=True)
    local_terms, read_blocks = row_terms(masked, write_vecs, read_vecs, row_decay, block_len)
    if lax.axis_size("col") == 1 and tile_mask.shape[1] == 1:
        y_row = local_terms[0].reshape(features.shape)
    else:
        zero_states = jnp.zeros((tile_rows,) + local_terms[1].shape[2:], jnp.float32)
        closing_states, unused_states = jax.vmap(enter_states)(
            local_terms[2], local_terms[1], zero_states
        )
        device_decay = jnp.prod(local_terms[2], axis=1)
        identity = (jnp.ones_like(device_decay), jnp.zeros_like(closing_states))
        decay_before, state_before = entering_2((device_decay, closing_states), "col", link, identity)
        y_row = row_finish(local_terms, read_blocks, state_before)
    skip_vector = jnp.repeat(skip_gain, span_width // head_count)
    total = y_row + col_out.astype(jnp.float32) + skip_vector * features.astype(jnp.float32)
    return (patch_mask[..., None].astype(jnp.float32) * total).astype(jnp.bfloat16)


def solution(mesh):
    return jax.shard_map(
        per_device,
        mesh=mesh,
        in_specs=(
            P(("slides", "row"), "col", None),
            P(("slides", "row"), "col", None),
            P(("slides", "row"), "col", None),
            P(("slides", "row"), "col", None),
            P(("slides", "row"), "col", None),
            P(("slides", "row"), "col"),
            P(),
        ),
        out_specs=P(("slides", "row"), "col", None),
        check_vma=False,
    )
```

```python
import functools

import jax
import jax.numpy as jnp
from jax import lax
from jax.experimental import pallas as pl
from jax.experimental.pallas import tpu as pltpu
from jax.sharding import PartitionSpec as P


def entering_2(array, axis, combine, identity):
    devices, here = (lax.axis_size(axis), lax.axis_index(axis))
    everything = jax.tree.map(
        lambda part, kind: lax.all_gather(part.astype(kind), axis),
        array,
        (jnp.bfloat16, jnp.bfloat16),
    )
    start = jax.tree.map(
        lambda part, zero: jnp.broadcast_to(jnp.asarray(zero, part.dtype), part.shape),
        array,
        identity,
    )

    def step(k, before):
        reached = k < here
        new = combine(
            before, jax.tree.map(lambda part, own: part[k].astype(own.dtype), everything, array)
        )
        return jax.tree.map(lambda a, b: jnp.where(reached, a, b), new, before)

    return lax.fori_loop(0, devices, step, start)


def block_local(masked, write_vecs, read_vecs, decays):
    blocks, length, span_width = masked.shape
    head_count = decays.shape[-1]
    head_width = span_width // head_count
    slots = jnp.arange(length)
    upto = (slots[:, None] >= slots[None, :]).astype(decays.dtype)
    running = jnp.einsum("ts,ksh->kht", upto, decays, preferred_element_type=jnp.float32)
    scores = jnp.einsum("ktn,ksn->kts", read_vecs, write_vecs, preferred_element_type=jnp.float32)
    target_slots = jnp.arange(length)
    causal = target_slots[:, None] >= target_slots[None, :]
    spread = jnp.where(causal, running[:, :, :, None] - running[:, :, None, :], jnp.float32(0.0))
    weights = jnp.where(causal, scores[:, None] * jnp.exp(spread), jnp.float32(0.0)).astype(
        jnp.bfloat16
    )
    values = masked.reshape(blocks, length, head_count, head_width)
    inside = jnp.einsum("khts,kshp->kthp", weights, values, preferred_element_type=jnp.float32)
    closing = running[:, :, -1]
    scaled = (
        write_vecs.astype(jnp.float32)[:, None] * jnp.exp(closing[:, :, None] - running)[..., None]
    ).astype(jnp.bfloat16)
    block_state = jnp.einsum("khsn,kshp->khnp", scaled, values, preferred_element_type=jnp.float32)
    return (inside, block_state, jnp.exp(closing), running)


def enter_states(damping, block_state, initial):

    def advance(carry_state, element):
        factor, fresh_term = element
        return (factor[:, None, None] * carry_state + fresh_term, carry_state)

    return lax.scan(advance, initial, (damping, block_state))


def combine_out(inside, entering, read_blocks, running):
    carried = jnp.einsum(
        "ktn,khnp->kthp", read_blocks.astype(jnp.float32), entering, precision=lax.Precision.HIGHEST
    )
    total = inside + carried * jnp.swapaxes(jnp.exp(running), 1, 2)[..., None]
    return total.reshape(total.shape[0] * total.shape[1], total.shape[2] * total.shape[3])


def to_blocks(array, block_len):
    return array.reshape(
        array.shape[:-2] + (array.shape[-2] // block_len, block_len, array.shape[-1])
    )


def column_chains(masked, write_vecs, read_vecs, decays, block_len):

    def one_column(masked_c, write_c, read_c, decay_c):
        read_blocks = to_blocks(read_c, block_len)
        inside, block_state, damping, running = block_local(
            to_blocks(masked_c, block_len),
            to_blocks(write_c, block_len),
            read_blocks,
            to_blocks(decay_c, block_len),
        )
        if read_blocks.shape[0] == 1:
            return inside.reshape(masked_c.shape)
        zero_state = jnp.zeros(block_state.shape[1:], jnp.float32)
        closing_state, entering = enter_states(damping, block_state, zero_state)
        return combine_out(inside, entering, read_blocks, running)

    results = jax.vmap(one_column, in_axes=1, out_axes=1)(masked, write_vecs, read_vecs, decays)
    return results.astype(jnp.bfloat16)


def row_terms(masked, write_vecs, read_vecs, decays, block_len):
    read_blocks = to_blocks(read_vecs, block_len)
    local_terms = jax.vmap(block_local)(
        to_blocks(masked, block_len),
        to_blocks(write_vecs, block_len),
        read_blocks,
        to_blocks(decays, block_len),
    )
    return (local_terms, read_blocks)


def row_finish(local_terms, read_blocks, incoming):
    inside, block_state, damping, running = local_terms
    closing_state, entering = jax.vmap(enter_states)(damping, block_state, incoming)
    return jax.vmap(combine_out)(inside, entering, read_blocks, running)


def link(earlier, later):
    return (earlier[0] * later[0], later[0][..., None, None] * earlier[1] + later[1])


MESH = pl.DeviceIdType.MESH
CHUNKS = 4


def fused_kernel(
    shape,
    mask_hbm,
    skip_hbm,
    x_hbm,
    write_hbm,
    read_hbm,
    row_hbm,
    col_hbm,
    out_ref,
    mask_ref,
    skip_ref,
    x_ref,
    write_ref,
    read_ref,
    row_ref,
    col_ref,
    aux_out,
    aux_in,
    help_in,
    scores_out,
    scores_in,
    col_scores,
    decay_out,
    decay_in,
    sent,
    got,
    col_sent,
    col_got,
    total,
    grow,
    fade,
    load_sems,
    x_sems,
    aux_sems,
    help_sems,
    score_sems,
    decay_sems,
    there_sems,
    back_sems,
    late_sem,
):
    devices, tile_rows, tile_cols, heads = shape
    per = tile_cols // devices
    block = tile_rows * per
    patches = tile_rows * tile_cols
    chunks, _, width = sent.shape
    head_width = chunks * width // heads
    state = write_ref.shape[-1]
    f32, bf16 = jnp.float32, jnp.bfloat16
    me = lax.axis_index("row")
    own = pl.ds(pl.multiple_of(me * block, block), block)

    def dot(a, b):
        return jnp.dot(a, b, preferred_element_type=f32)

    quarter, half = devices // 4, devices // 2
    middle = patches // 2
    upper = me < half
    first = devices - quarter
    last = me >= first
    soon = jnp.where(last, devices - 1, first - 1)

    def peer(step):
        return lax.rem(me + 1 + step, devices)

    def soon_peer(step):
        return lax.rem(me + 1 + step, soon + 1)

    def late_peer(step):
        return first + lax.rem(me + step, quarter)

    barrier = pltpu.get_barrier_semaphore()

    def each(steps, act):
        def body(step, carry):
            act(step)
            return carry

        lax.fori_loop(0, steps, body, 0)

    def greet(other, semaphore=barrier):
        pl.semaphore_signal(semaphore, inc=1, device_id={"row": other}, device_id_type=MESH)

    @pl.when(last)
    def _():
        each(quarter - 1, lambda step: greet(first + lax.rem(me + 1 + step, quarter)))

    @pl.when(jnp.logical_not(last))
    def _():
        each(devices - 1, lambda step: greet(peer(step)))

    loads = [
        pltpu.make_async_copy(source, target, load_sems.at[i])
        for i, (source, target) in enumerate(
            (
                (mask_hbm, mask_ref),
                (write_hbm, write_ref),
                (read_hbm, read_ref),
                (col_hbm, col_ref),
                (row_hbm, row_ref),
                (skip_hbm, skip_ref),
            )
        )
    ]
    x_loads = [
        pltpu.make_async_copy(
            x_hbm.at[:, pl.ds(c * width, width)], x_ref.at[:, pl.ds(c * width, width)], x_sems.at[c]
        )
        for c in range(chunks)
    ]
    for load in loads[:4] + x_loads + loads[4:]:
        load.start()

    def send(source, target, sems, other):
        pltpu.make_async_remote_copy(
            src_ref=source.at[pl.ds(pl.multiple_of(other * block, block), block)],
            dst_ref=target.at[own],
            send_sem=sems.at[0],
            recv_sem=sems.at[1],
            device_id={"row": other},
            device_id_type=MESH,
        ).start()

    tail = me == devices - 1
    head = me == 0

    def scatter_soon(source, target, sems):
        each(soon, lambda step: send(source, target, sems, soon_peer(step)))

    def scatter_late(source, target, sems):
        each(quarter, lambda step: send(source, target, sems, late_peer(step)))

    def give_back(source, target, sems):
        def act(step):
            other = peer(step)

            @pl.when(other != 0)
            def _():
                send(source, target, sems, other)

        each(devices - 1, act)

    def wait(buffer, sem, count=devices - 1):
        part = buffer.at[pl.ds(0, block * count)]
        pltpu.make_async_copy(part, part, sem).wait()

    def wait_either(buffer, sem, all_of_them):
        @pl.when(all_of_them)
        def _():
            wait(buffer, sem)

        @pl.when(jnp.logical_not(all_of_them))
        def _():
            wait(buffer, sem, devices - 2)

    def shift(i, size):
        return lax.shift_right_logical(i, size.bit_length() - 1)

    down = lax.broadcasted_iota(jnp.int32, (patches, 1), 0)
    across = lax.broadcasted_iota(jnp.int32, (1, patches), 1)

    def home(i):
        row = shift(i, per) & (tile_rows - 1)
        return row * tile_cols + shift(i, block) * per + (i & (per - 1))

    def ones(where):
        return where.astype(f32).astype(bf16)

    from_home = home(down)
    order = ones(from_home == across)

    def turned(places, ref):
        lanes = lax.broadcasted_iota(jnp.int32, (1, tile_cols), 1)
        return sum(
            lax.dot_general(
                ones(places == lanes + r * tile_cols),
                ref[r],
                (((1,), (1,)), ((), ())),
                preferred_element_type=f32,
            )
            for r in range(tile_rows)
        ).astype(bf16)

    for load in loads[:4]:
        load.wait()
    tile = [mask_ref[r].astype(f32) for r in range(tile_rows)]

    def keep(value):
        return jnp.concatenate(
            [value[r * tile_cols : (r + 1) * tile_cols] * tile[r] for r in range(tile_rows)]
        )

    aux_out[:, :state] = dot(order, keep(write_ref[...].astype(f32)).astype(bf16)).astype(bf16)
    aux_out[:, state : 2 * state] = dot(order, read_ref[...]).astype(bf16)
    lanes = per * heads
    groups = patches // per
    lane_head = lax.broadcasted_iota(jnp.int32, (heads, lanes), 1) & (heads - 1)
    copies = ones(lax.broadcasted_iota(jnp.int32, (heads, lanes), 0) == lane_head)
    lane_col = shift(lax.broadcasted_iota(jnp.int32, (tile_cols, lanes), 1), heads)
    kept = (lax.broadcasted_iota(jnp.int32, (tile_cols, lanes), 0) & (per - 1)) == lane_col
    group = lax.broadcasted_iota(jnp.int32, (groups, tile_cols), 0)
    group_col = lax.broadcasted_iota(jnp.int32, (groups, tile_cols), 1)
    packed = jnp.zeros((groups, lanes), f32)
    for r in range(tile_rows):
        wide = lax.dot_general(
            col_ref[r], copies, (((0,), (0,)), ((), ())), preferred_element_type=f32
        )
        wide = jnp.where(kept, wide, 0.0).astype(bf16)
        packed += dot(ones(group == shift(group_col, per) * tile_rows + r), wide)
    decay_out[...] = packed.astype(bf16).reshape(decay_out.shape)

    @pl.when(last)
    def _():
        pl.semaphore_wait(barrier, devices - 1)
        each(first, lambda step: greet(lax.rem(me + step, first), late_sem))

    @pl.when(jnp.logical_not(last))
    def _():
        pl.semaphore_wait(barrier, first - 1)

    def send_aux(other):
        def rows(index):
            return pl.ds(pl.multiple_of(index * block, block), block)

        def copy(source, target, send_sem, recv_sem):
            pltpu.make_async_remote_copy(
                src_ref=source,
                dst_ref=target,
                send_sem=send_sem,
                recv_sem=recv_sem,
                device_id={"row": other},
                device_id_type=MESH,
            ).start()

        above = other < half

        @pl.when(jnp.logical_or(above, jnp.logical_not(upper)))
        def _():
            copy(aux_out.at[rows(other)], aux_in.at[own], aux_sems.at[0], aux_sems.at[1])

        @pl.when(jnp.logical_and(above, upper))
        def _():
            copy(aux_out.at[rows(other + half)], help_in.at[own], help_sems.at[0], help_sems.at[1])

        @pl.when(jnp.logical_and(above, jnp.logical_not(upper)))
        def _():
            copy(
                aux_out.at[rows(other + half), pl.ds(state, state)],
                help_in.at[own, pl.ds(state, state)],
                help_sems.at[0],
                help_sems.at[2],
            )

        copy(decay_out.at[other], decay_in.at[me], decay_sems.at[0], decay_sems.at[1])

    each(soon, lambda step: send_aux(soon_peer(step)))
    aux_in[own, :] = aux_out[own, :]
    decay_in[me] = decay_out[me]

    @pl.when(upper)
    def _():
        twin = pl.ds(pl.multiple_of((me + half) * block, block), block)
        help_in[own, :] = aux_out[twin, :]


    for c in range(chunks):
        x_loads[c].wait()
        sent[c] = dot(order, x_ref[:, c * width : (c + 1) * width]).astype(bf16)
        got[c, block * (devices - 1) :, :] = jnp.zeros((block, width), bf16)
        got[c, own, :] = sent[c, own, :]

        @pl.when(jnp.logical_not(tail))
        def _():
            if c:
                each(devices - 1, lambda step: send(sent.at[c], got.at[c], there_sems.at[c], peer(step)))
            else:
                scatter_soon(sent.at[c], got.at[c], there_sems.at[c])

        if not c:

            @pl.when(jnp.logical_not(last))
            def _():
                pl.semaphore_wait(late_sem, quarter)
                each(quarter, lambda step: send_aux(late_peer(step)))
                scatter_late(sent.at[c], got.at[c], there_sems.at[c])

    def spread(c, count=heads):
        head = lax.broadcasted_iota(jnp.int32, (count, width), 0) & (heads - 1)
        lane = lax.broadcasted_iota(jnp.int32, (count, width), 1)
        return (head == shift(lane + c * width, head_width)).astype(f32)

    def running(below, decays, c):
        own_head = spread(c, decays.shape[1]).astype(bf16)
        return dot(below, dot(decays, own_head).astype(bf16))

    def products(reads, writes):
        return lax.dot_general(
            reads, writes, (((1,), (1,)), ((), ())), preferred_element_type=f32
        )

    def causal(scores, allowed):
        return jnp.where(allowed, scores, 0.0).astype(bf16)

    same_col = (down & (per - 1)) == (across & (per - 1))
    earlier = (shift(down, block) > shift(across, block)) & same_col

    fold = ones(lax.broadcasted_iota(jnp.int32, (groups, 1), 0) == shift(across, per))
    slot = lax.broadcasted_iota(jnp.int32, (middle, middle), 0)
    slot = (slot & (per - 1)) * (middle // per) + shift(slot, per)
    swap = ones(slot == lax.broadcasted_iota(jnp.int32, (middle, middle), 1))

    @pl.when(upper)
    def _():
        part = help_in.at[pl.ds(0, block * (half - 1))]
        pltpu.make_async_copy(part, part, help_sems.at[1]).wait()
        part = help_in.at[pl.ds(0, block * half), pl.ds(0, state)]
        pltpu.make_async_copy(part, part, help_sems.at[2]).wait()
        known = causal(
            products(help_in[:, state:], help_in[:middle, :state]), earlier[:, :middle]
        )
        scores_out[...] = dot(fold, dot(known, swap).astype(bf16)).astype(bf16)
        pltpu.make_async_remote_copy(
            src_ref=scores_out,
            dst_ref=scores_in,
            send_sem=score_sems.at[0],
            recv_sem=score_sems.at[1],
            device_id={"row": me + half},
            device_id_type=MESH,
        ).start()

    restore = ones(down == home(across))
    in_row = (down >= across) & (shift(down, tile_cols) == shift(across, tile_cols))
    row_below = ones(in_row)
    for load in loads[4:]:
        load.wait()
    row_decays = turned(down, row_ref)
    own_scores = products(read_ref[...], write_ref[...])
    row_scores = causal(own_scores, in_row)
    in_home = (down >= across) & ((down & (tile_cols - 1)) == (across & (tile_cols - 1)))
    home_below = ones(in_home)
    home_decays = turned(down, col_ref)
    origin = shift(across, tile_cols)
    present = sum(jnp.where(origin == r, tile[r], 0.0) for r in range(tile_rows))
    home_scores = causal(own_scores * present, in_home)
    skip = jnp.broadcast_to(skip_ref[...], (8, heads))
    for c in range(chunks):
        cut = slice(c * width, (c + 1) * width)
        run = running(row_below, row_decays, c)
        faded = (x_ref[:, cut].astype(f32) * jnp.exp(-run)).astype(bf16)
        gain = jnp.dot(
            skip, spread(c), precision=lax.Precision.HIGHEST, preferred_element_type=f32
        )[:1]
        total[:, cut] = jnp.exp(run) * dot(row_scores, faded) + gain * x_ref[:, cut].astype(f32)

    col_below = ones((down >= across) & same_col)

    @pl.when(upper)
    def _():
        wait(aux_in, aux_sems.at[1])
        col_scores[...] = causal(products(aux_in[:, state:], aux_in[:, :state]), earlier)

    @pl.when(jnp.logical_not(upper))
    def _():
        wait(aux_in, aux_sems.at[1], half - 1)
        col_scores[:middle, middle:] = jnp.zeros((middle, middle), bf16)
        col_scores[middle:, middle:] = causal(
            products(aux_in[middle:, state:], aux_in[middle:, :state]), earlier[middle:, middle:]
        )
        pltpu.make_async_copy(scores_in, scores_in, score_sems.at[1]).wait()
        wide = lax.dot_general(
            fold, scores_in[...], (((0,), (0,)), ((), ())), preferred_element_type=f32
        )
        place = lax.broadcasted_iota(jnp.int32, (1, middle), 1)
        wide = jnp.where(shift(place, middle // per) == (down & (per - 1)), wide, 0.0)
        col_scores[:, :middle] = lax.dot_general(
            wide.astype(bf16), swap, (((1,), (1,)), ((), ())), preferred_element_type=f32
        ).astype(bf16)

    pieces = decay_in.at[pl.ds(0, devices - 1)]
    pltpu.make_async_copy(pieces, pieces, decay_sems.at[1]).wait()
    wide = lax.dot_general(
        fold,
        decay_in[...].reshape(groups, lanes),
        (((0,), (0,)), ((), ())),
        preferred_element_type=f32,
    )
    place = lax.broadcasted_iota(jnp.int32, (1, lanes), 1)
    col_decays = jnp.where(shift(place, heads) == (down & (per - 1)), wide, 0.0).astype(bf16)
    for c in range(chunks):
        run = running(col_below, col_decays, c)
        grow[c] = jnp.exp(run)
        fade[c] = jnp.exp(-run)

    for c in range(chunks):
        wait_either(got.at[c], there_sems.at[c, 1], tail)
        faded = (got[c].astype(f32) * fade[c]).astype(bf16)
        col_sent[c] = (grow[c] * dot(col_scores[...], faded)).astype(bf16)
        give_back(col_sent.at[c], col_got.at[c], back_sems.at[c])
        col_got[c, own, :] = col_sent[c, own, :]
        cut = slice(c * width, (c + 1) * width)
        run = running(home_below, home_decays, c)
        faded = (x_ref[:, cut].astype(f32) * jnp.exp(-run)).astype(bf16)
        total[:, cut] += jnp.exp(run) * dot(home_scores, faded)

    for c in range(chunks):
        cut = slice(c * width, (c + 1) * width)

        @pl.when(head)
        def _():
            col_got[c] = jnp.zeros((patches, width), bf16)

        @pl.when(jnp.logical_not(head))
        def _():
            wait(col_got.at[c], back_sems.at[c, 1])

        out_ref[:, cut] = keep(total[:, cut] + dot(restore, col_got[c])).astype(bf16)

    pltpu.make_async_copy(pieces, pieces, decay_sems.at[0]).wait()

    @pl.when(upper)
    def _():
        wait(aux_out, aux_sems.at[0], half - 1)
        wait(aux_out, help_sems.at[0], half - 1)
        pltpu.make_async_copy(scores_out, scores_out, score_sems.at[0]).wait()

    @pl.when(jnp.logical_not(upper))
    def _():
        wait(aux_out, aux_sems.at[0])
        part = help_in.at[pl.ds(0, block * half), pl.ds(0, state)]
        pltpu.make_async_copy(part, part, help_sems.at[0]).wait()

    for c in range(chunks):
        wait_either(col_sent.at[c], back_sems.at[c, 0], head)

        @pl.when(jnp.logical_not(tail))
        def _():
            wait(sent.at[c], there_sems.at[c, 0])


def fused(features, write_vecs, read_vecs, row_decay, col_decay, tile_mask, skip_gain):
    tile_rows, tile_cols, span_width = features.shape
    heads, state = row_decay.shape[-1], write_vecs.shape[-1]
    patches = tile_rows * tile_cols
    devices = lax.axis_size("row")
    width = span_width // CHUNKS

    def flat(array):
        return array.reshape(patches, array.shape[-1])

    vmem = pl.BlockSpec(memory_space=pltpu.VMEM)
    piece = (CHUNKS, patches, width)
    aux = pltpu.VMEM((patches, 2 * state), jnp.bfloat16)
    per = tile_cols // devices
    scores = pltpu.VMEM((patches // per, patches // 2), jnp.bfloat16)
    decays = pltpu.VMEM((devices, tile_rows, per * heads), jnp.bfloat16)
    result = pl.pallas_call(
        functools.partial(fused_kernel, (devices, tile_rows, tile_cols, heads)),
        out_shape=pltpu.VMEM((patches, span_width), jnp.bfloat16),
        in_specs=[pl.BlockSpec(memory_space=pl.ANY)] * 7,
        out_specs=vmem,
        scratch_shapes=[
            pltpu.SMEM((tile_rows,), jnp.int32),
            pltpu.VMEM((1, heads), jnp.float32),
            pltpu.VMEM((patches, span_width), jnp.bfloat16),
            pltpu.VMEM((patches, state), jnp.bfloat16),
            pltpu.VMEM((patches, state), jnp.bfloat16),
            pltpu.VMEM((tile_rows, heads, tile_cols), jnp.bfloat16),
            pltpu.VMEM((tile_rows, heads, tile_cols), jnp.bfloat16),
            aux,
            aux,
            aux,
            scores,
            scores,
            pltpu.VMEM((patches, patches), jnp.bfloat16),
            decays,
            decays,
            pltpu.VMEM(piece, jnp.bfloat16),
            pltpu.VMEM(piece, jnp.bfloat16),
            pltpu.VMEM(piece, jnp.bfloat16),
            pltpu.VMEM(piece, jnp.bfloat16),
            pltpu.VMEM((patches, span_width), jnp.float32),
            pltpu.VMEM(piece, jnp.float32),
            pltpu.VMEM(piece, jnp.float32),
            pltpu.SemaphoreType.DMA((6,)),
            pltpu.SemaphoreType.DMA((CHUNKS,)),
            pltpu.SemaphoreType.DMA((2,)),
            pltpu.SemaphoreType.DMA((3,)),
            pltpu.SemaphoreType.DMA((2,)),
            pltpu.SemaphoreType.DMA((2,)),
            pltpu.SemaphoreType.DMA((CHUNKS, 2)),
            pltpu.SemaphoreType.DMA((CHUNKS, 2)),
            pltpu.SemaphoreType.REGULAR,
        ],
        compiler_params=pltpu.CompilerParams(
            collective_id=0, has_side_effects=True, vmem_limit_bytes=60 * 2**20
        ),
    )(
        tile_mask.reshape(-1),
        skip_gain.reshape(1, heads),
        flat(features),
        flat(write_vecs),
        flat(read_vecs),
        jnp.swapaxes(row_decay, 1, 2),
        jnp.swapaxes(col_decay, 1, 2),
    )
    return result.reshape(features.shape)


def fits_fused(features, row_decay, tile_mask):
    tile_rows, tile_cols, span_width = features.shape
    devices = lax.axis_size("row")
    return (
        lax.axis_size("col") == 1
        and tile_mask.shape[1] == 1
        and tile_rows * devices == tile_cols
        and devices % 4 == 0
        and tile_cols <= 64
        and (tile_rows * (tile_cols // devices)) % 16 == 0
        and span_width % (CHUNKS * 128) == 0
        and (tile_cols // devices) * row_decay.shape[-1] == 128
        and tile_rows * tile_cols % 256 == 0
        and all(
            size.bit_count() == 1
            for size in (tile_rows, tile_cols, devices, span_width // row_decay.shape[-1])
        )
    )


def per_device(features, write_vecs, read_vecs, row_decay, col_decay, tile_mask, skip_gain):
    tile_rows, tile_cols, span_width = features.shape
    if fits_fused(features, row_decay, tile_mask):
        return fused(features, write_vecs, read_vecs, row_decay, col_decay, tile_mask, skip_gain)
    head_count = row_decay.shape[-1]
    block_len = tile_cols // tile_mask.shape[1]
    patch_mask = jnp.repeat(tile_mask, block_len, axis=1)
    masked = jnp.where(patch_mask[..., None] > 0, features, jnp.zeros((), features.dtype))
    moved = (
        lax.all_to_all(masked, "row", split_axis=1, concat_axis=0, tiled=True),
        lax.all_to_all(write_vecs, "row", split_axis=1, concat_axis=0, tiled=True),
        lax.all_to_all(read_vecs, "row", split_axis=1, concat_axis=0, tiled=True),
        lax.all_to_all(col_decay, "row", split_axis=1, concat_axis=0, tiled=True),
    )
    result = column_chains(moved[0], moved[1], moved[2], moved[3], block_len)
    col_out = lax.all_to_all(result, "row", split_axis=0, concat_axis=1, tiled=True)
    local_terms, read_blocks = row_terms(masked, write_vecs, read_vecs, row_decay, block_len)
    if lax.axis_size("col") == 1 and tile_mask.shape[1] == 1:
        y_row = local_terms[0].reshape(features.shape)
    else:
        zero_states = jnp.zeros((tile_rows,) + local_terms[1].shape[2:], jnp.float32)
        closing_states, unused_states = jax.vmap(enter_states)(
            local_terms[2], local_terms[1], zero_states
        )
        device_decay = jnp.prod(local_terms[2], axis=1)
        identity = (jnp.ones_like(device_decay), jnp.zeros_like(closing_states))
        decay_before, state_before = entering_2((device_decay, closing_states), "col", link, identity)
        y_row = row_finish(local_terms, read_blocks, state_before)
    skip_vector = jnp.repeat(skip_gain, span_width // head_count)
    total = y_row + col_out.astype(jnp.float32) + skip_vector * features.astype(jnp.float32)
    return (patch_mask[..., None].astype(jnp.float32) * total).astype(jnp.bfloat16)


def solution(mesh):
    return jax.shard_map(
        per_device,
        mesh=mesh,
        in_specs=(
            P(("slides", "row"), "col", None),
            P(("slides", "row"), "col", None),
            P(("slides", "row"), "col", None),
            P(("slides", "row"), "col", None),
            P(("slides", "row"), "col", None),
            P(("slides", "row"), "col"),
            P(),
        ),
        out_specs=P(("slides", "row"), "col", None),
        check_vma=False,
    )
```

```python
import functools

import jax
import jax.numpy as jnp
from jax import lax
from jax.experimental import pallas as pl
from jax.experimental.pallas import tpu as pltpu
from jax.sharding import PartitionSpec as P


def entering_2(array, axis, combine, identity):
    devices, here = (lax.axis_size(axis), lax.axis_index(axis))
    everything = jax.tree.map(
        lambda part, kind: lax.all_gather(part.astype(kind), axis),
        array,
        (jnp.bfloat16, jnp.bfloat16),
    )
    start = jax.tree.map(
        lambda part, zero: jnp.broadcast_to(jnp.asarray(zero, part.dtype), part.shape),
        array,
        identity,
    )

    def step(k, before):
        reached = k < here
        new = combine(
            before, jax.tree.map(lambda part, own: part[k].astype(own.dtype), everything, array)
        )
        return jax.tree.map(lambda a, b: jnp.where(reached, a, b), new, before)

    return lax.fori_loop(0, devices, step, start)


def block_local(masked, write_vecs, read_vecs, decays):
    blocks, length, span_width = masked.shape
    head_count = decays.shape[-1]
    head_width = span_width // head_count
    slots = jnp.arange(length)
    upto = (slots[:, None] >= slots[None, :]).astype(decays.dtype)
    running = jnp.einsum("ts,ksh->kht", upto, decays, preferred_element_type=jnp.float32)
    scores = jnp.einsum("ktn,ksn->kts", read_vecs, write_vecs, preferred_element_type=jnp.float32)
    target_slots = jnp.arange(length)
    causal = target_slots[:, None] >= target_slots[None, :]
    spread = jnp.where(causal, running[:, :, :, None] - running[:, :, None, :], jnp.float32(0.0))
    weights = jnp.where(causal, scores[:, None] * jnp.exp(spread), jnp.float32(0.0)).astype(
        jnp.bfloat16
    )
    values = masked.reshape(blocks, length, head_count, head_width)
    inside = jnp.einsum("khts,kshp->kthp", weights, values, preferred_element_type=jnp.float32)
    closing = running[:, :, -1]
    scaled = (
        write_vecs.astype(jnp.float32)[:, None] * jnp.exp(closing[:, :, None] - running)[..., None]
    ).astype(jnp.bfloat16)
    block_state = jnp.einsum("khsn,kshp->khnp", scaled, values, preferred_element_type=jnp.float32)
    return (inside, block_state, jnp.exp(closing), running)


def enter_states(damping, block_state, initial):

    def advance(carry_state, element):
        factor, fresh_term = element
        return (factor[:, None, None] * carry_state + fresh_term, carry_state)

    return lax.scan(advance, initial, (damping, block_state))


def combine_out(inside, entering, read_blocks, running):
    carried = jnp.einsum(
        "ktn,khnp->kthp", read_blocks.astype(jnp.float32), entering, precision=lax.Precision.HIGHEST
    )
    total = inside + carried * jnp.swapaxes(jnp.exp(running), 1, 2)[..., None]
    return total.reshape(total.shape[0] * total.shape[1], total.shape[2] * total.shape[3])


def to_blocks(array, block_len):
    return array.reshape(
        array.shape[:-2] + (array.shape[-2] // block_len, block_len, array.shape[-1])
    )


def column_chains(masked, write_vecs, read_vecs, decays, block_len):

    def one_column(masked_c, write_c, read_c, decay_c):
        read_blocks = to_blocks(read_c, block_len)
        inside, block_state, damping, running = block_local(
            to_blocks(masked_c, block_len),
            to_blocks(write_c, block_len),
            read_blocks,
            to_blocks(decay_c, block_len),
        )
        if read_blocks.shape[0] == 1:
            return inside.reshape(masked_c.shape)
        zero_state = jnp.zeros(block_state.shape[1:], jnp.float32)
        closing_state, entering = enter_states(damping, block_state, zero_state)
        return combine_out(inside, entering, read_blocks, running)

    results = jax.vmap(one_column, in_axes=1, out_axes=1)(masked, write_vecs, read_vecs, decays)
    return results.astype(jnp.bfloat16)


def row_terms(masked, write_vecs, read_vecs, decays, block_len):
    read_blocks = to_blocks(read_vecs, block_len)
    local_terms = jax.vmap(block_local)(
        to_blocks(masked, block_len),
        to_blocks(write_vecs, block_len),
        read_blocks,
        to_blocks(decays, block_len),
    )
    return (local_terms, read_blocks)


def row_finish(local_terms, read_blocks, incoming):
    inside, block_state, damping, running = local_terms
    closing_state, entering = jax.vmap(enter_states)(damping, block_state, incoming)
    return jax.vmap(combine_out)(inside, entering, read_blocks, running)


def link(earlier, later):
    return (earlier[0] * later[0], later[0][..., None, None] * earlier[1] + later[1])


MESH = pl.DeviceIdType.MESH
CHUNKS = 4


def fused_kernel(
    shape,
    mask_hbm,
    skip_hbm,
    x_hbm,
    write_hbm,
    read_hbm,
    row_hbm,
    col_hbm,
    out_ref,
    mask_ref,
    skip_ref,
    x_ref,
    write_ref,
    read_ref,
    row_ref,
    col_ref,
    aux_out,
    aux_in,
    help_in,
    scores_out,
    scores_in,
    col_scores,
    decay_out,
    decay_in,
    sent,
    got,
    col_sent,
    col_got,
    total,
    grow,
    fade,
    load_sems,
    x_sems,
    aux_sems,
    help_sems,
    score_sems,
    decay_sems,
    there_sems,
    back_sems,
    late_sem,
):
    devices, tile_rows, tile_cols, heads = shape
    per = tile_cols // devices
    block = tile_rows * per
    patches = tile_rows * tile_cols
    chunks, _, width = sent.shape
    head_width = chunks * width // heads
    state = write_ref.shape[-1]
    f32, bf16 = jnp.float32, jnp.bfloat16
    me = lax.axis_index("row")
    own = pl.ds(pl.multiple_of(me * block, block), block)

    def dot(a, b):
        return jnp.dot(a, b, preferred_element_type=f32)

    quarter, half = devices // 4, devices // 2
    middle = patches // 2
    upper = me < half
    first = devices - quarter
    last = me >= first
    soon = jnp.where(last, devices - 1, first - 1)

    def peer(step):
        return lax.rem(me + 1 + step, devices)

    def soon_peer(step):
        return lax.rem(me + 1 + step, soon + 1)

    def late_peer(step):
        return first + lax.rem(me + step, quarter)

    barrier = pltpu.get_barrier_semaphore()

    def each(steps, act):
        def body(step, carry):
            act(step)
            return carry

        lax.fori_loop(0, steps, body, 0)

    def greet(other, semaphore=barrier):
        pl.semaphore_signal(semaphore, inc=1, device_id={"row": other}, device_id_type=MESH)

    @pl.when(last)
    def _():
        each(quarter - 1, lambda step: greet(first + lax.rem(me + 1 + step, quarter)))

    @pl.when(jnp.logical_not(last))
    def _():
        each(devices - 1, lambda step: greet(peer(step)))

    loads = [
        pltpu.make_async_copy(source, target, load_sems.at[i])
        for i, (source, target) in enumerate(
            (
                (mask_hbm, mask_ref),
                (write_hbm, write_ref),
                (read_hbm, read_ref),
                (col_hbm, col_ref),
                (row_hbm, row_ref),
                (skip_hbm, skip_ref),
            )
        )
    ]
    x_loads = [
        pltpu.make_async_copy(
            x_hbm.at[:, pl.ds(c * width, width)], x_ref.at[:, pl.ds(c * width, width)], x_sems.at[c]
        )
        for c in range(chunks)
    ]
    for load in loads[:4] + x_loads + loads[4:]:
        load.start()

    def send(source, target, sems, other):
        pltpu.make_async_remote_copy(
            src_ref=source.at[pl.ds(pl.multiple_of(other * block, block), block)],
            dst_ref=target.at[own],
            send_sem=sems.at[0],
            recv_sem=sems.at[1],
            device_id={"row": other},
            device_id_type=MESH,
        ).start()

    tail = me == devices - 1
    head = me == 0

    def scatter_soon(source, target, sems):
        each(soon, lambda step: send(source, target, sems, soon_peer(step)))

    def scatter_late(source, target, sems):
        each(quarter, lambda step: send(source, target, sems, late_peer(step)))

    def give_back(source, target, sems):
        def act(step):
            other = peer(step)

            @pl.when(other != 0)
            def _():
                send(source, target, sems, other)

        each(devices - 1, act)

    def wait(buffer, sem, count=devices - 1):
        part = buffer.at[pl.ds(0, block * count)]
        pltpu.make_async_copy(part, part, sem).wait()

    def wait_either(buffer, sem, all_of_them):
        @pl.when(all_of_them)
        def _():
            wait(buffer, sem)

        @pl.when(jnp.logical_not(all_of_them))
        def _():
            wait(buffer, sem, devices - 2)

    def shift(i, size):
        return lax.shift_right_logical(i, size.bit_length() - 1)

    down = lax.broadcasted_iota(jnp.int32, (patches, 1), 0)
    across = lax.broadcasted_iota(jnp.int32, (1, patches), 1)

    def home(i):
        row = shift(i, per) & (tile_rows - 1)
        return row * tile_cols + shift(i, block) * per + (i & (per - 1))

    def ones(where):
        return where.astype(f32).astype(bf16)

    from_home = home(down)
    order = ones(from_home == across)

    def turned(places, ref):
        lanes = lax.broadcasted_iota(jnp.int32, (1, tile_cols), 1)
        return sum(
            lax.dot_general(
                ones(places == lanes + r * tile_cols),
                ref[r],
                (((1,), (1,)), ((), ())),
                preferred_element_type=f32,
            )
            for r in range(tile_rows)
        ).astype(bf16)

    for load in loads[:4]:
        load.wait()
    tile = [mask_ref[r].astype(f32) for r in range(tile_rows)]

    def keep(value):
        return jnp.concatenate(
            [value[r * tile_cols : (r + 1) * tile_cols] * tile[r] for r in range(tile_rows)]
        )

    aux_out[:, :state] = dot(order, keep(write_ref[...].astype(f32)).astype(bf16)).astype(bf16)
    aux_out[:, state : 2 * state] = dot(order, read_ref[...]).astype(bf16)
    lanes = per * heads
    groups = patches // per
    lane_head = lax.broadcasted_iota(jnp.int32, (heads, lanes), 1) & (heads - 1)
    copies = ones(lax.broadcasted_iota(jnp.int32, (heads, lanes), 0) == lane_head)
    lane_col = shift(lax.broadcasted_iota(jnp.int32, (tile_cols, lanes), 1), heads)
    kept = (lax.broadcasted_iota(jnp.int32, (tile_cols, lanes), 0) & (per - 1)) == lane_col
    group = lax.broadcasted_iota(jnp.int32, (groups, tile_cols), 0)
    group_col = lax.broadcasted_iota(jnp.int32, (groups, tile_cols), 1)
    packed = jnp.zeros((groups, lanes), f32)
    for r in range(tile_rows):
        wide = lax.dot_general(
            col_ref[r], copies, (((0,), (0,)), ((), ())), preferred_element_type=f32
        )
        wide = jnp.where(kept, wide, 0.0).astype(bf16)
        packed += dot(ones(group == shift(group_col, per) * tile_rows + r), wide)
    decay_out[...] = packed.astype(bf16).reshape(decay_out.shape)

    @pl.when(last)
    def _():
        pl.semaphore_wait(barrier, devices - 1)
        each(first, lambda step: greet(lax.rem(me + step, first), late_sem))

    @pl.when(jnp.logical_not(last))
    def _():
        pl.semaphore_wait(barrier, first - 1)

    def send_aux(other):
        def rows(index):
            return pl.ds(pl.multiple_of(index * block, block), block)

        def copy(source, target, send_sem, recv_sem):
            pltpu.make_async_remote_copy(
                src_ref=source,
                dst_ref=target,
                send_sem=send_sem,
                recv_sem=recv_sem,
                device_id={"row": other},
                device_id_type=MESH,
            ).start()

        above = other < half

        @pl.when(jnp.logical_or(above, jnp.logical_not(upper)))
        def _():
            copy(aux_out.at[rows(other)], aux_in.at[own], aux_sems.at[0], aux_sems.at[1])

        @pl.when(jnp.logical_and(above, upper))
        def _():
            copy(aux_out.at[rows(other + half)], help_in.at[own], help_sems.at[0], help_sems.at[1])

        @pl.when(jnp.logical_and(above, jnp.logical_not(upper)))
        def _():
            copy(
                aux_out.at[rows(other + half), pl.ds(state, state)],
                help_in.at[own, pl.ds(state, state)],
                help_sems.at[0],
                help_sems.at[2],
            )

        copy(decay_out.at[other], decay_in.at[me], decay_sems.at[0], decay_sems.at[1])

    each(soon, lambda step: send_aux(soon_peer(step)))
    aux_in[own, :] = aux_out[own, :]
    decay_in[me] = decay_out[me]

    @pl.when(upper)
    def _():
        twin = pl.ds(pl.multiple_of((me + half) * block, block), block)
        help_in[own, :] = aux_out[twin, :]


    def products(reads, writes):
        return lax.dot_general(
            reads, writes, (((1,), (1,)), ((), ())), preferred_element_type=f32
        )

    def causal(scores, allowed):
        return jnp.where(allowed, scores, 0.0).astype(bf16)

    same_col = (down & (per - 1)) == (across & (per - 1))
    earlier = (shift(down, block) > shift(across, block)) & same_col

    fold = ones(lax.broadcasted_iota(jnp.int32, (groups, 1), 0) == shift(across, per))
    slot = lax.broadcasted_iota(jnp.int32, (middle, middle), 0)
    slot = (slot & (per - 1)) * (middle // per) + shift(slot, per)
    swap = ones(slot == lax.broadcasted_iota(jnp.int32, (middle, middle), 1))

    def help_below():
        part = help_in.at[pl.ds(0, block * (half - 1))]
        pltpu.make_async_copy(part, part, help_sems.at[1]).wait()
        part = help_in.at[pl.ds(0, block * half), pl.ds(0, state)]
        pltpu.make_async_copy(part, part, help_sems.at[2]).wait()
        known = causal(
            products(help_in[:, state:], help_in[:middle, :state]), earlier[:, :middle]
        )
        scores_out[...] = dot(fold, dot(known, swap).astype(bf16)).astype(bf16)
        pltpu.make_async_remote_copy(
            src_ref=scores_out,
            dst_ref=scores_in,
            send_sem=score_sems.at[0],
            recv_sem=score_sems.at[1],
            device_id={"row": me + half},
            device_id_type=MESH,
        ).start()

    for c in range(chunks):
        x_loads[c].wait()
        sent[c] = dot(order, x_ref[:, c * width : (c + 1) * width]).astype(bf16)
        got[c, block * (devices - 1) :, :] = jnp.zeros((block, width), bf16)
        got[c, own, :] = sent[c, own, :]

        @pl.when(jnp.logical_not(tail))
        def _():
            if c:
                each(devices - 1, lambda step: send(sent.at[c], got.at[c], there_sems.at[c], peer(step)))
            else:
                scatter_soon(sent.at[c], got.at[c], there_sems.at[c])

        if not c:

            @pl.when(jnp.logical_not(last))
            def _():
                pl.semaphore_wait(late_sem, quarter)
                each(quarter, lambda step: send_aux(late_peer(step)))
                scatter_late(sent.at[c], got.at[c], there_sems.at[c])

        if c == 1:

            @pl.when(upper)
            def _():
                help_below()

    def spread(c, count=heads):
        head = lax.broadcasted_iota(jnp.int32, (count, width), 0) & (heads - 1)
        lane = lax.broadcasted_iota(jnp.int32, (count, width), 1)
        return (head == shift(lane + c * width, head_width)).astype(f32)

    def running(below, decays, c):
        own_head = spread(c, decays.shape[1]).astype(bf16)
        return dot(below, dot(decays, own_head).astype(bf16))

    restore = ones(down == home(across))
    in_row = (down >= across) & (shift(down, tile_cols) == shift(across, tile_cols))
    row_below = ones(in_row)
    for load in loads[4:]:
        load.wait()
    row_decays = turned(down, row_ref)
    own_scores = products(read_ref[...], write_ref[...])
    row_scores = causal(own_scores, in_row)
    in_home = (down >= across) & ((down & (tile_cols - 1)) == (across & (tile_cols - 1)))
    home_below = ones(in_home)
    home_decays = turned(down, col_ref)
    origin = shift(across, tile_cols)
    present = sum(jnp.where(origin == r, tile[r], 0.0) for r in range(tile_rows))
    home_scores = causal(own_scores * present, in_home)
    skip = jnp.broadcast_to(skip_ref[...], (8, heads))
    for c in range(chunks):
        cut = slice(c * width, (c + 1) * width)
        run = running(row_below, row_decays, c)
        faded = (x_ref[:, cut].astype(f32) * jnp.exp(-run)).astype(bf16)
        gain = jnp.dot(
            skip, spread(c), precision=lax.Precision.HIGHEST, preferred_element_type=f32
        )[:1]
        total[:, cut] = jnp.exp(run) * dot(row_scores, faded) + gain * x_ref[:, cut].astype(f32)

    col_below = ones((down >= across) & same_col)

    @pl.when(upper)
    def _():
        wait(aux_in, aux_sems.at[1])
        col_scores[...] = causal(products(aux_in[:, state:], aux_in[:, :state]), earlier)

    @pl.when(jnp.logical_not(upper))
    def _():
        wait(aux_in, aux_sems.at[1], half - 1)
        col_scores[:middle, middle:] = jnp.zeros((middle, middle), bf16)
        col_scores[middle:, middle:] = causal(
            products(aux_in[middle:, state:], aux_in[middle:, :state]), earlier[middle:, middle:]
        )
        pltpu.make_async_copy(scores_in, scores_in, score_sems.at[1]).wait()
        wide = lax.dot_general(
            fold, scores_in[...], (((0,), (0,)), ((), ())), preferred_element_type=f32
        )
        place = lax.broadcasted_iota(jnp.int32, (1, middle), 1)
        wide = jnp.where(shift(place, middle // per) == (down & (per - 1)), wide, 0.0)
        col_scores[:, :middle] = lax.dot_general(
            wide.astype(bf16), swap, (((1,), (1,)), ((), ())), preferred_element_type=f32
        ).astype(bf16)

    pieces = decay_in.at[pl.ds(0, devices - 1)]
    pltpu.make_async_copy(pieces, pieces, decay_sems.at[1]).wait()
    wide = lax.dot_general(
        fold,
        decay_in[...].reshape(groups, lanes),
        (((0,), (0,)), ((), ())),
        preferred_element_type=f32,
    )
    place = lax.broadcasted_iota(jnp.int32, (1, lanes), 1)
    col_decays = jnp.where(shift(place, heads) == (down & (per - 1)), wide, 0.0).astype(bf16)
    for c in range(chunks):
        run = running(col_below, col_decays, c)
        grow[c] = jnp.exp(run)
        fade[c] = jnp.exp(-run)

    for c in range(chunks):
        wait_either(got.at[c], there_sems.at[c, 1], tail)
        faded = (got[c].astype(f32) * fade[c]).astype(bf16)
        col_sent[c] = (grow[c] * dot(col_scores[...], faded)).astype(bf16)
        give_back(col_sent.at[c], col_got.at[c], back_sems.at[c])
        col_got[c, own, :] = col_sent[c, own, :]
        cut = slice(c * width, (c + 1) * width)
        run = running(home_below, home_decays, c)
        faded = (x_ref[:, cut].astype(f32) * jnp.exp(-run)).astype(bf16)
        total[:, cut] += jnp.exp(run) * dot(home_scores, faded)

    for c in range(chunks):
        cut = slice(c * width, (c + 1) * width)

        @pl.when(head)
        def _():
            col_got[c] = jnp.zeros((patches, width), bf16)

        @pl.when(jnp.logical_not(head))
        def _():
            wait(col_got.at[c], back_sems.at[c, 1])

        out_ref[:, cut] = keep(total[:, cut] + dot(restore, col_got[c])).astype(bf16)

    pltpu.make_async_copy(pieces, pieces, decay_sems.at[0]).wait()

    @pl.when(upper)
    def _():
        wait(aux_out, aux_sems.at[0], half - 1)
        wait(aux_out, help_sems.at[0], half - 1)
        pltpu.make_async_copy(scores_out, scores_out, score_sems.at[0]).wait()

    @pl.when(jnp.logical_not(upper))
    def _():
        wait(aux_out, aux_sems.at[0])
        part = help_in.at[pl.ds(0, block * half), pl.ds(0, state)]
        pltpu.make_async_copy(part, part, help_sems.at[0]).wait()

    for c in range(chunks):
        wait_either(col_sent.at[c], back_sems.at[c, 0], head)

        @pl.when(jnp.logical_not(tail))
        def _():
            wait(sent.at[c], there_sems.at[c, 0])


def fused(features, write_vecs, read_vecs, row_decay, col_decay, tile_mask, skip_gain):
    tile_rows, tile_cols, span_width = features.shape
    heads, state = row_decay.shape[-1], write_vecs.shape[-1]
    patches = tile_rows * tile_cols
    devices = lax.axis_size("row")
    width = span_width // CHUNKS

    def flat(array):
        return array.reshape(patches, array.shape[-1])

    vmem = pl.BlockSpec(memory_space=pltpu.VMEM)
    piece = (CHUNKS, patches, width)
    aux = pltpu.VMEM((patches, 2 * state), jnp.bfloat16)
    per = tile_cols // devices
    scores = pltpu.VMEM((patches // per, patches // 2), jnp.bfloat16)
    decays = pltpu.VMEM((devices, tile_rows, per * heads), jnp.bfloat16)
    result = pl.pallas_call(
        functools.partial(fused_kernel, (devices, tile_rows, tile_cols, heads)),
        out_shape=pltpu.VMEM((patches, span_width), jnp.bfloat16),
        in_specs=[pl.BlockSpec(memory_space=pl.ANY)] * 7,
        out_specs=vmem,
        scratch_shapes=[
            pltpu.SMEM((tile_rows,), jnp.int32),
            pltpu.VMEM((1, heads), jnp.float32),
            pltpu.VMEM((patches, span_width), jnp.bfloat16),
            pltpu.VMEM((patches, state), jnp.bfloat16),
            pltpu.VMEM((patches, state), jnp.bfloat16),
            pltpu.VMEM((tile_rows, heads, tile_cols), jnp.bfloat16),
            pltpu.VMEM((tile_rows, heads, tile_cols), jnp.bfloat16),
            aux,
            aux,
            aux,
            scores,
            scores,
            pltpu.VMEM((patches, patches), jnp.bfloat16),
            decays,
            decays,
            pltpu.VMEM(piece, jnp.bfloat16),
            pltpu.VMEM(piece, jnp.bfloat16),
            pltpu.VMEM(piece, jnp.bfloat16),
            pltpu.VMEM(piece, jnp.bfloat16),
            pltpu.VMEM((patches, span_width), jnp.float32),
            pltpu.VMEM(piece, jnp.float32),
            pltpu.VMEM(piece, jnp.float32),
            pltpu.SemaphoreType.DMA((6,)),
            pltpu.SemaphoreType.DMA((CHUNKS,)),
            pltpu.SemaphoreType.DMA((2,)),
            pltpu.SemaphoreType.DMA((3,)),
            pltpu.SemaphoreType.DMA((2,)),
            pltpu.SemaphoreType.DMA((2,)),
            pltpu.SemaphoreType.DMA((CHUNKS, 2)),
            pltpu.SemaphoreType.DMA((CHUNKS, 2)),
            pltpu.SemaphoreType.REGULAR,
        ],
        compiler_params=pltpu.CompilerParams(
            collective_id=0, has_side_effects=True, vmem_limit_bytes=60 * 2**20
        ),
    )(
        tile_mask.reshape(-1),
        skip_gain.reshape(1, heads),
        flat(features),
        flat(write_vecs),
        flat(read_vecs),
        jnp.swapaxes(row_decay, 1, 2),
        jnp.swapaxes(col_decay, 1, 2),
    )
    return result.reshape(features.shape)


def fits_fused(features, row_decay, tile_mask):
    tile_rows, tile_cols, span_width = features.shape
    devices = lax.axis_size("row")
    return (
        lax.axis_size("col") == 1
        and tile_mask.shape[1] == 1
        and tile_rows * devices == tile_cols
        and devices % 4 == 0
        and tile_cols <= 64
        and (tile_rows * (tile_cols // devices)) % 16 == 0
        and span_width % (CHUNKS * 128) == 0
        and (tile_cols // devices) * row_decay.shape[-1] == 128
        and tile_rows * tile_cols % 256 == 0
        and all(
            size.bit_count() == 1
            for size in (tile_rows, tile_cols, devices, span_width // row_decay.shape[-1])
        )
    )


def per_device(features, write_vecs, read_vecs, row_decay, col_decay, tile_mask, skip_gain):
    tile_rows, tile_cols, span_width = features.shape
    if fits_fused(features, row_decay, tile_mask):
        return fused(features, write_vecs, read_vecs, row_decay, col_decay, tile_mask, skip_gain)
    head_count = row_decay.shape[-1]
    block_len = tile_cols // tile_mask.shape[1]
    patch_mask = jnp.repeat(tile_mask, block_len, axis=1)
    masked = jnp.where(patch_mask[..., None] > 0, features, jnp.zeros((), features.dtype))
    moved = (
        lax.all_to_all(masked, "row", split_axis=1, concat_axis=0, tiled=True),
        lax.all_to_all(write_vecs, "row", split_axis=1, concat_axis=0, tiled=True),
        lax.all_to_all(read_vecs, "row", split_axis=1, concat_axis=0, tiled=True),
        lax.all_to_all(col_decay, "row", split_axis=1, concat_axis=0, tiled=True),
    )
    result = column_chains(moved[0], moved[1], moved[2], moved[3], block_len)
    col_out = lax.all_to_all(result, "row", split_axis=0, concat_axis=1, tiled=True)
    local_terms, read_blocks = row_terms(masked, write_vecs, read_vecs, row_decay, block_len)
    if lax.axis_size("col") == 1 and tile_mask.shape[1] == 1:
        y_row = local_terms[0].reshape(features.shape)
    else:
        zero_states = jnp.zeros((tile_rows,) + local_terms[1].shape[2:], jnp.float32)
        closing_states, unused_states = jax.vmap(enter_states)(
            local_terms[2], local_terms[1], zero_states
        )
        device_decay = jnp.prod(local_terms[2], axis=1)
        identity = (jnp.ones_like(device_decay), jnp.zeros_like(closing_states))
        decay_before, state_before = entering_2((device_decay, closing_states), "col", link, identity)
        y_row = row_finish(local_terms, read_blocks, state_before)
    skip_vector = jnp.repeat(skip_gain, span_width // head_count)
    total = y_row + col_out.astype(jnp.float32) + skip_vector * features.astype(jnp.float32)
    return (patch_mask[..., None].astype(jnp.float32) * total).astype(jnp.bfloat16)


def solution(mesh):
    return jax.shard_map(
        per_device,
        mesh=mesh,
        in_specs=(
            P(("slides", "row"), "col", None),
            P(("slides", "row"), "col", None),
            P(("slides", "row"), "col", None),
            P(("slides", "row"), "col", None),
            P(("slides", "row"), "col", None),
            P(("slides", "row"), "col"),
            P(),
        ),
        out_specs=P(("slides", "row"), "col", None),
        check_vma=False,
    )
```

```python
import functools

import jax
import jax.numpy as jnp
from jax import lax
from jax.experimental import pallas as pl
from jax.experimental.pallas import tpu as pltpu
from jax.sharding import PartitionSpec as P


def entering_2(array, axis, combine, identity):
    devices, here = (lax.axis_size(axis), lax.axis_index(axis))
    everything = jax.tree.map(
        lambda part, kind: lax.all_gather(part.astype(kind), axis),
        array,
        (jnp.bfloat16, jnp.bfloat16),
    )
    start = jax.tree.map(
        lambda part, zero: jnp.broadcast_to(jnp.asarray(zero, part.dtype), part.shape),
        array,
        identity,
    )

    def step(k, before):
        reached = k < here
        new = combine(
            before, jax.tree.map(lambda part, own: part[k].astype(own.dtype), everything, array)
        )
        return jax.tree.map(lambda a, b: jnp.where(reached, a, b), new, before)

    return lax.fori_loop(0, devices, step, start)


def block_local(masked, write_vecs, read_vecs, decays):
    blocks, length, span_width = masked.shape
    head_count = decays.shape[-1]
    head_width = span_width // head_count
    slots = jnp.arange(length)
    upto = (slots[:, None] >= slots[None, :]).astype(decays.dtype)
    running = jnp.einsum("ts,ksh->kht", upto, decays, preferred_element_type=jnp.float32)
    scores = jnp.einsum("ktn,ksn->kts", read_vecs, write_vecs, preferred_element_type=jnp.float32)
    target_slots = jnp.arange(length)
    causal = target_slots[:, None] >= target_slots[None, :]
    spread = jnp.where(causal, running[:, :, :, None] - running[:, :, None, :], jnp.float32(0.0))
    weights = jnp.where(causal, scores[:, None] * jnp.exp(spread), jnp.float32(0.0)).astype(
        jnp.bfloat16
    )
    values = masked.reshape(blocks, length, head_count, head_width)
    inside = jnp.einsum("khts,kshp->kthp", weights, values, preferred_element_type=jnp.float32)
    closing = running[:, :, -1]
    scaled = (
        write_vecs.astype(jnp.float32)[:, None] * jnp.exp(closing[:, :, None] - running)[..., None]
    ).astype(jnp.bfloat16)
    block_state = jnp.einsum("khsn,kshp->khnp", scaled, values, preferred_element_type=jnp.float32)
    return (inside, block_state, jnp.exp(closing), running)


def enter_states(damping, block_state, initial):

    def advance(carry_state, element):
        factor, fresh_term = element
        return (factor[:, None, None] * carry_state + fresh_term, carry_state)

    return lax.scan(advance, initial, (damping, block_state))


def combine_out(inside, entering, read_blocks, running):
    carried = jnp.einsum(
        "ktn,khnp->kthp", read_blocks.astype(jnp.float32), entering, precision=lax.Precision.HIGHEST
    )
    total = inside + carried * jnp.swapaxes(jnp.exp(running), 1, 2)[..., None]
    return total.reshape(total.shape[0] * total.shape[1], total.shape[2] * total.shape[3])


def to_blocks(array, block_len):
    return array.reshape(
        array.shape[:-2] + (array.shape[-2] // block_len, block_len, array.shape[-1])
    )


def column_chains(masked, write_vecs, read_vecs, decays, block_len):

    def one_column(masked_c, write_c, read_c, decay_c):
        read_blocks = to_blocks(read_c, block_len)
        inside, block_state, damping, running = block_local(
            to_blocks(masked_c, block_len),
            to_blocks(write_c, block_len),
            read_blocks,
            to_blocks(decay_c, block_len),
        )
        if read_blocks.shape[0] == 1:
            return inside.reshape(masked_c.shape)
        zero_state = jnp.zeros(block_state.shape[1:], jnp.float32)
        closing_state, entering = enter_states(damping, block_state, zero_state)
        return combine_out(inside, entering, read_blocks, running)

    results = jax.vmap(one_column, in_axes=1, out_axes=1)(masked, write_vecs, read_vecs, decays)
    return results.astype(jnp.bfloat16)


def row_terms(masked, write_vecs, read_vecs, decays, block_len):
    read_blocks = to_blocks(read_vecs, block_len)
    local_terms = jax.vmap(block_local)(
        to_blocks(masked, block_len),
        to_blocks(write_vecs, block_len),
        read_blocks,
        to_blocks(decays, block_len),
    )
    return (local_terms, read_blocks)


def row_finish(local_terms, read_blocks, incoming):
    inside, block_state, damping, running = local_terms
    closing_state, entering = jax.vmap(enter_states)(damping, block_state, incoming)
    return jax.vmap(combine_out)(inside, entering, read_blocks, running)


def link(earlier, later):
    return (earlier[0] * later[0], later[0][..., None, None] * earlier[1] + later[1])


MESH = pl.DeviceIdType.MESH
CHUNKS = 4


def fused_kernel(
    shape,
    mask_hbm,
    skip_hbm,
    x_hbm,
    write_hbm,
    read_hbm,
    row_hbm,
    col_hbm,
    out_ref,
    mask_ref,
    skip_ref,
    x_ref,
    write_ref,
    read_ref,
    row_ref,
    col_ref,
    aux_out,
    aux_in,
    help_in,
    scores_out,
    scores_in,
    col_scores,
    decay_out,
    decay_in,
    pair_x,
    pair_write,
    pair_col,
    kept_write,
    sent,
    got,
    col_sent,
    col_got,
    total,
    grow,
    fade,
    load_sems,
    x_sems,
    aux_sems,
    help_sems,
    score_sems,
    decay_sems,
    pair_sems,
    there_sems,
    back_sems,
    late_sem,
):
    devices, tile_rows, tile_cols, heads = shape
    per = tile_cols // devices
    block = tile_rows * per
    patches = tile_rows * tile_cols
    chunks, _, width = sent.shape
    head_width = chunks * width // heads
    state = write_ref.shape[-1]
    f32, bf16 = jnp.float32, jnp.bfloat16
    me = lax.axis_index("row")
    own = pl.ds(pl.multiple_of(me * block, block), block)

    def dot(a, b):
        return jnp.dot(a, b, preferred_element_type=f32)

    quarter, half = devices // 4, devices // 2
    middle = patches // 2
    upper = me < half
    first = devices - quarter
    last = me >= first
    soon = jnp.where(last, devices - 1, first - 1)

    def peer(step):
        return lax.rem(me + 1 + step, devices)

    def soon_peer(step):
        return lax.rem(me + 1 + step, soon + 1)

    def late_peer(step):
        return first + lax.rem(me + step, quarter)

    barrier = pltpu.get_barrier_semaphore()

    def each(steps, act):
        def body(step, carry):
            act(step)
            return carry

        lax.fori_loop(0, steps, body, 0)

    def greet(other, semaphore=barrier):
        pl.semaphore_signal(semaphore, inc=1, device_id={"row": other}, device_id_type=MESH)

    @pl.when(last)
    def _():
        each(quarter - 1, lambda step: greet(first + lax.rem(me + 1 + step, quarter)))

    @pl.when(jnp.logical_not(last))
    def _():
        each(devices - 1, lambda step: greet(peer(step)))

    loads = [
        pltpu.make_async_copy(source, target, load_sems.at[i])
        for i, (source, target) in enumerate(
            (
                (mask_hbm, mask_ref),
                (write_hbm, write_ref),
                (read_hbm, read_ref),
                (col_hbm, col_ref),
                (row_hbm, row_ref),
                (skip_hbm, skip_ref),
            )
        )
    ]
    x_loads = [
        pltpu.make_async_copy(
            x_hbm.at[:, pl.ds(c * width, width)], x_ref.at[:, pl.ds(c * width, width)], x_sems.at[c]
        )
        for c in range(chunks)
    ]
    for load in loads[:4] + x_loads + loads[4:]:
        load.start()

    def send(source, target, sems, other):
        pltpu.make_async_remote_copy(
            src_ref=source.at[pl.ds(pl.multiple_of(other * block, block), block)],
            dst_ref=target.at[own],
            send_sem=sems.at[0],
            recv_sem=sems.at[1],
            device_id={"row": other},
            device_id_type=MESH,
        ).start()

    tail = me >= devices - 2
    head = me < 2
    odd = (me & 1) == 1

    def scatter_soon(source, target, sems):
        each(soon, lambda step: send(source, target, sems, soon_peer(step)))

    def scatter_late(source, target, sems):
        each(quarter, lambda step: send(source, target, sems, late_peer(step)))

    def give_back(source, target, sems):
        def act(step):
            other = peer(step)

            @pl.when(other >= 2)
            def _():
                send(source, target, sems, other)

        each(devices - 1, act)

    def wait(buffer, sem, count=devices - 1):
        part = buffer.at[pl.ds(0, block * count)]
        pltpu.make_async_copy(part, part, sem).wait()

    def wait_either(buffer, sem, one_more):
        @pl.when(one_more)
        def _():
            wait(buffer, sem, devices - 2)

        @pl.when(jnp.logical_not(one_more))
        def _():
            wait(buffer, sem, devices - 3)

    pairs = [(x_ref, pair_x), (kept_write, pair_write), (col_ref, pair_col)]

    def shift(i, size):
        return lax.shift_right_logical(i, size.bit_length() - 1)

    down = lax.broadcasted_iota(jnp.int32, (patches, 1), 0)
    across = lax.broadcasted_iota(jnp.int32, (1, patches), 1)

    def home(i):
        row = shift(i, per) & (tile_rows - 1)
        return row * tile_cols + shift(i, block) * per + (i & (per - 1))

    def ones(where):
        return where.astype(f32).astype(bf16)

    from_home = home(down)
    order = ones(from_home == across)

    def turned(places, ref):
        lanes = lax.broadcasted_iota(jnp.int32, (1, tile_cols), 1)
        return sum(
            lax.dot_general(
                ones(places == lanes + r * tile_cols),
                ref[r],
                (((1,), (1,)), ((), ())),
                preferred_element_type=f32,
            )
            for r in range(tile_rows)
        ).astype(bf16)

    x_loads[0].wait()
    sent[0] = dot(order, x_ref[:, :width]).astype(bf16)

    @pl.when(last)
    def _():
        pl.semaphore_wait(barrier, devices - 1)
        each(first, lambda step: greet(lax.rem(me + step, first), late_sem))

    @pl.when(jnp.logical_not(last))
    def _():
        pl.semaphore_wait(barrier, first - 1)

    @pl.when(jnp.logical_not(tail))
    def _():
        scatter_soon(sent.at[0], got.at[0], there_sems.at[0])

    for load in loads[:4]:
        load.wait()
    tile = [mask_ref[r].astype(f32) for r in range(tile_rows)]

    def keep(value):
        return jnp.concatenate(
            [value[r * tile_cols : (r + 1) * tile_cols] * tile[r] for r in range(tile_rows)]
        )

    kept_write[...] = keep(write_ref[...].astype(f32)).astype(bf16)
    aux_out[:, :state] = dot(order, kept_write[...]).astype(bf16)
    aux_out[:, state : 2 * state] = dot(order, read_ref[...]).astype(bf16)
    lanes = per * heads
    groups = patches // per
    lane_head = lax.broadcasted_iota(jnp.int32, (heads, lanes), 1) & (heads - 1)
    copies = ones(lax.broadcasted_iota(jnp.int32, (heads, lanes), 0) == lane_head)
    lane_col = shift(lax.broadcasted_iota(jnp.int32, (tile_cols, lanes), 1), heads)
    kept = (lax.broadcasted_iota(jnp.int32, (tile_cols, lanes), 0) & (per - 1)) == lane_col
    group = lax.broadcasted_iota(jnp.int32, (groups, tile_cols), 0)
    group_col = lax.broadcasted_iota(jnp.int32, (groups, tile_cols), 1)
    packed = jnp.zeros((groups, lanes), f32)
    for r in range(tile_rows):
        wide = lax.dot_general(
            col_ref[r], copies, (((0,), (0,)), ((), ())), preferred_element_type=f32
        )
        wide = jnp.where(kept, wide, 0.0).astype(bf16)
        packed += dot(ones(group == shift(group_col, per) * tile_rows + r), wide)
    decay_out[...] = packed.astype(bf16).reshape(decay_out.shape)

    def send_aux(other):
        def rows(index):
            return pl.ds(pl.multiple_of(index * block, block), block)

        def copy(source, target, send_sem, recv_sem):
            pltpu.make_async_remote_copy(
                src_ref=source,
                dst_ref=target,
                send_sem=send_sem,
                recv_sem=recv_sem,
                device_id={"row": other},
                device_id_type=MESH,
            ).start()

        above = other < half

        @pl.when(jnp.logical_or(above, jnp.logical_not(upper)))
        def _():
            copy(aux_out.at[rows(other)], aux_in.at[own], aux_sems.at[0], aux_sems.at[1])

        @pl.when(jnp.logical_and(above, upper))
        def _():
            copy(aux_out.at[rows(other + half)], help_in.at[own], help_sems.at[0], help_sems.at[1])

        @pl.when(jnp.logical_and(above, jnp.logical_not(upper)))
        def _():
            copy(
                aux_out.at[rows(other + half), pl.ds(state, state)],
                help_in.at[own, pl.ds(state, state)],
                help_sems.at[0],
                help_sems.at[2],
            )

        copy(decay_out.at[other], decay_in.at[me], decay_sems.at[0], decay_sems.at[1])

    each(soon, lambda step: send_aux(soon_peer(step)))
    aux_in[own, :] = aux_out[own, :]
    decay_in[me] = decay_out[me]

    @pl.when(upper)
    def _():
        twin = pl.ds(pl.multiple_of((me + half) * block, block), block)
        help_in[own, :] = aux_out[twin, :]


    def products(reads, writes):
        return lax.dot_general(
            reads, writes, (((1,), (1,)), ((), ())), preferred_element_type=f32
        )

    def causal(scores, allowed):
        return jnp.where(allowed, scores, 0.0).astype(bf16)

    same_col = (down & (per - 1)) == (across & (per - 1))
    earlier = (shift(down, 2 * block) > shift(across, 2 * block)) & same_col

    fold = ones(lax.broadcasted_iota(jnp.int32, (groups, 1), 0) == shift(across, per))
    slot = lax.broadcasted_iota(jnp.int32, (middle, middle), 0)
    slot = (slot & (per - 1)) * (middle // per) + shift(slot, per)
    swap = ones(slot == lax.broadcasted_iota(jnp.int32, (middle, middle), 1))

    def help_below():
        part = help_in.at[pl.ds(0, block * (half - 1))]
        pltpu.make_async_copy(part, part, help_sems.at[1]).wait()
        part = help_in.at[pl.ds(0, block * half), pl.ds(0, state)]
        pltpu.make_async_copy(part, part, help_sems.at[2]).wait()
        known = causal(
            products(help_in[:, state:], help_in[:middle, :state]), earlier[:, :middle]
        )
        scores_out[...] = dot(fold, dot(known, swap).astype(bf16)).astype(bf16)
        pltpu.make_async_remote_copy(
            src_ref=scores_out,
            dst_ref=scores_in,
            send_sem=score_sems.at[0],
            recv_sem=score_sems.at[1],
            device_id={"row": me + half},
            device_id_type=MESH,
        ).start()

    for c in range(chunks):
        if c:
            x_loads[c].wait()
            sent[c] = dot(order, x_ref[:, c * width : (c + 1) * width]).astype(bf16)
        got[c, block * (devices - 2) :, :] = jnp.zeros((2 * block, width), bf16)
        got[c, own, :] = sent[c, own, :]

        if c:

            @pl.when(jnp.logical_not(tail))
            def _():
                each(devices - 1, lambda step: send(sent.at[c], got.at[c], there_sems.at[c], peer(step)))

        else:

            @pl.when(jnp.logical_not(last))
            def _():
                pl.semaphore_wait(late_sem, quarter)
                each(quarter, lambda step: send_aux(late_peer(step)))
                scatter_late(sent.at[c], got.at[c], there_sems.at[c])

        if c == 2:

            @pl.when(upper)
            def _():
                help_below()

    @pl.when(jnp.logical_not(odd))
    def _():
        for i, (source, target) in enumerate(pairs):
            pltpu.make_async_remote_copy(
                src_ref=source,
                dst_ref=target,
                send_sem=pair_sems.at[i, 0],
                recv_sem=pair_sems.at[i, 1],
                device_id={"row": me + 1},
                device_id_type=MESH,
            ).start()

    def spread(c, count=heads):
        head = lax.broadcasted_iota(jnp.int32, (count, width), 0) & (heads - 1)
        lane = lax.broadcasted_iota(jnp.int32, (count, width), 1)
        return (head == shift(lane + c * width, head_width)).astype(f32)

    def running(below, decays, c):
        own_head = spread(c, decays.shape[1]).astype(bf16)
        return dot(below, dot(decays, own_head).astype(bf16))

    restore = ones(down == home(across))
    in_row = (down >= across) & (shift(down, tile_cols) == shift(across, tile_cols))
    row_below = ones(in_row)
    for load in loads[4:]:
        load.wait()
    row_decays = turned(down, row_ref)
    own_scores = products(read_ref[...], write_ref[...])
    row_scores = causal(own_scores, in_row)
    in_home = (down >= across) & ((down & (tile_cols - 1)) == (across & (tile_cols - 1)))
    home_below = ones(in_home)
    home_decays = turned(down, col_ref)
    origin = shift(across, tile_cols)
    present = sum(jnp.where(origin == r, tile[r], 0.0) for r in range(tile_rows))
    home_scores = causal(own_scores * present, in_home)
    skip = jnp.broadcast_to(skip_ref[...], (8, heads))
    for c in range(chunks):
        cut = slice(c * width, (c + 1) * width)
        run = running(row_below, row_decays, c)
        faded = (x_ref[:, cut].astype(f32) * jnp.exp(-run)).astype(bf16)
        gain = jnp.dot(
            skip, spread(c), precision=lax.Precision.HIGHEST, preferred_element_type=f32
        )[:1]
        total[:, cut] = jnp.exp(run) * dot(row_scores, faded) + gain * x_ref[:, cut].astype(f32)

    col_below = ones((down >= across) & same_col)

    @pl.when(upper)
    def _():
        wait(aux_in, aux_sems.at[1])
        col_scores[...] = causal(products(aux_in[:, state:], aux_in[:, :state]), earlier)

    @pl.when(jnp.logical_not(upper))
    def _():
        wait(aux_in, aux_sems.at[1], half - 1)
        col_scores[:middle, middle:] = jnp.zeros((middle, middle), bf16)
        col_scores[middle:, middle:] = causal(
            products(aux_in[middle:, state:], aux_in[middle:, :state]), earlier[middle:, middle:]
        )
        pltpu.make_async_copy(scores_in, scores_in, score_sems.at[1]).wait()
        wide = lax.dot_general(
            fold, scores_in[...], (((0,), (0,)), ((), ())), preferred_element_type=f32
        )
        place = lax.broadcasted_iota(jnp.int32, (1, middle), 1)
        wide = jnp.where(shift(place, middle // per) == (down & (per - 1)), wide, 0.0)
        col_scores[:, :middle] = lax.dot_general(
            wide.astype(bf16), swap, (((1,), (1,)), ((), ())), preferred_element_type=f32
        ).astype(bf16)

    pieces = decay_in.at[pl.ds(0, devices - 1)]
    pltpu.make_async_copy(pieces, pieces, decay_sems.at[1]).wait()
    wide = lax.dot_general(
        fold,
        decay_in[...].reshape(groups, lanes),
        (((0,), (0,)), ((), ())),
        preferred_element_type=f32,
    )
    place = lax.broadcasted_iota(jnp.int32, (1, lanes), 1)
    col_decays = jnp.where(shift(place, heads) == (down & (per - 1)), wide, 0.0).astype(bf16)
    for c in range(chunks):
        run = running(col_below, col_decays, c)
        grow[c] = jnp.exp(run)
        fade[c] = jnp.exp(-run)

    for c in range(chunks):
        wait_either(got.at[c], there_sems.at[c, 1], tail)
        faded = (got[c].astype(f32) * fade[c]).astype(bf16)
        col_sent[c] = (grow[c] * dot(col_scores[...], faded)).astype(bf16)
        give_back(col_sent.at[c], col_got.at[c], back_sems.at[c])
        col_got[c, own, :] = col_sent[c, own, :]

    for c in range(chunks):
        cut = slice(c * width, (c + 1) * width)
        run = running(home_below, home_decays, c)
        grow[c] = jnp.exp(run)
        faded = (x_ref[:, cut].astype(f32) * jnp.exp(-run)).astype(bf16)
        total[:, cut] += grow[c] * dot(home_scores, faded)

    @pl.when(odd)
    def _():
        for i, (source, target) in enumerate(pairs):
            pltpu.make_async_copy(target, target, pair_sems.at[i, 1]).wait()
        alike = (down & (tile_cols - 1)) == (across & (tile_cols - 1))
        pair_after = ones((shift(down, tile_cols) < shift(across, tile_cols)) & alike)
        pair_decays = turned(down, pair_col)
        pair_scores = causal(products(read_ref[...], pair_write[...]), alike)
        for c in range(chunks):
            cut = slice(c * width, (c + 1) * width)
            run = running(pair_after, pair_decays, c)
            faded = (pair_x[:, cut].astype(f32) * jnp.exp(run)).astype(bf16)
            total[:, cut] += grow[c] * dot(pair_scores, faded)

    @pl.when(jnp.logical_not(odd))
    def _():
        for i, (source, target) in enumerate(pairs):
            pltpu.make_async_copy(source, source, pair_sems.at[i, 0]).wait()

    for c in range(chunks):
        cut = slice(c * width, (c + 1) * width)

        @pl.when(head)
        def _():
            col_got[c] = jnp.zeros((patches, width), bf16)

        @pl.when(jnp.logical_not(head))
        def _():
            wait(col_got.at[c], back_sems.at[c, 1])

        out_ref[:, cut] = keep(total[:, cut] + dot(restore, col_got[c])).astype(bf16)

    pltpu.make_async_copy(pieces, pieces, decay_sems.at[0]).wait()

    @pl.when(upper)
    def _():
        wait(aux_out, aux_sems.at[0], half - 1)
        wait(aux_out, help_sems.at[0], half - 1)
        pltpu.make_async_copy(scores_out, scores_out, score_sems.at[0]).wait()

    @pl.when(jnp.logical_not(upper))
    def _():
        wait(aux_out, aux_sems.at[0])
        part = help_in.at[pl.ds(0, block * half), pl.ds(0, state)]
        pltpu.make_async_copy(part, part, help_sems.at[0]).wait()

    for c in range(chunks):
        wait_either(col_sent.at[c], back_sems.at[c, 0], head)

        @pl.when(jnp.logical_not(tail))
        def _():
            wait(sent.at[c], there_sems.at[c, 0])


def fused(features, write_vecs, read_vecs, row_decay, col_decay, tile_mask, skip_gain):
    tile_rows, tile_cols, span_width = features.shape
    heads, state = row_decay.shape[-1], write_vecs.shape[-1]
    patches = tile_rows * tile_cols
    devices = lax.axis_size("row")
    width = span_width // CHUNKS

    def flat(array):
        return array.reshape(patches, array.shape[-1])

    vmem = pl.BlockSpec(memory_space=pltpu.VMEM)
    piece = (CHUNKS, patches, width)
    aux = pltpu.VMEM((patches, 2 * state), jnp.bfloat16)
    per = tile_cols // devices
    scores = pltpu.VMEM((patches // per, patches // 2), jnp.bfloat16)
    decays = pltpu.VMEM((devices, tile_rows, per * heads), jnp.bfloat16)
    result = pl.pallas_call(
        functools.partial(fused_kernel, (devices, tile_rows, tile_cols, heads)),
        out_shape=pltpu.VMEM((patches, span_width), jnp.bfloat16),
        in_specs=[pl.BlockSpec(memory_space=pl.ANY)] * 7,
        out_specs=vmem,
        scratch_shapes=[
            pltpu.SMEM((tile_rows,), jnp.int32),
            pltpu.VMEM((1, heads), jnp.float32),
            pltpu.VMEM((patches, span_width), jnp.bfloat16),
            pltpu.VMEM((patches, state), jnp.bfloat16),
            pltpu.VMEM((patches, state), jnp.bfloat16),
            pltpu.VMEM((tile_rows, heads, tile_cols), jnp.bfloat16),
            pltpu.VMEM((tile_rows, heads, tile_cols), jnp.bfloat16),
            aux,
            aux,
            aux,
            scores,
            scores,
            pltpu.VMEM((patches, patches), jnp.bfloat16),
            decays,
            decays,
            pltpu.VMEM((patches, span_width), jnp.bfloat16),
            pltpu.VMEM((patches, state), jnp.bfloat16),
            pltpu.VMEM((tile_rows, heads, tile_cols), jnp.bfloat16),
            pltpu.VMEM((patches, state), jnp.bfloat16),
            pltpu.VMEM(piece, jnp.bfloat16),
            pltpu.VMEM(piece, jnp.bfloat16),
            pltpu.VMEM(piece, jnp.bfloat16),
            pltpu.VMEM(piece, jnp.bfloat16),
            pltpu.VMEM((patches, span_width), jnp.float32),
            pltpu.VMEM(piece, jnp.float32),
            pltpu.VMEM(piece, jnp.float32),
            pltpu.SemaphoreType.DMA((6,)),
            pltpu.SemaphoreType.DMA((CHUNKS,)),
            pltpu.SemaphoreType.DMA((2,)),
            pltpu.SemaphoreType.DMA((3,)),
            pltpu.SemaphoreType.DMA((2,)),
            pltpu.SemaphoreType.DMA((2,)),
            pltpu.SemaphoreType.DMA((3, 2)),
            pltpu.SemaphoreType.DMA((CHUNKS, 2)),
            pltpu.SemaphoreType.DMA((CHUNKS, 2)),
            pltpu.SemaphoreType.REGULAR,
        ],
        compiler_params=pltpu.CompilerParams(
            collective_id=0, has_side_effects=True, vmem_limit_bytes=60 * 2**20
        ),
    )(
        tile_mask.reshape(-1),
        skip_gain.reshape(1, heads),
        flat(features),
        flat(write_vecs),
        flat(read_vecs),
        jnp.swapaxes(row_decay, 1, 2),
        jnp.swapaxes(col_decay, 1, 2),
    )
    return result.reshape(features.shape)


def fits_fused(features, row_decay, tile_mask):
    tile_rows, tile_cols, span_width = features.shape
    devices = lax.axis_size("row")
    return (
        lax.axis_size("col") == 1
        and tile_mask.shape[1] == 1
        and tile_rows * devices == tile_cols
        and devices % 4 == 0
        and tile_cols <= 64
        and (tile_rows * (tile_cols // devices)) % 16 == 0
        and span_width % (CHUNKS * 128) == 0
        and (tile_cols // devices) * row_decay.shape[-1] == 128
        and tile_rows * tile_cols % 256 == 0
        and all(
            size.bit_count() == 1
            for size in (tile_rows, tile_cols, devices, span_width // row_decay.shape[-1])
        )
    )


def per_device(features, write_vecs, read_vecs, row_decay, col_decay, tile_mask, skip_gain):
    tile_rows, tile_cols, span_width = features.shape
    if fits_fused(features, row_decay, tile_mask):
        return fused(features, write_vecs, read_vecs, row_decay, col_decay, tile_mask, skip_gain)
    head_count = row_decay.shape[-1]
    block_len = tile_cols // tile_mask.shape[1]
    patch_mask = jnp.repeat(tile_mask, block_len, axis=1)
    masked = jnp.where(patch_mask[..., None] > 0, features, jnp.zeros((), features.dtype))
    moved = (
        lax.all_to_all(masked, "row", split_axis=1, concat_axis=0, tiled=True),
        lax.all_to_all(write_vecs, "row", split_axis=1, concat_axis=0, tiled=True),
        lax.all_to_all(read_vecs, "row", split_axis=1, concat_axis=0, tiled=True),
        lax.all_to_all(col_decay, "row", split_axis=1, concat_axis=0, tiled=True),
    )
    result = column_chains(moved[0], moved[1], moved[2], moved[3], block_len)
    col_out = lax.all_to_all(result, "row", split_axis=0, concat_axis=1, tiled=True)
    local_terms, read_blocks = row_terms(masked, write_vecs, read_vecs, row_decay, block_len)
    if lax.axis_size("col") == 1 and tile_mask.shape[1] == 1:
        y_row = local_terms[0].reshape(features.shape)
    else:
        zero_states = jnp.zeros((tile_rows,) + local_terms[1].shape[2:], jnp.float32)
        closing_states, unused_states = jax.vmap(enter_states)(
            local_terms[2], local_terms[1], zero_states
        )
        device_decay = jnp.prod(local_terms[2], axis=1)
        identity = (jnp.ones_like(device_decay), jnp.zeros_like(closing_states))
        decay_before, state_before = entering_2((device_decay, closing_states), "col", link, identity)
        y_row = row_finish(local_terms, read_blocks, state_before)
    skip_vector = jnp.repeat(skip_gain, span_width // head_count)
    total = y_row + col_out.astype(jnp.float32) + skip_vector * features.astype(jnp.float32)
    return (patch_mask[..., None].astype(jnp.float32) * total).astype(jnp.bfloat16)


def solution(mesh):
    return jax.shard_map(
        per_device,
        mesh=mesh,
        in_specs=(
            P(("slides", "row"), "col", None),
            P(("slides", "row"), "col", None),
            P(("slides", "row"), "col", None),
            P(("slides", "row"), "col", None),
            P(("slides", "row"), "col", None),
            P(("slides", "row"), "col"),
            P(),
        ),
        out_specs=P(("slides", "row"), "col", None),
        check_vma=False,
    )
```

```python
import functools

import jax
import jax.numpy as jnp
from jax import lax
from jax.experimental import pallas as pl
from jax.experimental.pallas import tpu as pltpu
from jax.sharding import PartitionSpec as P


def entering_2(array, axis, combine, identity):
    devices, here = (lax.axis_size(axis), lax.axis_index(axis))
    everything = jax.tree.map(
        lambda part, kind: lax.all_gather(part.astype(kind), axis),
        array,
        (jnp.bfloat16, jnp.bfloat16),
    )
    start = jax.tree.map(
        lambda part, zero: jnp.broadcast_to(jnp.asarray(zero, part.dtype), part.shape),
        array,
        identity,
    )

    def step(k, before):
        reached = k < here
        new = combine(
            before, jax.tree.map(lambda part, own: part[k].astype(own.dtype), everything, array)
        )
        return jax.tree.map(lambda a, b: jnp.where(reached, a, b), new, before)

    return lax.fori_loop(0, devices, step, start)


def block_local(masked, write_vecs, read_vecs, decays):
    blocks, length, span_width = masked.shape
    head_count = decays.shape[-1]
    head_width = span_width // head_count
    slots = jnp.arange(length)
    upto = (slots[:, None] >= slots[None, :]).astype(decays.dtype)
    running = jnp.einsum("ts,ksh->kht", upto, decays, preferred_element_type=jnp.float32)
    scores = jnp.einsum("ktn,ksn->kts", read_vecs, write_vecs, preferred_element_type=jnp.float32)
    target_slots = jnp.arange(length)
    causal = target_slots[:, None] >= target_slots[None, :]
    spread = jnp.where(causal, running[:, :, :, None] - running[:, :, None, :], jnp.float32(0.0))
    weights = jnp.where(causal, scores[:, None] * jnp.exp(spread), jnp.float32(0.0)).astype(
        jnp.bfloat16
    )
    values = masked.reshape(blocks, length, head_count, head_width)
    inside = jnp.einsum("khts,kshp->kthp", weights, values, preferred_element_type=jnp.float32)
    closing = running[:, :, -1]
    scaled = (
        write_vecs.astype(jnp.float32)[:, None] * jnp.exp(closing[:, :, None] - running)[..., None]
    ).astype(jnp.bfloat16)
    block_state = jnp.einsum("khsn,kshp->khnp", scaled, values, preferred_element_type=jnp.float32)
    return (inside, block_state, jnp.exp(closing), running)


def enter_states(damping, block_state, initial):

    def advance(carry_state, element):
        factor, fresh_term = element
        return (factor[:, None, None] * carry_state + fresh_term, carry_state)

    return lax.scan(advance, initial, (damping, block_state))


def combine_out(inside, entering, read_blocks, running):
    carried = jnp.einsum(
        "ktn,khnp->kthp", read_blocks.astype(jnp.float32), entering, precision=lax.Precision.HIGHEST
    )
    total = inside + carried * jnp.swapaxes(jnp.exp(running), 1, 2)[..., None]
    return total.reshape(total.shape[0] * total.shape[1], total.shape[2] * total.shape[3])


def to_blocks(array, block_len):
    return array.reshape(
        array.shape[:-2] + (array.shape[-2] // block_len, block_len, array.shape[-1])
    )


def column_chains(masked, write_vecs, read_vecs, decays, block_len):

    def one_column(masked_c, write_c, read_c, decay_c):
        read_blocks = to_blocks(read_c, block_len)
        inside, block_state, damping, running = block_local(
            to_blocks(masked_c, block_len),
            to_blocks(write_c, block_len),
            read_blocks,
            to_blocks(decay_c, block_len),
        )
        if read_blocks.shape[0] == 1:
            return inside.reshape(masked_c.shape)
        zero_state = jnp.zeros(block_state.shape[1:], jnp.float32)
        closing_state, entering = enter_states(damping, block_state, zero_state)
        return combine_out(inside, entering, read_blocks, running)

    results = jax.vmap(one_column, in_axes=1, out_axes=1)(masked, write_vecs, read_vecs, decays)
    return results.astype(jnp.bfloat16)


def row_terms(masked, write_vecs, read_vecs, decays, block_len):
    read_blocks = to_blocks(read_vecs, block_len)
    local_terms = jax.vmap(block_local)(
        to_blocks(masked, block_len),
        to_blocks(write_vecs, block_len),
        read_blocks,
        to_blocks(decays, block_len),
    )
    return (local_terms, read_blocks)


def row_finish(local_terms, read_blocks, incoming):
    inside, block_state, damping, running = local_terms
    closing_state, entering = jax.vmap(enter_states)(damping, block_state, incoming)
    return jax.vmap(combine_out)(inside, entering, read_blocks, running)


def link(earlier, later):
    return (earlier[0] * later[0], later[0][..., None, None] * earlier[1] + later[1])


MESH = pl.DeviceIdType.MESH
CHUNKS = 4


def fused_kernel(
    shape,
    mask_hbm,
    skip_hbm,
    x_hbm,
    write_hbm,
    read_hbm,
    row_hbm,
    col_hbm,
    out_ref,
    mask_ref,
    skip_ref,
    x_ref,
    write_ref,
    read_ref,
    row_ref,
    col_ref,
    aux_out,
    aux_in,
    help_in,
    scores_out,
    scores_in,
    col_scores,
    decay_out,
    decay_in,
    pair_x,
    pair_write,
    pair_col,
    kept_write,
    sent,
    got,
    col_sent,
    col_got,
    total,
    grow,
    fade,
    load_sems,
    x_sems,
    aux_sems,
    help_sems,
    score_sems,
    decay_sems,
    pair_sems,
    there_sems,
    back_sems,
    late_sem,
):
    devices, tile_rows, tile_cols, heads = shape
    per = tile_cols // devices
    block = tile_rows * per
    patches = tile_rows * tile_cols
    chunks, _, width = sent.shape
    head_width = chunks * width // heads
    state = write_ref.shape[-1]
    f32, bf16 = jnp.float32, jnp.bfloat16
    me = lax.axis_index("row")
    own = pl.ds(pl.multiple_of(me * block, block), block)

    def dot(a, b):
        return jnp.dot(a, b, preferred_element_type=f32)

    quarter, half = devices // 4, devices // 2
    middle = patches // 2
    upper = me < half
    first = devices - quarter
    last = me >= first
    soon = jnp.where(last, devices - 1, first - 1)

    def peer(step):
        return lax.rem(me + 1 + step, devices)

    def soon_peer(step):
        return lax.rem(me + 1 + step, soon + 1)

    def late_peer(step):
        return first + lax.rem(me + step, quarter)

    barrier = pltpu.get_barrier_semaphore()

    def each(steps, act):
        def body(step, carry):
            act(step)
            return carry

        lax.fori_loop(0, steps, body, 0)

    def greet(other, semaphore=barrier):
        pl.semaphore_signal(semaphore, inc=1, device_id={"row": other}, device_id_type=MESH)

    @pl.when(last)
    def _():
        each(quarter - 1, lambda step: greet(first + lax.rem(me + 1 + step, quarter)))

    @pl.when(jnp.logical_not(last))
    def _():
        each(devices - 1, lambda step: greet(lax.rem(me - 1 - step + devices, devices)))

    loads = [
        pltpu.make_async_copy(source, target, load_sems.at[i])
        for i, (source, target) in enumerate(
            (
                (mask_hbm, mask_ref),
                (write_hbm, write_ref),
                (read_hbm, read_ref),
                (col_hbm, col_ref),
                (row_hbm, row_ref),
                (skip_hbm, skip_ref),
            )
        )
    ]
    x_loads = [
        pltpu.make_async_copy(
            x_hbm.at[:, pl.ds(c * width, width)], x_ref.at[:, pl.ds(c * width, width)], x_sems.at[c]
        )
        for c in range(chunks)
    ]
    for load in loads[:4] + x_loads + loads[4:]:
        load.start()

    def send(source, target, sems, other):
        pltpu.make_async_remote_copy(
            src_ref=source.at[pl.ds(pl.multiple_of(other * block, block), block)],
            dst_ref=target.at[own],
            send_sem=sems.at[0],
            recv_sem=sems.at[1],
            device_id={"row": other},
            device_id_type=MESH,
        ).start()

    tail = me >= devices - 2
    head = me < 2
    odd = (me & 1) == 1

    def scatter_soon(source, target, sems):
        each(soon, lambda step: send(source, target, sems, soon_peer(step)))

    def scatter_late(source, target, sems):
        each(quarter, lambda step: send(source, target, sems, late_peer(step)))

    def give_back(source, target, sems):
        def act(step):
            other = peer(step)

            @pl.when(other >= 2)
            def _():
                send(source, target, sems, other)

        each(devices - 1, act)

    def wait(buffer, sem, count=devices - 1):
        part = buffer.at[pl.ds(0, block * count)]
        pltpu.make_async_copy(part, part, sem).wait()

    def wait_either(buffer, sem, one_more):
        @pl.when(one_more)
        def _():
            wait(buffer, sem, devices - 2)

        @pl.when(jnp.logical_not(one_more))
        def _():
            wait(buffer, sem, devices - 3)

    pairs = [(x_ref, pair_x), (kept_write, pair_write), (col_ref, pair_col)]

    def shift(i, size):
        return lax.shift_right_logical(i, size.bit_length() - 1)

    down = lax.broadcasted_iota(jnp.int32, (patches, 1), 0)
    across = lax.broadcasted_iota(jnp.int32, (1, patches), 1)

    def home(i):
        row = shift(i, per) & (tile_rows - 1)
        return row * tile_cols + shift(i, block) * per + (i & (per - 1))

    def ones(where):
        return where.astype(f32).astype(bf16)

    from_home = home(down)
    order = ones(from_home == across)

    def turned(places, ref):
        lanes = lax.broadcasted_iota(jnp.int32, (1, tile_cols), 1)
        return sum(
            lax.dot_general(
                ones(places == lanes + r * tile_cols),
                ref[r],
                (((1,), (1,)), ((), ())),
                preferred_element_type=f32,
            )
            for r in range(tile_rows)
        ).astype(bf16)

    x_loads[0].wait()
    sent[0] = dot(order, x_ref[:, :width]).astype(bf16)

    @pl.when(last)
    def _():
        pl.semaphore_wait(barrier, devices - 1)
        each(first, lambda step: greet(first - 1 - lax.rem(me + step, first), late_sem))

    @pl.when(jnp.logical_not(last))
    def _():
        pl.semaphore_wait(barrier, first - 1)

    @pl.when(jnp.logical_not(tail))
    def _():
        scatter_soon(sent.at[0], got.at[0], there_sems.at[0])

    for load in loads[:4]:
        load.wait()
    tile = [mask_ref[r].astype(f32) for r in range(tile_rows)]

    def keep(value):
        return jnp.concatenate(
            [value[r * tile_cols : (r + 1) * tile_cols] * tile[r] for r in range(tile_rows)]
        )

    kept_write[...] = keep(write_ref[...].astype(f32)).astype(bf16)
    aux_out[:, :state] = dot(order, kept_write[...]).astype(bf16)
    aux_out[:, state : 2 * state] = dot(order, read_ref[...]).astype(bf16)
    lanes = per * heads
    groups = patches // per
    lane_head = lax.broadcasted_iota(jnp.int32, (heads, lanes), 1) & (heads - 1)
    copies = ones(lax.broadcasted_iota(jnp.int32, (heads, lanes), 0) == lane_head)
    lane_col = shift(lax.broadcasted_iota(jnp.int32, (tile_cols, lanes), 1), heads)
    kept = (lax.broadcasted_iota(jnp.int32, (tile_cols, lanes), 0) & (per - 1)) == lane_col
    group = lax.broadcasted_iota(jnp.int32, (groups, tile_cols), 0)
    group_col = lax.broadcasted_iota(jnp.int32, (groups, tile_cols), 1)
    packed = jnp.zeros((groups, lanes), f32)
    for r in range(tile_rows):
        wide = lax.dot_general(
            col_ref[r], copies, (((0,), (0,)), ((), ())), preferred_element_type=f32
        )
        wide = jnp.where(kept, wide, 0.0).astype(bf16)
        packed += dot(ones(group == shift(group_col, per) * tile_rows + r), wide)
    decay_out[...] = packed.astype(bf16).reshape(decay_out.shape)

    def send_aux(other):
        def rows(index):
            return pl.ds(pl.multiple_of(index * block, block), block)

        def copy(source, target, send_sem, recv_sem):
            pltpu.make_async_remote_copy(
                src_ref=source,
                dst_ref=target,
                send_sem=send_sem,
                recv_sem=recv_sem,
                device_id={"row": other},
                device_id_type=MESH,
            ).start()

        above = other < half

        @pl.when(jnp.logical_or(above, jnp.logical_not(upper)))
        def _():
            copy(aux_out.at[rows(other)], aux_in.at[own], aux_sems.at[0], aux_sems.at[1])

        @pl.when(jnp.logical_and(above, upper))
        def _():
            copy(aux_out.at[rows(other + half)], help_in.at[own], help_sems.at[0], help_sems.at[1])

        @pl.when(jnp.logical_and(above, jnp.logical_not(upper)))
        def _():
            copy(
                aux_out.at[rows(other + half), pl.ds(state, state)],
                help_in.at[own, pl.ds(state, state)],
                help_sems.at[0],
                help_sems.at[2],
            )

        copy(decay_out.at[other], decay_in.at[me], decay_sems.at[0], decay_sems.at[1])

    each(soon, lambda step: send_aux(soon_peer(step)))
    aux_in[own, :] = aux_out[own, :]
    decay_in[me] = decay_out[me]

    @pl.when(upper)
    def _():
        twin = pl.ds(pl.multiple_of((me + half) * block, block), block)
        help_in[own, :] = aux_out[twin, :]


    def products(reads, writes):
        return lax.dot_general(
            reads, writes, (((1,), (1,)), ((), ())), preferred_element_type=f32
        )

    def causal(scores, allowed):
        return jnp.where(allowed, scores, 0.0).astype(bf16)

    same_col = (down & (per - 1)) == (across & (per - 1))
    earlier = (shift(down, 2 * block) > shift(across, 2 * block)) & same_col

    fold = ones(lax.broadcasted_iota(jnp.int32, (groups, 1), 0) == shift(across, per))
    slot = lax.broadcasted_iota(jnp.int32, (middle, middle), 0)
    slot = (slot & (per - 1)) * (middle // per) + shift(slot, per)
    swap = ones(slot == lax.broadcasted_iota(jnp.int32, (middle, middle), 1))

    def help_below():
        part = help_in.at[pl.ds(0, block * (half - 1))]
        pltpu.make_async_copy(part, part, help_sems.at[1]).wait()
        part = help_in.at[pl.ds(0, block * half), pl.ds(0, state)]
        pltpu.make_async_copy(part, part, help_sems.at[2]).wait()
        known = causal(
            products(help_in[:, state:], help_in[:middle, :state]), earlier[:, :middle]
        )
        scores_out[...] = dot(fold, dot(known, swap).astype(bf16)).astype(bf16)
        pltpu.make_async_remote_copy(
            src_ref=scores_out,
            dst_ref=scores_in,
            send_sem=score_sems.at[0],
            recv_sem=score_sems.at[1],
            device_id={"row": me + half},
            device_id_type=MESH,
        ).start()

    for c in range(chunks):
        if c:
            x_loads[c].wait()
            sent[c] = dot(order, x_ref[:, c * width : (c + 1) * width]).astype(bf16)
        got[c, block * (devices - 2) :, :] = jnp.zeros((2 * block, width), bf16)
        got[c, own, :] = sent[c, own, :]

        if c:

            @pl.when(jnp.logical_not(tail))
            def _():
                each(devices - 1, lambda step: send(sent.at[c], got.at[c], there_sems.at[c], peer(step)))

        else:

            @pl.when(jnp.logical_not(last))
            def _():
                pl.semaphore_wait(late_sem, quarter)
                each(quarter, lambda step: send_aux(late_peer(step)))
                scatter_late(sent.at[c], got.at[c], there_sems.at[c])

        if c == 2:

            @pl.when(upper)
            def _():
                help_below()

    @pl.when(jnp.logical_not(odd))
    def _():
        for i, (source, target) in enumerate(pairs):
            pltpu.make_async_remote_copy(
                src_ref=source,
                dst_ref=target,
                send_sem=pair_sems.at[i, 0],
                recv_sem=pair_sems.at[i, 1],
                device_id={"row": me + 1},
                device_id_type=MESH,
            ).start()

    def spread(c, count=heads):
        head = lax.broadcasted_iota(jnp.int32, (count, width), 0) & (heads - 1)
        lane = lax.broadcasted_iota(jnp.int32, (count, width), 1)
        return (head == shift(lane + c * width, head_width)).astype(f32)

    def running(below, decays, c):
        own_head = spread(c, decays.shape[1]).astype(bf16)
        return dot(below, dot(decays, own_head).astype(bf16))

    restore = ones(down == home(across))
    in_row = (down >= across) & (shift(down, tile_cols) == shift(across, tile_cols))
    row_below = ones(in_row)
    for load in loads[4:]:
        load.wait()
    row_decays = turned(down, row_ref)
    own_scores = products(read_ref[...], write_ref[...])
    row_scores = causal(own_scores, in_row)
    in_home = (down >= across) & ((down & (tile_cols - 1)) == (across & (tile_cols - 1)))
    home_below = ones(in_home)
    home_decays = turned(down, col_ref)
    origin = shift(across, tile_cols)
    present = sum(jnp.where(origin == r, tile[r], 0.0) for r in range(tile_rows))
    home_scores = causal(own_scores * present, in_home)
    skip = jnp.broadcast_to(skip_ref[...], (8, heads))
    for c in range(chunks):
        cut = slice(c * width, (c + 1) * width)
        run = running(row_below, row_decays, c)
        faded = (x_ref[:, cut].astype(f32) * jnp.exp(-run)).astype(bf16)
        gain = jnp.dot(
            skip, spread(c), precision=lax.Precision.HIGHEST, preferred_element_type=f32
        )[:1]
        total[:, cut] = jnp.exp(run) * dot(row_scores, faded) + gain * x_ref[:, cut].astype(f32)

    col_below = ones((down >= across) & same_col)

    @pl.when(upper)
    def _():
        wait(aux_in, aux_sems.at[1])
        col_scores[...] = causal(products(aux_in[:, state:], aux_in[:, :state]), earlier)

    @pl.when(jnp.logical_not(upper))
    def _():
        wait(aux_in, aux_sems.at[1], half - 1)
        col_scores[:middle, middle:] = jnp.zeros((middle, middle), bf16)
        col_scores[middle:, middle:] = causal(
            products(aux_in[middle:, state:], aux_in[middle:, :state]), earlier[middle:, middle:]
        )
        pltpu.make_async_copy(scores_in, scores_in, score_sems.at[1]).wait()
        wide = lax.dot_general(
            fold, scores_in[...], (((0,), (0,)), ((), ())), preferred_element_type=f32
        )
        place = lax.broadcasted_iota(jnp.int32, (1, middle), 1)
        wide = jnp.where(shift(place, middle // per) == (down & (per - 1)), wide, 0.0)
        col_scores[:, :middle] = lax.dot_general(
            wide.astype(bf16), swap, (((1,), (1,)), ((), ())), preferred_element_type=f32
        ).astype(bf16)

    pieces = decay_in.at[pl.ds(0, devices - 1)]
    pltpu.make_async_copy(pieces, pieces, decay_sems.at[1]).wait()
    wide = lax.dot_general(
        fold,
        decay_in[...].reshape(groups, lanes),
        (((0,), (0,)), ((), ())),
        preferred_element_type=f32,
    )
    place = lax.broadcasted_iota(jnp.int32, (1, lanes), 1)
    col_decays = jnp.where(shift(place, heads) == (down & (per - 1)), wide, 0.0).astype(bf16)
    for c in range(chunks):
        run = running(col_below, col_decays, c)
        grow[c] = jnp.exp(run)
        fade[c] = jnp.exp(-run)

    for c in range(chunks):
        wait_either(got.at[c], there_sems.at[c, 1], tail)
        faded = (got[c].astype(f32) * fade[c]).astype(bf16)
        col_sent[c] = (grow[c] * dot(col_scores[...], faded)).astype(bf16)
        give_back(col_sent.at[c], col_got.at[c], back_sems.at[c])
        col_got[c, own, :] = col_sent[c, own, :]

    for c in range(chunks):
        cut = slice(c * width, (c + 1) * width)
        run = running(home_below, home_decays, c)
        grow[c] = jnp.exp(run)
        faded = (x_ref[:, cut].astype(f32) * jnp.exp(-run)).astype(bf16)
        total[:, cut] += grow[c] * dot(home_scores, faded)

    @pl.when(odd)
    def _():
        for i, (source, target) in enumerate(pairs):
            pltpu.make_async_copy(target, target, pair_sems.at[i, 1]).wait()
        alike = (down & (tile_cols - 1)) == (across & (tile_cols - 1))
        pair_after = ones((shift(down, tile_cols) < shift(across, tile_cols)) & alike)
        pair_decays = turned(down, pair_col)
        pair_scores = causal(products(read_ref[...], pair_write[...]), alike)
        for c in range(chunks):
            cut = slice(c * width, (c + 1) * width)
            run = running(pair_after, pair_decays, c)
            faded = (pair_x[:, cut].astype(f32) * jnp.exp(run)).astype(bf16)
            total[:, cut] += grow[c] * dot(pair_scores, faded)

    @pl.when(jnp.logical_not(odd))
    def _():
        for i, (source, target) in enumerate(pairs):
            pltpu.make_async_copy(source, source, pair_sems.at[i, 0]).wait()

    for c in range(chunks):
        cut = slice(c * width, (c + 1) * width)

        @pl.when(head)
        def _():
            col_got[c] = jnp.zeros((patches, width), bf16)

        @pl.when(jnp.logical_not(head))
        def _():
            wait(col_got.at[c], back_sems.at[c, 1])

        out_ref[:, cut] = keep(total[:, cut] + dot(restore, col_got[c])).astype(bf16)

    pltpu.make_async_copy(pieces, pieces, decay_sems.at[0]).wait()

    @pl.when(upper)
    def _():
        wait(aux_out, aux_sems.at[0], half - 1)
        wait(aux_out, help_sems.at[0], half - 1)
        pltpu.make_async_copy(scores_out, scores_out, score_sems.at[0]).wait()

    @pl.when(jnp.logical_not(upper))
    def _():
        wait(aux_out, aux_sems.at[0])
        part = help_in.at[pl.ds(0, block * half), pl.ds(0, state)]
        pltpu.make_async_copy(part, part, help_sems.at[0]).wait()

    for c in range(chunks):
        wait_either(col_sent.at[c], back_sems.at[c, 0], head)

        @pl.when(jnp.logical_not(tail))
        def _():
            wait(sent.at[c], there_sems.at[c, 0])


def fused(features, write_vecs, read_vecs, row_decay, col_decay, tile_mask, skip_gain):
    tile_rows, tile_cols, span_width = features.shape
    heads, state = row_decay.shape[-1], write_vecs.shape[-1]
    patches = tile_rows * tile_cols
    devices = lax.axis_size("row")
    width = span_width // CHUNKS

    def flat(array):
        return array.reshape(patches, array.shape[-1])

    vmem = pl.BlockSpec(memory_space=pltpu.VMEM)
    piece = (CHUNKS, patches, width)
    aux = pltpu.VMEM((patches, 2 * state), jnp.bfloat16)
    per = tile_cols // devices
    scores = pltpu.VMEM((patches // per, patches // 2), jnp.bfloat16)
    decays = pltpu.VMEM((devices, tile_rows, per * heads), jnp.bfloat16)
    result = pl.pallas_call(
        functools.partial(fused_kernel, (devices, tile_rows, tile_cols, heads)),
        out_shape=pltpu.VMEM((patches, span_width), jnp.bfloat16),
        in_specs=[pl.BlockSpec(memory_space=pl.ANY)] * 7,
        out_specs=vmem,
        scratch_shapes=[
            pltpu.SMEM((tile_rows,), jnp.int32),
            pltpu.VMEM((1, heads), jnp.float32),
            pltpu.VMEM((patches, span_width), jnp.bfloat16),
            pltpu.VMEM((patches, state), jnp.bfloat16),
            pltpu.VMEM((patches, state), jnp.bfloat16),
            pltpu.VMEM((tile_rows, heads, tile_cols), jnp.bfloat16),
            pltpu.VMEM((tile_rows, heads, tile_cols), jnp.bfloat16),
            aux,
            aux,
            aux,
            scores,
            scores,
            pltpu.VMEM((patches, patches), jnp.bfloat16),
            decays,
            decays,
            pltpu.VMEM((patches, span_width), jnp.bfloat16),
            pltpu.VMEM((patches, state), jnp.bfloat16),
            pltpu.VMEM((tile_rows, heads, tile_cols), jnp.bfloat16),
            pltpu.VMEM((patches, state), jnp.bfloat16),
            pltpu.VMEM(piece, jnp.bfloat16),
            pltpu.VMEM(piece, jnp.bfloat16),
            pltpu.VMEM(piece, jnp.bfloat16),
            pltpu.VMEM(piece, jnp.bfloat16),
            pltpu.VMEM((patches, span_width), jnp.float32),
            pltpu.VMEM(piece, jnp.float32),
            pltpu.VMEM(piece, jnp.float32),
            pltpu.SemaphoreType.DMA((6,)),
            pltpu.SemaphoreType.DMA((CHUNKS,)),
            pltpu.SemaphoreType.DMA((2,)),
            pltpu.SemaphoreType.DMA((3,)),
            pltpu.SemaphoreType.DMA((2,)),
            pltpu.SemaphoreType.DMA((2,)),
            pltpu.SemaphoreType.DMA((3, 2)),
            pltpu.SemaphoreType.DMA((CHUNKS, 2)),
            pltpu.SemaphoreType.DMA((CHUNKS, 2)),
            pltpu.SemaphoreType.REGULAR,
        ],
        compiler_params=pltpu.CompilerParams(
            collective_id=0, has_side_effects=True, vmem_limit_bytes=60 * 2**20
        ),
    )(
        tile_mask.reshape(-1),
        skip_gain.reshape(1, heads),
        flat(features),
        flat(write_vecs),
        flat(read_vecs),
        jnp.swapaxes(row_decay, 1, 2),
        jnp.swapaxes(col_decay, 1, 2),
    )
    return result.reshape(features.shape)


def fits_fused(features, row_decay, tile_mask):
    tile_rows, tile_cols, span_width = features.shape
    devices = lax.axis_size("row")
    return (
        lax.axis_size("col") == 1
        and tile_mask.shape[1] == 1
        and tile_rows * devices == tile_cols
        and devices % 4 == 0
        and tile_cols <= 64
        and (tile_rows * (tile_cols // devices)) % 16 == 0
        and span_width % (CHUNKS * 128) == 0
        and (tile_cols // devices) * row_decay.shape[-1] == 128
        and tile_rows * tile_cols % 256 == 0
        and all(
            size.bit_count() == 1
            for size in (tile_rows, tile_cols, devices, span_width // row_decay.shape[-1])
        )
    )


def per_device(features, write_vecs, read_vecs, row_decay, col_decay, tile_mask, skip_gain):
    tile_rows, tile_cols, span_width = features.shape
    if fits_fused(features, row_decay, tile_mask):
        return fused(features, write_vecs, read_vecs, row_decay, col_decay, tile_mask, skip_gain)
    head_count = row_decay.shape[-1]
    block_len = tile_cols // tile_mask.shape[1]
    patch_mask = jnp.repeat(tile_mask, block_len, axis=1)
    masked = jnp.where(patch_mask[..., None] > 0, features, jnp.zeros((), features.dtype))
    moved = (
        lax.all_to_all(masked, "row", split_axis=1, concat_axis=0, tiled=True),
        lax.all_to_all(write_vecs, "row", split_axis=1, concat_axis=0, tiled=True),
        lax.all_to_all(read_vecs, "row", split_axis=1, concat_axis=0, tiled=True),
        lax.all_to_all(col_decay, "row", split_axis=1, concat_axis=0, tiled=True),
    )
    result = column_chains(moved[0], moved[1], moved[2], moved[3], block_len)
    col_out = lax.all_to_all(result, "row", split_axis=0, concat_axis=1, tiled=True)
    local_terms, read_blocks = row_terms(masked, write_vecs, read_vecs, row_decay, block_len)
    if lax.axis_size("col") == 1 and tile_mask.shape[1] == 1:
        y_row = local_terms[0].reshape(features.shape)
    else:
        zero_states = jnp.zeros((tile_rows,) + local_terms[1].shape[2:], jnp.float32)
        closing_states, unused_states = jax.vmap(enter_states)(
            local_terms[2], local_terms[1], zero_states
        )
        device_decay = jnp.prod(local_terms[2], axis=1)
        identity = (jnp.ones_like(device_decay), jnp.zeros_like(closing_states))
        decay_before, state_before = entering_2((device_decay, closing_states), "col", link, identity)
        y_row = row_finish(local_terms, read_blocks, state_before)
    skip_vector = jnp.repeat(skip_gain, span_width // head_count)
    total = y_row + col_out.astype(jnp.float32) + skip_vector * features.astype(jnp.float32)
    return (patch_mask[..., None].astype(jnp.float32) * total).astype(jnp.bfloat16)


def solution(mesh):
    return jax.shard_map(
        per_device,
        mesh=mesh,
        in_specs=(
            P(("slides", "row"), "col", None),
            P(("slides", "row"), "col", None),
            P(("slides", "row"), "col", None),
            P(("slides", "row"), "col", None),
            P(("slides", "row"), "col", None),
            P(("slides", "row"), "col"),
            P(),
        ),
        out_specs=P(("slides", "row"), "col", None),
        check_vma=False,
    )
```

```python
import functools

import jax
import jax.numpy as jnp
from jax import lax
from jax.experimental import pallas as pl
from jax.experimental.pallas import tpu as pltpu
from jax.sharding import PartitionSpec as P


def entering_2(array, axis, combine, identity):
    devices, here = (lax.axis_size(axis), lax.axis_index(axis))
    everything = jax.tree.map(
        lambda part, kind: lax.all_gather(part.astype(kind), axis),
        array,
        (jnp.bfloat16, jnp.bfloat16),
    )
    start = jax.tree.map(
        lambda part, zero: jnp.broadcast_to(jnp.asarray(zero, part.dtype), part.shape),
        array,
        identity,
    )

    def step(k, before):
        reached = k < here
        new = combine(
            before, jax.tree.map(lambda part, own: part[k].astype(own.dtype), everything, array)
        )
        return jax.tree.map(lambda a, b: jnp.where(reached, a, b), new, before)

    return lax.fori_loop(0, devices, step, start)


def block_local(masked, write_vecs, read_vecs, decays):
    blocks, length, span_width = masked.shape
    head_count = decays.shape[-1]
    head_width = span_width // head_count
    slots = jnp.arange(length)
    upto = (slots[:, None] >= slots[None, :]).astype(decays.dtype)
    running = jnp.einsum("ts,ksh->kht", upto, decays, preferred_element_type=jnp.float32)
    scores = jnp.einsum("ktn,ksn->kts", read_vecs, write_vecs, preferred_element_type=jnp.float32)
    target_slots = jnp.arange(length)
    causal = target_slots[:, None] >= target_slots[None, :]
    spread = jnp.where(causal, running[:, :, :, None] - running[:, :, None, :], jnp.float32(0.0))
    weights = jnp.where(causal, scores[:, None] * jnp.exp(spread), jnp.float32(0.0)).astype(
        jnp.bfloat16
    )
    values = masked.reshape(blocks, length, head_count, head_width)
    inside = jnp.einsum("khts,kshp->kthp", weights, values, preferred_element_type=jnp.float32)
    closing = running[:, :, -1]
    scaled = (
        write_vecs.astype(jnp.float32)[:, None] * jnp.exp(closing[:, :, None] - running)[..., None]
    ).astype(jnp.bfloat16)
    block_state = jnp.einsum("khsn,kshp->khnp", scaled, values, preferred_element_type=jnp.float32)
    return (inside, block_state, jnp.exp(closing), running)


def enter_states(damping, block_state, initial):

    def advance(carry_state, element):
        factor, fresh_term = element
        return (factor[:, None, None] * carry_state + fresh_term, carry_state)

    return lax.scan(advance, initial, (damping, block_state))


def combine_out(inside, entering, read_blocks, running):
    carried = jnp.einsum(
        "ktn,khnp->kthp", read_blocks.astype(jnp.float32), entering, precision=lax.Precision.HIGHEST
    )
    total = inside + carried * jnp.swapaxes(jnp.exp(running), 1, 2)[..., None]
    return total.reshape(total.shape[0] * total.shape[1], total.shape[2] * total.shape[3])


def to_blocks(array, block_len):
    return array.reshape(
        array.shape[:-2] + (array.shape[-2] // block_len, block_len, array.shape[-1])
    )


def column_chains(masked, write_vecs, read_vecs, decays, block_len):

    def one_column(masked_c, write_c, read_c, decay_c):
        read_blocks = to_blocks(read_c, block_len)
        inside, block_state, damping, running = block_local(
            to_blocks(masked_c, block_len),
            to_blocks(write_c, block_len),
            read_blocks,
            to_blocks(decay_c, block_len),
        )
        if read_blocks.shape[0] == 1:
            return inside.reshape(masked_c.shape)
        zero_state = jnp.zeros(block_state.shape[1:], jnp.float32)
        closing_state, entering = enter_states(damping, block_state, zero_state)
        return combine_out(inside, entering, read_blocks, running)

    results = jax.vmap(one_column, in_axes=1, out_axes=1)(masked, write_vecs, read_vecs, decays)
    return results.astype(jnp.bfloat16)


def row_terms(masked, write_vecs, read_vecs, decays, block_len):
    read_blocks = to_blocks(read_vecs, block_len)
    local_terms = jax.vmap(block_local)(
        to_blocks(masked, block_len),
        to_blocks(write_vecs, block_len),
        read_blocks,
        to_blocks(decays, block_len),
    )
    return (local_terms, read_blocks)


def row_finish(local_terms, read_blocks, incoming):
    inside, block_state, damping, running = local_terms
    closing_state, entering = jax.vmap(enter_states)(damping, block_state, incoming)
    return jax.vmap(combine_out)(inside, entering, read_blocks, running)


def link(earlier, later):
    return (earlier[0] * later[0], later[0][..., None, None] * earlier[1] + later[1])


MESH = pl.DeviceIdType.MESH
CHUNKS = 4


def fused_kernel(
    shape,
    mask_hbm,
    skip_hbm,
    x_hbm,
    write_hbm,
    read_hbm,
    row_hbm,
    col_hbm,
    out_ref,
    mask_ref,
    skip_ref,
    x_ref,
    write_ref,
    read_ref,
    row_ref,
    col_ref,
    aux_out,
    aux_in,
    help_in,
    scores_out,
    scores_in,
    col_scores,
    decay_out,
    decay_in,
    pair_x,
    pair_write,
    pair_col,
    kept_write,
    sent,
    got,
    col_sent,
    col_got,
    total,
    grow,
    fade,
    load_sems,
    x_sems,
    aux_sems,
    help_sems,
    score_sems,
    decay_sems,
    pair_sems,
    there_sems,
    back_sems,
    late_sem,
):
    devices, tile_rows, tile_cols, heads = shape
    per = tile_cols // devices
    block = tile_rows * per
    patches = tile_rows * tile_cols
    chunks, _, width = sent.shape
    head_width = chunks * width // heads
    state = write_ref.shape[-1]
    f32, bf16 = jnp.float32, jnp.bfloat16
    me = lax.axis_index("row")
    own = pl.ds(pl.multiple_of(me * block, block), block)

    def dot(a, b):
        return jnp.dot(a, b, preferred_element_type=f32)

    quarter, half = devices // 4, devices // 2
    middle = patches // 2
    upper = me < half
    first = devices - quarter
    last = me >= first
    soon = jnp.where(last, devices - 1, first - 1)

    def peer(step):
        return lax.rem(me + 1 + step, devices)

    def soon_peer(step):
        across_first = jnp.where(
            step < quarter, half + lax.rem(me + step, quarter), lax.rem(me + 1 + step - quarter, half)
        )
        return jnp.where(upper, across_first, lax.rem(me + 1 + step, soon + 1))

    def far_peer(step):
        across_first = jnp.where(
            step < half, half + lax.rem(me + step, half), lax.rem(me + 1 + step - half, half)
        )
        return jnp.where(upper, across_first, peer(step))

    def late_peer(step):
        return first + lax.rem(me + step, quarter)

    barrier = pltpu.get_barrier_semaphore()

    def each(steps, act):
        def body(step, carry):
            act(step)
            return carry

        lax.fori_loop(0, steps, body, 0)

    def greet(other, semaphore=barrier):
        pl.semaphore_signal(semaphore, inc=1, device_id={"row": other}, device_id_type=MESH)

    @pl.when(last)
    def _():
        each(quarter - 1, lambda step: greet(first + lax.rem(me + 1 + step, quarter)))

    @pl.when(jnp.logical_not(last))
    def _():
        each(devices - 1, lambda step: greet(lax.rem(me - 1 - step + devices, devices)))

    loads = [
        pltpu.make_async_copy(source, target, load_sems.at[i])
        for i, (source, target) in enumerate(
            (
                (mask_hbm, mask_ref),
                (write_hbm, write_ref),
                (read_hbm, read_ref),
                (col_hbm, col_ref),
                (row_hbm, row_ref),
                (skip_hbm, skip_ref),
            )
        )
    ]
    x_loads = [
        pltpu.make_async_copy(
            x_hbm.at[:, pl.ds(c * width, width)], x_ref.at[:, pl.ds(c * width, width)], x_sems.at[c]
        )
        for c in range(chunks)
    ]
    for load in loads[:4] + x_loads + loads[4:]:
        load.start()

    def send(source, target, sems, other):
        pltpu.make_async_remote_copy(
            src_ref=source.at[pl.ds(pl.multiple_of(other * block, block), block)],
            dst_ref=target.at[own],
            send_sem=sems.at[0],
            recv_sem=sems.at[1],
            device_id={"row": other},
            device_id_type=MESH,
        ).start()

    tail = me >= devices - 2
    head = me < 2
    odd = (me & 1) == 1

    def scatter_soon(source, target, sems):
        each(soon, lambda step: send(source, target, sems, soon_peer(step)))

    def scatter_late(source, target, sems):
        each(quarter, lambda step: send(source, target, sems, late_peer(step)))

    def give_back(source, target, sems):
        def act(step):
            other = peer(step)

            @pl.when(other >= 2)
            def _():
                send(source, target, sems, other)

        each(devices - 1, act)

    def wait(buffer, sem, count=devices - 1):
        part = buffer.at[pl.ds(0, block * count)]
        pltpu.make_async_copy(part, part, sem).wait()

    def wait_either(buffer, sem, one_more):
        @pl.when(one_more)
        def _():
            wait(buffer, sem, devices - 2)

        @pl.when(jnp.logical_not(one_more))
        def _():
            wait(buffer, sem, devices - 3)

    pairs = [(x_ref, pair_x), (kept_write, pair_write), (col_ref, pair_col)]

    def shift(i, size):
        return lax.shift_right_logical(i, size.bit_length() - 1)

    down = lax.broadcasted_iota(jnp.int32, (patches, 1), 0)
    across = lax.broadcasted_iota(jnp.int32, (1, patches), 1)

    def home(i):
        row = shift(i, per) & (tile_rows - 1)
        return row * tile_cols + shift(i, block) * per + (i & (per - 1))

    def ones(where):
        return where.astype(f32).astype(bf16)

    from_home = home(down)
    order = ones(from_home == across)

    def turned(places, ref):
        lanes = lax.broadcasted_iota(jnp.int32, (1, tile_cols), 1)
        return sum(
            lax.dot_general(
                ones(places == lanes + r * tile_cols),
                ref[r],
                (((1,), (1,)), ((), ())),
                preferred_element_type=f32,
            )
            for r in range(tile_rows)
        ).astype(bf16)

    x_loads[0].wait()
    sent[0] = dot(order, x_ref[:, :width]).astype(bf16)

    @pl.when(last)
    def _():
        pl.semaphore_wait(barrier, devices - 1)
        each(first, lambda step: greet(first - 1 - lax.rem(me + step, first), late_sem))

    @pl.when(jnp.logical_not(last))
    def _():
        pl.semaphore_wait(barrier, first - 1)

    @pl.when(jnp.logical_not(tail))
    def _():
        scatter_soon(sent.at[0], got.at[0], there_sems.at[0])

    for load in loads[:4]:
        load.wait()
    tile = [mask_ref[r].astype(f32) for r in range(tile_rows)]

    def keep(value):
        return jnp.concatenate(
            [value[r * tile_cols : (r + 1) * tile_cols] * tile[r] for r in range(tile_rows)]
        )

    kept_write[...] = keep(write_ref[...].astype(f32)).astype(bf16)
    aux_out[:, :state] = dot(order, kept_write[...]).astype(bf16)
    aux_out[:, state : 2 * state] = dot(order, read_ref[...]).astype(bf16)
    lanes = per * heads
    groups = patches // per
    lane_head = lax.broadcasted_iota(jnp.int32, (heads, lanes), 1) & (heads - 1)
    copies = ones(lax.broadcasted_iota(jnp.int32, (heads, lanes), 0) == lane_head)
    lane_col = shift(lax.broadcasted_iota(jnp.int32, (tile_cols, lanes), 1), heads)
    kept = (lax.broadcasted_iota(jnp.int32, (tile_cols, lanes), 0) & (per - 1)) == lane_col
    group = lax.broadcasted_iota(jnp.int32, (groups, tile_cols), 0)
    group_col = lax.broadcasted_iota(jnp.int32, (groups, tile_cols), 1)
    packed = jnp.zeros((groups, lanes), f32)
    for r in range(tile_rows):
        wide = lax.dot_general(
            col_ref[r], copies, (((0,), (0,)), ((), ())), preferred_element_type=f32
        )
        wide = jnp.where(kept, wide, 0.0).astype(bf16)
        packed += dot(ones(group == shift(group_col, per) * tile_rows + r), wide)
    decay_out[...] = packed.astype(bf16).reshape(decay_out.shape)

    def send_aux(other):
        def rows(index):
            return pl.ds(pl.multiple_of(index * block, block), block)

        def copy(source, target, send_sem, recv_sem):
            pltpu.make_async_remote_copy(
                src_ref=source,
                dst_ref=target,
                send_sem=send_sem,
                recv_sem=recv_sem,
                device_id={"row": other},
                device_id_type=MESH,
            ).start()

        above = other < half

        @pl.when(jnp.logical_or(above, jnp.logical_not(upper)))
        def _():
            copy(aux_out.at[rows(other)], aux_in.at[own], aux_sems.at[0], aux_sems.at[1])

        @pl.when(jnp.logical_and(above, upper))
        def _():
            copy(aux_out.at[rows(other + half)], help_in.at[own], help_sems.at[0], help_sems.at[1])

        @pl.when(jnp.logical_and(above, jnp.logical_not(upper)))
        def _():
            copy(
                aux_out.at[rows(other + half), pl.ds(state, state)],
                help_in.at[own, pl.ds(state, state)],
                help_sems.at[0],
                help_sems.at[2],
            )

        copy(decay_out.at[other], decay_in.at[me], decay_sems.at[0], decay_sems.at[1])

    each(soon, lambda step: send_aux(soon_peer(step)))
    aux_in[own, :] = aux_out[own, :]
    decay_in[me] = decay_out[me]

    @pl.when(upper)
    def _():
        twin = pl.ds(pl.multiple_of((me + half) * block, block), block)
        help_in[own, :] = aux_out[twin, :]


    def products(reads, writes):
        return lax.dot_general(
            reads, writes, (((1,), (1,)), ((), ())), preferred_element_type=f32
        )

    def causal(scores, allowed):
        return jnp.where(allowed, scores, 0.0).astype(bf16)

    same_col = (down & (per - 1)) == (across & (per - 1))
    earlier = (shift(down, 2 * block) > shift(across, 2 * block)) & same_col

    fold = ones(lax.broadcasted_iota(jnp.int32, (groups, 1), 0) == shift(across, per))
    slot = lax.broadcasted_iota(jnp.int32, (middle, middle), 0)
    slot = (slot & (per - 1)) * (middle // per) + shift(slot, per)
    swap = ones(slot == lax.broadcasted_iota(jnp.int32, (middle, middle), 1))

    def help_below():
        part = help_in.at[pl.ds(0, block * (half - 1))]
        pltpu.make_async_copy(part, part, help_sems.at[1]).wait()
        part = help_in.at[pl.ds(0, block * half), pl.ds(0, state)]
        pltpu.make_async_copy(part, part, help_sems.at[2]).wait()
        known = causal(
            products(help_in[:, state:], help_in[:middle, :state]), earlier[:, :middle]
        )
        scores_out[...] = dot(fold, dot(known, swap).astype(bf16)).astype(bf16)
        pltpu.make_async_remote_copy(
            src_ref=scores_out,
            dst_ref=scores_in,
            send_sem=score_sems.at[0],
            recv_sem=score_sems.at[1],
            device_id={"row": me + half},
            device_id_type=MESH,
        ).start()

    for c in range(chunks):
        if c:
            x_loads[c].wait()
            sent[c] = dot(order, x_ref[:, c * width : (c + 1) * width]).astype(bf16)
        got[c, block * (devices - 2) :, :] = jnp.zeros((2 * block, width), bf16)
        got[c, own, :] = sent[c, own, :]

        if c:

            @pl.when(jnp.logical_not(tail))
            def _():
                each(devices - 1, lambda step: send(sent.at[c], got.at[c], there_sems.at[c], far_peer(step)))

        else:

            @pl.when(jnp.logical_not(last))
            def _():
                pl.semaphore_wait(late_sem, quarter)
                each(quarter, lambda step: send_aux(late_peer(step)))
                scatter_late(sent.at[c], got.at[c], there_sems.at[c])

        if c == 2:

            @pl.when(upper)
            def _():
                help_below()

    @pl.when(jnp.logical_not(odd))
    def _():
        for i, (source, target) in enumerate(pairs):
            pltpu.make_async_remote_copy(
                src_ref=source,
                dst_ref=target,
                send_sem=pair_sems.at[i, 0],
                recv_sem=pair_sems.at[i, 1],
                device_id={"row": me + 1},
                device_id_type=MESH,
            ).start()

    def spread(c, count=heads):
        head = lax.broadcasted_iota(jnp.int32, (count, width), 0) & (heads - 1)
        lane = lax.broadcasted_iota(jnp.int32, (count, width), 1)
        return (head == shift(lane + c * width, head_width)).astype(f32)

    def running(below, decays, c):
        own_head = spread(c, decays.shape[1]).astype(bf16)
        return dot(below, dot(decays, own_head).astype(bf16))

    restore = keep((down == home(across)).astype(f32)).astype(bf16)
    in_row = (down >= across) & (shift(down, tile_cols) == shift(across, tile_cols))
    row_below = ones(in_row)
    for load in loads[4:]:
        load.wait()
    row_decays = turned(down, row_ref)
    own_scores = products(read_ref[...], write_ref[...])
    row_scores = causal(own_scores, in_row)
    in_home = (down >= across) & ((down & (tile_cols - 1)) == (across & (tile_cols - 1)))
    home_below = ones(in_home)
    home_decays = turned(down, col_ref)
    origin = shift(across, tile_cols)
    present = sum(jnp.where(origin == r, tile[r], 0.0) for r in range(tile_rows))
    home_scores = causal(own_scores * present, in_home)
    skip = jnp.broadcast_to(skip_ref[...], (8, heads))
    for c in range(chunks):
        cut = slice(c * width, (c + 1) * width)
        run = running(row_below, row_decays, c)
        faded = (x_ref[:, cut].astype(f32) * jnp.exp(-run)).astype(bf16)
        gain = jnp.dot(
            skip, spread(c), precision=lax.Precision.HIGHEST, preferred_element_type=f32
        )[:1]
        total[:, cut] = jnp.exp(run) * dot(row_scores, faded) + gain * x_ref[:, cut].astype(f32)

    col_below = ones((down >= across) & same_col)

    @pl.when(upper)
    def _():
        wait(aux_in, aux_sems.at[1])
        col_scores[...] = causal(products(aux_in[:, state:], aux_in[:, :state]), earlier)

    @pl.when(jnp.logical_not(upper))
    def _():
        wait(aux_in, aux_sems.at[1], half - 1)
        col_scores[:middle, middle:] = jnp.zeros((middle, middle), bf16)
        col_scores[middle:, middle:] = causal(
            products(aux_in[middle:, state:], aux_in[middle:, :state]), earlier[middle:, middle:]
        )
        pltpu.make_async_copy(scores_in, scores_in, score_sems.at[1]).wait()
        wide = lax.dot_general(
            fold, scores_in[...], (((0,), (0,)), ((), ())), preferred_element_type=f32
        )
        place = lax.broadcasted_iota(jnp.int32, (1, middle), 1)
        wide = jnp.where(shift(place, middle // per) == (down & (per - 1)), wide, 0.0)
        col_scores[:, :middle] = lax.dot_general(
            wide.astype(bf16), swap, (((1,), (1,)), ((), ())), preferred_element_type=f32
        ).astype(bf16)

    pieces = decay_in.at[pl.ds(0, devices - 1)]
    pltpu.make_async_copy(pieces, pieces, decay_sems.at[1]).wait()
    wide = lax.dot_general(
        fold,
        decay_in[...].reshape(groups, lanes),
        (((0,), (0,)), ((), ())),
        preferred_element_type=f32,
    )
    place = lax.broadcasted_iota(jnp.int32, (1, lanes), 1)
    col_decays = jnp.where(shift(place, heads) == (down & (per - 1)), wide, 0.0).astype(bf16)
    for c in range(chunks):
        run = running(col_below, col_decays, c)
        grow[c] = jnp.exp(run)
        fade[c] = jnp.exp(-run)

    for c in range(chunks):
        wait_either(got.at[c], there_sems.at[c, 1], tail)
        faded = (got[c].astype(f32) * fade[c]).astype(bf16)
        col_sent[c] = (grow[c] * dot(col_scores[...], faded)).astype(bf16)
        give_back(col_sent.at[c], col_got.at[c], back_sems.at[c])
        col_got[c, own, :] = col_sent[c, own, :]

    for c in range(chunks):
        cut = slice(c * width, (c + 1) * width)
        run = running(home_below, home_decays, c)
        grow[c] = jnp.exp(run)
        faded = (x_ref[:, cut].astype(f32) * jnp.exp(-run)).astype(bf16)
        total[:, cut] += grow[c] * dot(home_scores, faded)

    @pl.when(odd)
    def _():
        for i, (source, target) in enumerate(pairs):
            pltpu.make_async_copy(target, target, pair_sems.at[i, 1]).wait()
        alike = (down & (tile_cols - 1)) == (across & (tile_cols - 1))
        pair_after = ones((shift(down, tile_cols) < shift(across, tile_cols)) & alike)
        pair_decays = turned(down, pair_col)
        pair_scores = causal(products(read_ref[...], pair_write[...]), alike)
        for c in range(chunks):
            cut = slice(c * width, (c + 1) * width)
            run = running(pair_after, pair_decays, c)
            faded = (pair_x[:, cut].astype(f32) * jnp.exp(run)).astype(bf16)
            total[:, cut] += grow[c] * dot(pair_scores, faded)

    @pl.when(jnp.logical_not(odd))
    def _():
        for i, (source, target) in enumerate(pairs):
            pltpu.make_async_copy(source, source, pair_sems.at[i, 0]).wait()

    total[...] = keep(total[...])
    for c in range(chunks):
        cut = slice(c * width, (c + 1) * width)

        @pl.when(head)
        def _():
            col_got[c] = jnp.zeros((patches, width), bf16)

        @pl.when(jnp.logical_not(head))
        def _():
            wait(col_got.at[c], back_sems.at[c, 1])

        out_ref[:, cut] = (total[:, cut] + dot(restore, col_got[c])).astype(bf16)

    pltpu.make_async_copy(pieces, pieces, decay_sems.at[0]).wait()

    @pl.when(upper)
    def _():
        wait(aux_out, aux_sems.at[0], half - 1)
        wait(aux_out, help_sems.at[0], half - 1)
        pltpu.make_async_copy(scores_out, scores_out, score_sems.at[0]).wait()

    @pl.when(jnp.logical_not(upper))
    def _():
        wait(aux_out, aux_sems.at[0])
        part = help_in.at[pl.ds(0, block * half), pl.ds(0, state)]
        pltpu.make_async_copy(part, part, help_sems.at[0]).wait()

    for c in range(chunks):
        wait_either(col_sent.at[c], back_sems.at[c, 0], head)

        @pl.when(jnp.logical_not(tail))
        def _():
            wait(sent.at[c], there_sems.at[c, 0])


def fused(features, write_vecs, read_vecs, row_decay, col_decay, tile_mask, skip_gain):
    tile_rows, tile_cols, span_width = features.shape
    heads, state = row_decay.shape[-1], write_vecs.shape[-1]
    patches = tile_rows * tile_cols
    devices = lax.axis_size("row")
    width = span_width // CHUNKS

    def flat(array):
        return array.reshape(patches, array.shape[-1])

    vmem = pl.BlockSpec(memory_space=pltpu.VMEM)
    piece = (CHUNKS, patches, width)
    aux = pltpu.VMEM((patches, 2 * state), jnp.bfloat16)
    per = tile_cols // devices
    scores = pltpu.VMEM((patches // per, patches // 2), jnp.bfloat16)
    decays = pltpu.VMEM((devices, tile_rows, per * heads), jnp.bfloat16)
    result = pl.pallas_call(
        functools.partial(fused_kernel, (devices, tile_rows, tile_cols, heads)),
        out_shape=pltpu.VMEM((patches, span_width), jnp.bfloat16),
        in_specs=[pl.BlockSpec(memory_space=pl.ANY)] * 7,
        out_specs=vmem,
        scratch_shapes=[
            pltpu.SMEM((tile_rows,), jnp.int32),
            pltpu.VMEM((1, heads), jnp.float32),
            pltpu.VMEM((patches, span_width), jnp.bfloat16),
            pltpu.VMEM((patches, state), jnp.bfloat16),
            pltpu.VMEM((patches, state), jnp.bfloat16),
            pltpu.VMEM((tile_rows, heads, tile_cols), jnp.bfloat16),
            pltpu.VMEM((tile_rows, heads, tile_cols), jnp.bfloat16),
            aux,
            aux,
            aux,
            scores,
            scores,
            pltpu.VMEM((patches, patches), jnp.bfloat16),
            decays,
            decays,
            pltpu.VMEM((patches, span_width), jnp.bfloat16),
            pltpu.VMEM((patches, state), jnp.bfloat16),
            pltpu.VMEM((tile_rows, heads, tile_cols), jnp.bfloat16),
            pltpu.VMEM((patches, state), jnp.bfloat16),
            pltpu.VMEM(piece, jnp.bfloat16),
            pltpu.VMEM(piece, jnp.bfloat16),
            pltpu.VMEM(piece, jnp.bfloat16),
            pltpu.VMEM(piece, jnp.bfloat16),
            pltpu.VMEM((patches, span_width), jnp.float32),
            pltpu.VMEM(piece, jnp.float32),
            pltpu.VMEM(piece, jnp.float32),
            pltpu.SemaphoreType.DMA((6,)),
            pltpu.SemaphoreType.DMA((CHUNKS,)),
            pltpu.SemaphoreType.DMA((2,)),
            pltpu.SemaphoreType.DMA((3,)),
            pltpu.SemaphoreType.DMA((2,)),
            pltpu.SemaphoreType.DMA((2,)),
            pltpu.SemaphoreType.DMA((3, 2)),
            pltpu.SemaphoreType.DMA((CHUNKS, 2)),
            pltpu.SemaphoreType.DMA((CHUNKS, 2)),
            pltpu.SemaphoreType.REGULAR,
        ],
        compiler_params=pltpu.CompilerParams(
            collective_id=0, has_side_effects=True, vmem_limit_bytes=60 * 2**20
        ),
    )(
        tile_mask.reshape(-1),
        skip_gain.reshape(1, heads),
        flat(features),
        flat(write_vecs),
        flat(read_vecs),
        jnp.swapaxes(row_decay, 1, 2),
        jnp.swapaxes(col_decay, 1, 2),
    )
    return result.reshape(features.shape)


def fits_fused(features, row_decay, tile_mask):
    tile_rows, tile_cols, span_width = features.shape
    devices = lax.axis_size("row")
    return (
        lax.axis_size("col") == 1
        and tile_mask.shape[1] == 1
        and tile_rows * devices == tile_cols
        and devices % 4 == 0
        and tile_cols <= 64
        and (tile_rows * (tile_cols // devices)) % 16 == 0
        and span_width % (CHUNKS * 128) == 0
        and (tile_cols // devices) * row_decay.shape[-1] == 128
        and tile_rows * tile_cols % 256 == 0
        and all(
            size.bit_count() == 1
            for size in (tile_rows, tile_cols, devices, span_width // row_decay.shape[-1])
        )
    )


def per_device(features, write_vecs, read_vecs, row_decay, col_decay, tile_mask, skip_gain):
    tile_rows, tile_cols, span_width = features.shape
    if fits_fused(features, row_decay, tile_mask):
        return fused(features, write_vecs, read_vecs, row_decay, col_decay, tile_mask, skip_gain)
    head_count = row_decay.shape[-1]
    block_len = tile_cols // tile_mask.shape[1]
    patch_mask = jnp.repeat(tile_mask, block_len, axis=1)
    masked = jnp.where(patch_mask[..., None] > 0, features, jnp.zeros((), features.dtype))
    moved = (
        lax.all_to_all(masked, "row", split_axis=1, concat_axis=0, tiled=True),
        lax.all_to_all(write_vecs, "row", split_axis=1, concat_axis=0, tiled=True),
        lax.all_to_all(read_vecs, "row", split_axis=1, concat_axis=0, tiled=True),
        lax.all_to_all(col_decay, "row", split_axis=1, concat_axis=0, tiled=True),
    )
    result = column_chains(moved[0], moved[1], moved[2], moved[3], block_len)
    col_out = lax.all_to_all(result, "row", split_axis=0, concat_axis=1, tiled=True)
    local_terms, read_blocks = row_terms(masked, write_vecs, read_vecs, row_decay, block_len)
    if lax.axis_size("col") == 1 and tile_mask.shape[1] == 1:
        y_row = local_terms[0].reshape(features.shape)
    else:
        zero_states = jnp.zeros((tile_rows,) + local_terms[1].shape[2:], jnp.float32)
        closing_states, unused_states = jax.vmap(enter_states)(
            local_terms[2], local_terms[1], zero_states
        )
        device_decay = jnp.prod(local_terms[2], axis=1)
        identity = (jnp.ones_like(device_decay), jnp.zeros_like(closing_states))
        decay_before, state_before = entering_2((device_decay, closing_states), "col", link, identity)
        y_row = row_finish(local_terms, read_blocks, state_before)
    skip_vector = jnp.repeat(skip_gain, span_width // head_count)
    total = y_row + col_out.astype(jnp.float32) + skip_vector * features.astype(jnp.float32)
    return (patch_mask[..., None].astype(jnp.float32) * total).astype(jnp.bfloat16)


def solution(mesh):
    return jax.shard_map(
        per_device,
        mesh=mesh,
        in_specs=(
            P(("slides", "row"), "col", None),
            P(("slides", "row"), "col", None),
            P(("slides", "row"), "col", None),
            P(("slides", "row"), "col", None),
            P(("slides", "row"), "col", None),
            P(("slides", "row"), "col"),
            P(),
        ),
        out_specs=P(("slides", "row"), "col", None),
        check_vma=False,
    )
```

```python
import functools

import jax
import jax.numpy as jnp
from jax import lax
from jax.experimental import pallas as pl
from jax.experimental.pallas import tpu as pltpu
from jax.sharding import PartitionSpec as P


def entering_2(array, axis, combine, identity):
    devices, here = (lax.axis_size(axis), lax.axis_index(axis))
    everything = jax.tree.map(
        lambda part, kind: lax.all_gather(part.astype(kind), axis),
        array,
        (jnp.bfloat16, jnp.bfloat16),
    )
    start = jax.tree.map(
        lambda part, zero: jnp.broadcast_to(jnp.asarray(zero, part.dtype), part.shape),
        array,
        identity,
    )

    def step(k, before):
        reached = k < here
        new = combine(
            before, jax.tree.map(lambda part, own: part[k].astype(own.dtype), everything, array)
        )
        return jax.tree.map(lambda a, b: jnp.where(reached, a, b), new, before)

    return lax.fori_loop(0, devices, step, start)


def block_local(masked, write_vecs, read_vecs, decays):
    blocks, length, span_width = masked.shape
    head_count = decays.shape[-1]
    head_width = span_width // head_count
    slots = jnp.arange(length)
    upto = (slots[:, None] >= slots[None, :]).astype(decays.dtype)
    running = jnp.einsum("ts,ksh->kht", upto, decays, preferred_element_type=jnp.float32)
    scores = jnp.einsum("ktn,ksn->kts", read_vecs, write_vecs, preferred_element_type=jnp.float32)
    target_slots = jnp.arange(length)
    causal = target_slots[:, None] >= target_slots[None, :]
    spread = jnp.where(causal, running[:, :, :, None] - running[:, :, None, :], jnp.float32(0.0))
    weights = jnp.where(causal, scores[:, None] * jnp.exp(spread), jnp.float32(0.0)).astype(
        jnp.bfloat16
    )
    values = masked.reshape(blocks, length, head_count, head_width)
    inside = jnp.einsum("khts,kshp->kthp", weights, values, preferred_element_type=jnp.float32)
    closing = running[:, :, -1]
    scaled = (
        write_vecs.astype(jnp.float32)[:, None] * jnp.exp(closing[:, :, None] - running)[..., None]
    ).astype(jnp.bfloat16)
    block_state = jnp.einsum("khsn,kshp->khnp", scaled, values, preferred_element_type=jnp.float32)
    return (inside, block_state, jnp.exp(closing), running)


def enter_states(damping, block_state, initial):

    def advance(carry_state, element):
        factor, fresh_term = element
        return (factor[:, None, None] * carry_state + fresh_term, carry_state)

    return lax.scan(advance, initial, (damping, block_state))


def combine_out(inside, entering, read_blocks, running):
    carried = jnp.einsum(
        "ktn,khnp->kthp", read_blocks.astype(jnp.float32), entering, precision=lax.Precision.HIGHEST
    )
    total = inside + carried * jnp.swapaxes(jnp.exp(running), 1, 2)[..., None]
    return total.reshape(total.shape[0] * total.shape[1], total.shape[2] * total.shape[3])


def to_blocks(array, block_len):
    return array.reshape(
        array.shape[:-2] + (array.shape[-2] // block_len, block_len, array.shape[-1])
    )


def column_chains(masked, write_vecs, read_vecs, decays, block_len):

    def one_column(masked_c, write_c, read_c, decay_c):
        read_blocks = to_blocks(read_c, block_len)
        inside, block_state, damping, running = block_local(
            to_blocks(masked_c, block_len),
            to_blocks(write_c, block_len),
            read_blocks,
            to_blocks(decay_c, block_len),
        )
        if read_blocks.shape[0] == 1:
            return inside.reshape(masked_c.shape)
        zero_state = jnp.zeros(block_state.shape[1:], jnp.float32)
        closing_state, entering = enter_states(damping, block_state, zero_state)
        return combine_out(inside, entering, read_blocks, running)

    results = jax.vmap(one_column, in_axes=1, out_axes=1)(masked, write_vecs, read_vecs, decays)
    return results.astype(jnp.bfloat16)


def row_terms(masked, write_vecs, read_vecs, decays, block_len):
    read_blocks = to_blocks(read_vecs, block_len)
    local_terms = jax.vmap(block_local)(
        to_blocks(masked, block_len),
        to_blocks(write_vecs, block_len),
        read_blocks,
        to_blocks(decays, block_len),
    )
    return (local_terms, read_blocks)


def row_finish(local_terms, read_blocks, incoming):
    inside, block_state, damping, running = local_terms
    closing_state, entering = jax.vmap(enter_states)(damping, block_state, incoming)
    return jax.vmap(combine_out)(inside, entering, read_blocks, running)


def link(earlier, later):
    return (earlier[0] * later[0], later[0][..., None, None] * earlier[1] + later[1])


MESH = pl.DeviceIdType.MESH
CHUNKS = 4
PIECES = 2


def fused_kernel(
    shape,
    mask_hbm,
    skip_hbm,
    x_hbm,
    write_hbm,
    read_hbm,
    row_hbm,
    col_hbm,
    out_ref,
    rest_ref,
    final_ref,
    restore_ref,
    mask_ref,
    skip_ref,
    x_ref,
    write_ref,
    read_ref,
    row_ref,
    col_ref,
    aux_out,
    aux_in,
    help_in,
    scores_out,
    scores_in,
    col_scores,
    decay_out,
    decay_in,
    pair_x,
    pair_write,
    pair_col,
    kept_write,
    sent,
    got,
    col_sent,
    col_got,
    total,
    grow,
    fade,
    load_sems,
    x_sems,
    aux_sems,
    help_sems,
    score_sems,
    decay_sems,
    pair_sems,
    there_sems,
    back_sems,
    late_sem,
):
    devices, tile_rows, tile_cols, heads = shape
    per = tile_cols // devices
    block = tile_rows * per
    patches = tile_rows * tile_cols
    chunks, _, width = sent.shape
    head_width = chunks * width // heads
    state = write_ref.shape[-1]
    f32, bf16 = jnp.float32, jnp.bfloat16
    me = lax.axis_index("row")
    own = pl.ds(pl.multiple_of(me * block, block), block)

    def dot(a, b):
        return jnp.dot(a, b, preferred_element_type=f32)

    quarter, half = devices // 4, devices // 2
    middle = patches // 2
    upper = me < half
    first = devices - quarter
    last = me >= first
    soon = jnp.where(last, devices - 1, first - 1)

    def peer(step):
        return lax.rem(me + 1 + step, devices)

    def soon_peer(step):
        across_first = jnp.where(
            step < quarter, half + lax.rem(me + step, quarter), lax.rem(me + 1 + step - quarter, half)
        )
        return jnp.where(upper, across_first, lax.rem(me + 1 + step, soon + 1))

    def far_peer(step):
        across_first = jnp.where(
            step < half, half + lax.rem(me + step, half), lax.rem(me + 1 + step - half, half)
        )
        return jnp.where(upper, across_first, peer(step))

    def late_peer(step):
        return first + lax.rem(me + step, quarter)

    barrier = pltpu.get_barrier_semaphore()

    def each(steps, act):
        def body(step, carry):
            act(step)
            return carry

        lax.fori_loop(0, steps, body, 0)

    def greet(other, semaphore=barrier):
        pl.semaphore_signal(semaphore, inc=1, device_id={"row": other}, device_id_type=MESH)

    @pl.when(last)
    def _():
        each(quarter - 1, lambda step: greet(first + lax.rem(me + 1 + step, quarter)))

    @pl.when(jnp.logical_not(last))
    def _():
        each(devices - 1, lambda step: greet(lax.rem(me - 1 - step + devices, devices)))

    loads = [
        pltpu.make_async_copy(source, target, load_sems.at[i])
        for i, (source, target) in enumerate(
            (
                (mask_hbm, mask_ref),
                (write_hbm, write_ref),
                (read_hbm, read_ref),
                (col_hbm, col_ref),
                (row_hbm, row_ref),
                (skip_hbm, skip_ref),
            )
        )
    ]
    x_loads = [
        pltpu.make_async_copy(
            x_hbm.at[:, pl.ds(c * width, width)], x_ref.at[:, pl.ds(c * width, width)], x_sems.at[c]
        )
        for c in range(chunks)
    ]
    for load in loads[:4] + x_loads + loads[4:]:
        load.start()

    def send(source, target, sems, other):
        pltpu.make_async_remote_copy(
            src_ref=source.at[pl.ds(pl.multiple_of(other * block, block), block)],
            dst_ref=target.at[own],
            send_sem=sems.at[0],
            recv_sem=sems.at[1],
            device_id={"row": other},
            device_id_type=MESH,
        ).start()

    tail = me >= devices - 2
    head = me < 2
    odd = (me & 1) == 1

    def scatter_soon(source, target, sems):
        each(soon, lambda step: send(source, target, sems, soon_peer(step)))

    def scatter_late(source, target, sems):
        each(quarter, lambda step: send(source, target, sems, late_peer(step)))

    def give_back(source, target, sems):
        def act(step):
            other = peer(step)

            @pl.when(other >= 2)
            def _():
                send(source, target, sems, other)

        each(devices - 1, act)

    def wait(buffer, sem, count=devices - 1):
        part = buffer.at[pl.ds(0, block * count)]
        pltpu.make_async_copy(part, part, sem).wait()

    def wait_either(buffer, sem, one_more):
        @pl.when(one_more)
        def _():
            wait(buffer, sem, devices - 2)

        @pl.when(jnp.logical_not(one_more))
        def _():
            wait(buffer, sem, devices - 3)

    pairs = [(x_ref, pair_x), (kept_write, pair_write), (col_ref, pair_col)]

    def shift(i, size):
        return lax.shift_right_logical(i, size.bit_length() - 1)

    down = lax.broadcasted_iota(jnp.int32, (patches, 1), 0)
    across = lax.broadcasted_iota(jnp.int32, (1, patches), 1)

    def home(i):
        row = shift(i, per) & (tile_rows - 1)
        return row * tile_cols + shift(i, block) * per + (i & (per - 1))

    def ones(where):
        return where.astype(f32).astype(bf16)

    from_home = home(down)
    order = ones(from_home == across)

    def turned(places, ref):
        lanes = lax.broadcasted_iota(jnp.int32, (1, tile_cols), 1)
        return sum(
            lax.dot_general(
                ones(places == lanes + r * tile_cols),
                ref[r],
                (((1,), (1,)), ((), ())),
                preferred_element_type=f32,
            )
            for r in range(tile_rows)
        ).astype(bf16)

    x_loads[0].wait()
    sent[0] = dot(order, x_ref[:, :width]).astype(bf16)

    @pl.when(last)
    def _():
        pl.semaphore_wait(barrier, devices - 1)
        each(first, lambda step: greet(first - 1 - lax.rem(me + step, first), late_sem))

    @pl.when(jnp.logical_not(last))
    def _():
        pl.semaphore_wait(barrier, first - 1)

    @pl.when(jnp.logical_not(tail))
    def _():
        scatter_soon(sent.at[0], got.at[0], there_sems.at[0])

    for load in loads[:4]:
        load.wait()
    tile = [mask_ref[r].astype(f32) for r in range(tile_rows)]

    def keep(value):
        return jnp.concatenate(
            [value[r * tile_cols : (r + 1) * tile_cols] * tile[r] for r in range(tile_rows)]
        )

    kept_write[...] = keep(write_ref[...].astype(f32)).astype(bf16)
    aux_out[:, :state] = dot(order, kept_write[...]).astype(bf16)
    aux_out[:, state : 2 * state] = dot(order, read_ref[...]).astype(bf16)
    lanes = per * heads
    groups = patches // per
    lane_head = lax.broadcasted_iota(jnp.int32, (heads, lanes), 1) & (heads - 1)
    copies = ones(lax.broadcasted_iota(jnp.int32, (heads, lanes), 0) == lane_head)
    lane_col = shift(lax.broadcasted_iota(jnp.int32, (tile_cols, lanes), 1), heads)
    kept = (lax.broadcasted_iota(jnp.int32, (tile_cols, lanes), 0) & (per - 1)) == lane_col
    group = lax.broadcasted_iota(jnp.int32, (groups, tile_cols), 0)
    group_col = lax.broadcasted_iota(jnp.int32, (groups, tile_cols), 1)
    packed = jnp.zeros((groups, lanes), f32)
    for r in range(tile_rows):
        wide = lax.dot_general(
            col_ref[r], copies, (((0,), (0,)), ((), ())), preferred_element_type=f32
        )
        wide = jnp.where(kept, wide, 0.0).astype(bf16)
        packed += dot(ones(group == shift(group_col, per) * tile_rows + r), wide)
    decay_out[...] = packed.astype(bf16).reshape(decay_out.shape)

    def send_aux(other):
        def rows(index):
            return pl.ds(pl.multiple_of(index * block, block), block)

        def copy(source, target, send_sem, recv_sem):
            pltpu.make_async_remote_copy(
                src_ref=source,
                dst_ref=target,
                send_sem=send_sem,
                recv_sem=recv_sem,
                device_id={"row": other},
                device_id_type=MESH,
            ).start()

        above = other < half

        @pl.when(jnp.logical_or(above, jnp.logical_not(upper)))
        def _():
            copy(aux_out.at[rows(other)], aux_in.at[own], aux_sems.at[0], aux_sems.at[1])

        @pl.when(jnp.logical_and(above, upper))
        def _():
            copy(aux_out.at[rows(other + half)], help_in.at[own], help_sems.at[0], help_sems.at[1])

        @pl.when(jnp.logical_and(above, jnp.logical_not(upper)))
        def _():
            copy(
                aux_out.at[rows(other + half), pl.ds(state, state)],
                help_in.at[own, pl.ds(state, state)],
                help_sems.at[0],
                help_sems.at[2],
            )

        copy(decay_out.at[other], decay_in.at[me], decay_sems.at[0], decay_sems.at[1])

    each(soon, lambda step: send_aux(soon_peer(step)))
    aux_in[own, :] = aux_out[own, :]
    decay_in[me] = decay_out[me]

    @pl.when(upper)
    def _():
        twin = pl.ds(pl.multiple_of((me + half) * block, block), block)
        help_in[own, :] = aux_out[twin, :]


    def products(reads, writes):
        return lax.dot_general(
            reads, writes, (((1,), (1,)), ((), ())), preferred_element_type=f32
        )

    def causal(scores, allowed):
        return jnp.where(allowed, scores, 0.0).astype(bf16)

    same_col = (down & (per - 1)) == (across & (per - 1))
    earlier = (shift(down, 2 * block) > shift(across, 2 * block)) & same_col

    fold = ones(lax.broadcasted_iota(jnp.int32, (groups, 1), 0) == shift(across, per))
    slot = lax.broadcasted_iota(jnp.int32, (middle, middle), 0)
    slot = (slot & (per - 1)) * (middle // per) + shift(slot, per)
    swap = ones(slot == lax.broadcasted_iota(jnp.int32, (middle, middle), 1))

    def help_below():
        part = help_in.at[pl.ds(0, block * (half - 1))]
        pltpu.make_async_copy(part, part, help_sems.at[1]).wait()
        part = help_in.at[pl.ds(0, block * half), pl.ds(0, state)]
        pltpu.make_async_copy(part, part, help_sems.at[2]).wait()
        known = causal(
            products(help_in[:, state:], help_in[:middle, :state]), earlier[:, :middle]
        )
        scores_out[...] = dot(fold, dot(known, swap).astype(bf16)).astype(bf16)
        pltpu.make_async_remote_copy(
            src_ref=scores_out,
            dst_ref=scores_in,
            send_sem=score_sems.at[0],
            recv_sem=score_sems.at[1],
            device_id={"row": me + half},
            device_id_type=MESH,
        ).start()

    for c in range(chunks):
        if c:
            x_loads[c].wait()
            sent[c] = dot(order, x_ref[:, c * width : (c + 1) * width]).astype(bf16)
        got[c, block * (devices - 2) :, :] = jnp.zeros((2 * block, width), bf16)
        got[c, own, :] = sent[c, own, :]

        if c:

            @pl.when(jnp.logical_not(tail))
            def _():
                each(devices - 1, lambda step: send(sent.at[c], got.at[c], there_sems.at[c], far_peer(step)))

        else:

            @pl.when(jnp.logical_not(last))
            def _():
                pl.semaphore_wait(late_sem, quarter)
                each(quarter, lambda step: send_aux(late_peer(step)))
                scatter_late(sent.at[c], got.at[c], there_sems.at[c])

        if c == 2:

            @pl.when(upper)
            def _():
                help_below()

    @pl.when(jnp.logical_not(odd))
    def _():
        for i, (source, target) in enumerate(pairs):
            pltpu.make_async_remote_copy(
                src_ref=source,
                dst_ref=target,
                send_sem=pair_sems.at[i, 0],
                recv_sem=pair_sems.at[i, 1],
                device_id={"row": me + 1},
                device_id_type=MESH,
            ).start()

    def spread(c, count=heads):
        head = lax.broadcasted_iota(jnp.int32, (count, width), 0) & (heads - 1)
        lane = lax.broadcasted_iota(jnp.int32, (count, width), 1)
        return (head == shift(lane + c * width, head_width)).astype(f32)

    def running(below, decays, c):
        own_head = spread(c, decays.shape[1]).astype(bf16)
        return dot(below, dot(decays, own_head).astype(bf16))

    restore = keep((down == home(across)).astype(f32)).astype(bf16)
    in_row = (down >= across) & (shift(down, tile_cols) == shift(across, tile_cols))
    row_below = ones(in_row)
    for load in loads[4:]:
        load.wait()
    row_decays = turned(down, row_ref)
    own_scores = products(read_ref[...], write_ref[...])
    row_scores = causal(own_scores, in_row)
    in_home = (down >= across) & ((down & (tile_cols - 1)) == (across & (tile_cols - 1)))
    home_below = ones(in_home)
    home_decays = turned(down, col_ref)
    origin = shift(across, tile_cols)
    present = sum(jnp.where(origin == r, tile[r], 0.0) for r in range(tile_rows))
    home_scores = causal(own_scores * present, in_home)
    skip = jnp.broadcast_to(skip_ref[...], (8, heads))
    for c in range(chunks):
        cut = slice(c * width, (c + 1) * width)
        run = running(row_below, row_decays, c)
        faded = (x_ref[:, cut].astype(f32) * jnp.exp(-run)).astype(bf16)
        gain = jnp.dot(
            skip, spread(c), precision=lax.Precision.HIGHEST, preferred_element_type=f32
        )[:1]
        total[:, cut] = jnp.exp(run) * dot(row_scores, faded) + gain * x_ref[:, cut].astype(f32)

    col_below = ones((down >= across) & same_col)

    @pl.when(upper)
    def _():
        wait(aux_in, aux_sems.at[1])
        col_scores[...] = causal(products(aux_in[:, state:], aux_in[:, :state]), earlier)

    @pl.when(jnp.logical_not(upper))
    def _():
        wait(aux_in, aux_sems.at[1], half - 1)
        col_scores[:middle, middle:] = jnp.zeros((middle, middle), bf16)
        col_scores[middle:, middle:] = causal(
            products(aux_in[middle:, state:], aux_in[middle:, :state]), earlier[middle:, middle:]
        )
        pltpu.make_async_copy(scores_in, scores_in, score_sems.at[1]).wait()
        wide = lax.dot_general(
            fold, scores_in[...], (((0,), (0,)), ((), ())), preferred_element_type=f32
        )
        place = lax.broadcasted_iota(jnp.int32, (1, middle), 1)
        wide = jnp.where(shift(place, middle // per) == (down & (per - 1)), wide, 0.0)
        col_scores[:, :middle] = lax.dot_general(
            wide.astype(bf16), swap, (((1,), (1,)), ((), ())), preferred_element_type=f32
        ).astype(bf16)

    pieces = decay_in.at[pl.ds(0, devices - 1)]
    pltpu.make_async_copy(pieces, pieces, decay_sems.at[1]).wait()
    wide = lax.dot_general(
        fold,
        decay_in[...].reshape(groups, lanes),
        (((0,), (0,)), ((), ())),
        preferred_element_type=f32,
    )
    place = lax.broadcasted_iota(jnp.int32, (1, lanes), 1)
    col_decays = jnp.where(shift(place, heads) == (down & (per - 1)), wide, 0.0).astype(bf16)
    for c in range(chunks):
        run = running(col_below, col_decays, c)
        grow[c] = jnp.exp(run)
        fade[c] = jnp.exp(-run)

    for c in range(chunks):
        wait_either(got.at[c], there_sems.at[c, 1], tail)
        faded = (got[c].astype(f32) * fade[c]).astype(bf16)
        col_sent[c] = (grow[c] * dot(col_scores[...], faded)).astype(bf16)
        give_back(col_sent.at[c], col_got.at[c], back_sems.at[c])
        col_got[c, own, :] = col_sent[c, own, :]

    for c in range(chunks):
        cut = slice(c * width, (c + 1) * width)
        run = running(home_below, home_decays, c)
        grow[c] = jnp.exp(run)
        faded = (x_ref[:, cut].astype(f32) * jnp.exp(-run)).astype(bf16)
        total[:, cut] += grow[c] * dot(home_scores, faded)

    @pl.when(odd)
    def _():
        for i, (source, target) in enumerate(pairs):
            pltpu.make_async_copy(target, target, pair_sems.at[i, 1]).wait()
        alike = (down & (tile_cols - 1)) == (across & (tile_cols - 1))
        pair_after = ones((shift(down, tile_cols) < shift(across, tile_cols)) & alike)
        pair_decays = turned(down, pair_col)
        pair_scores = causal(products(read_ref[...], pair_write[...]), alike)
        for c in range(chunks):
            cut = slice(c * width, (c + 1) * width)
            run = running(pair_after, pair_decays, c)
            faded = (pair_x[:, cut].astype(f32) * jnp.exp(run)).astype(bf16)
            total[:, cut] += grow[c] * dot(pair_scores, faded)

    @pl.when(jnp.logical_not(odd))
    def _():
        for i, (source, target) in enumerate(pairs):
            pltpu.make_async_copy(source, source, pair_sems.at[i, 0]).wait()

    pltpu.make_async_copy(pieces, pieces, decay_sems.at[0]).wait()

    @pl.when(upper)
    def _():
        wait(aux_out, aux_sems.at[0], half - 1)
        wait(aux_out, help_sems.at[0], half - 1)
        pltpu.make_async_copy(scores_out, scores_out, score_sems.at[0]).wait()

    @pl.when(jnp.logical_not(upper))
    def _():
        wait(aux_out, aux_sems.at[0])
        part = help_in.at[pl.ds(0, block * half), pl.ds(0, state)]
        pltpu.make_async_copy(part, part, help_sems.at[0]).wait()

    @pl.when(jnp.logical_not(tail))
    def _():
        for c in range(chunks):
            wait(sent.at[c], there_sems.at[c, 0])

    total[...] = keep(total[...])
    rest_ref[...] = total[:, (chunks - 1) * width :]
    restore_ref[...] = restore
    for c in range(chunks):
        cut = slice(c * width, (c + 1) * width)

        if c:
            wait_either(col_sent.at[c - 1], back_sems.at[c - 1, 0], head)

        @pl.when(head)
        def _():
            col_got[c] = jnp.zeros((patches, width), bf16)

        @pl.when(jnp.logical_not(head))
        def _():
            wait(col_got.at[c], back_sems.at[c, 1])

        if c == chunks - 1:
            final_ref[...] = col_got[c]
        else:
            out_ref[:, cut] = (total[:, cut] + dot(restore, col_got[c])).astype(bf16)

    wait_either(col_sent.at[chunks - 1], back_sems.at[chunks - 1, 0], head)


def finish_kernel(done, rest, final, restore, out_hbm, last, sems):
    patches, width = final.shape
    ready = done.shape[1]
    rows = patches // PIECES
    copies = [pltpu.make_async_copy(done, out_hbm.at[:, pl.ds(0, ready)], sems.at[PIECES])]
    copies[0].start()
    for i in range(PIECES):
        part = pl.ds(i * rows, rows)
        back = jnp.dot(restore[part, :], final[...], preferred_element_type=jnp.float32)
        last[part, :] = (rest[part, :] + back).astype(jnp.bfloat16)
        copies.append(
            pltpu.make_async_copy(
                last.at[part], out_hbm.at[part, pl.ds(ready, width)], sems.at[i]
            )
        )
        copies[-1].start()
    for copy in copies:
        copy.wait()


def fused(features, write_vecs, read_vecs, row_decay, col_decay, tile_mask, skip_gain):
    tile_rows, tile_cols, span_width = features.shape
    heads, state = row_decay.shape[-1], write_vecs.shape[-1]
    patches = tile_rows * tile_cols
    devices = lax.axis_size("row")
    width = span_width // CHUNKS

    def flat(array):
        return array.reshape(patches, array.shape[-1])

    vmem = pl.BlockSpec(memory_space=pltpu.VMEM)
    piece = (CHUNKS, patches, width)
    aux = pltpu.VMEM((patches, 2 * state), jnp.bfloat16)
    per = tile_cols // devices
    scores = pltpu.VMEM((patches // per, patches // 2), jnp.bfloat16)
    decays = pltpu.VMEM((devices, tile_rows, per * heads), jnp.bfloat16)
    result = pl.pallas_call(
        functools.partial(fused_kernel, (devices, tile_rows, tile_cols, heads)),
        out_shape=(
            pltpu.VMEM((patches, span_width - width), jnp.bfloat16),
            pltpu.VMEM((patches, width), jnp.float32),
            pltpu.VMEM((patches, width), jnp.bfloat16),
            pltpu.VMEM((patches, patches), jnp.bfloat16),
        ),
        in_specs=[pl.BlockSpec(memory_space=pl.ANY)] * 7,
        out_specs=(vmem,) * 4,
        scratch_shapes=[
            pltpu.SMEM((tile_rows,), jnp.int32),
            pltpu.VMEM((1, heads), jnp.float32),
            pltpu.VMEM((patches, span_width), jnp.bfloat16),
            pltpu.VMEM((patches, state), jnp.bfloat16),
            pltpu.VMEM((patches, state), jnp.bfloat16),
            pltpu.VMEM((tile_rows, heads, tile_cols), jnp.bfloat16),
            pltpu.VMEM((tile_rows, heads, tile_cols), jnp.bfloat16),
            aux,
            aux,
            aux,
            scores,
            scores,
            pltpu.VMEM((patches, patches), jnp.bfloat16),
            decays,
            decays,
            pltpu.VMEM((patches, span_width), jnp.bfloat16),
            pltpu.VMEM((patches, state), jnp.bfloat16),
            pltpu.VMEM((tile_rows, heads, tile_cols), jnp.bfloat16),
            pltpu.VMEM((patches, state), jnp.bfloat16),
            pltpu.VMEM(piece, jnp.bfloat16),
            pltpu.VMEM(piece, jnp.bfloat16),
            pltpu.VMEM(piece, jnp.bfloat16),
            pltpu.VMEM(piece, jnp.bfloat16),
            pltpu.VMEM((patches, span_width), jnp.float32),
            pltpu.VMEM(piece, jnp.float32),
            pltpu.VMEM(piece, jnp.float32),
            pltpu.SemaphoreType.DMA((6,)),
            pltpu.SemaphoreType.DMA((CHUNKS,)),
            pltpu.SemaphoreType.DMA((2,)),
            pltpu.SemaphoreType.DMA((3,)),
            pltpu.SemaphoreType.DMA((2,)),
            pltpu.SemaphoreType.DMA((2,)),
            pltpu.SemaphoreType.DMA((3, 2)),
            pltpu.SemaphoreType.DMA((CHUNKS, 2)),
            pltpu.SemaphoreType.DMA((CHUNKS, 2)),
            pltpu.SemaphoreType.REGULAR,
        ],
        compiler_params=pltpu.CompilerParams(
            collective_id=0, has_side_effects=True, vmem_limit_bytes=60 * 2**20
        ),
    )(
        tile_mask.reshape(-1),
        skip_gain.reshape(1, heads),
        flat(features),
        flat(write_vecs),
        flat(read_vecs),
        jnp.swapaxes(row_decay, 1, 2),
        jnp.swapaxes(col_decay, 1, 2),
    )
    stored = pl.pallas_call(
        finish_kernel,
        out_shape=jax.ShapeDtypeStruct((patches, span_width), jnp.bfloat16),
        in_specs=[vmem] * 4,
        out_specs=pl.BlockSpec(memory_space=pl.ANY),
        scratch_shapes=[
            pltpu.VMEM((patches, width), jnp.bfloat16),
            pltpu.SemaphoreType.DMA((PIECES + 1,)),
        ],
    )(*(pltpu.with_memory_space_constraint(part, pltpu.VMEM) for part in result))
    return stored.reshape(features.shape)


def fits_fused(features, row_decay, tile_mask):
    tile_rows, tile_cols, span_width = features.shape
    devices = lax.axis_size("row")
    return (
        lax.axis_size("col") == 1
        and tile_mask.shape[1] == 1
        and tile_rows * devices == tile_cols
        and devices % 4 == 0
        and tile_cols <= 64
        and (tile_rows * (tile_cols // devices)) % 16 == 0
        and span_width % (CHUNKS * 128) == 0
        and (tile_cols // devices) * row_decay.shape[-1] == 128
        and tile_rows * tile_cols % 256 == 0
        and all(
            size.bit_count() == 1
            for size in (tile_rows, tile_cols, devices, span_width // row_decay.shape[-1])
        )
    )


def per_device(features, write_vecs, read_vecs, row_decay, col_decay, tile_mask, skip_gain):
    tile_rows, tile_cols, span_width = features.shape
    if fits_fused(features, row_decay, tile_mask):
        return fused(features, write_vecs, read_vecs, row_decay, col_decay, tile_mask, skip_gain)
    head_count = row_decay.shape[-1]
    block_len = tile_cols // tile_mask.shape[1]
    patch_mask = jnp.repeat(tile_mask, block_len, axis=1)
    masked = jnp.where(patch_mask[..., None] > 0, features, jnp.zeros((), features.dtype))
    moved = (
        lax.all_to_all(masked, "row", split_axis=1, concat_axis=0, tiled=True),
        lax.all_to_all(write_vecs, "row", split_axis=1, concat_axis=0, tiled=True),
        lax.all_to_all(read_vecs, "row", split_axis=1, concat_axis=0, tiled=True),
        lax.all_to_all(col_decay, "row", split_axis=1, concat_axis=0, tiled=True),
    )
    result = column_chains(moved[0], moved[1], moved[2], moved[3], block_len)
    col_out = lax.all_to_all(result, "row", split_axis=0, concat_axis=1, tiled=True)
    local_terms, read_blocks = row_terms(masked, write_vecs, read_vecs, row_decay, block_len)
    if lax.axis_size("col") == 1 and tile_mask.shape[1] == 1:
        y_row = local_terms[0].reshape(features.shape)
    else:
        zero_states = jnp.zeros((tile_rows,) + local_terms[1].shape[2:], jnp.float32)
        closing_states, unused_states = jax.vmap(enter_states)(
            local_terms[2], local_terms[1], zero_states
        )
        device_decay = jnp.prod(local_terms[2], axis=1)
        identity = (jnp.ones_like(device_decay), jnp.zeros_like(closing_states))
        decay_before, state_before = entering_2((device_decay, closing_states), "col", link, identity)
        y_row = row_finish(local_terms, read_blocks, state_before)
    skip_vector = jnp.repeat(skip_gain, span_width // head_count)
    total = y_row + col_out.astype(jnp.float32) + skip_vector * features.astype(jnp.float32)
    return (patch_mask[..., None].astype(jnp.float32) * total).astype(jnp.bfloat16)


def solution(mesh):
    return jax.shard_map(
        per_device,
        mesh=mesh,
        in_specs=(
            P(("slides", "row"), "col", None),
            P(("slides", "row"), "col", None),
            P(("slides", "row"), "col", None),
            P(("slides", "row"), "col", None),
            P(("slides", "row"), "col", None),
            P(("slides", "row"), "col"),
            P(),
        ),
        out_specs=P(("slides", "row"), "col", None),
        check_vma=False,
    )
```

```python
import functools

import jax
import jax.numpy as jnp
from jax import lax
from jax.experimental import pallas as pl
from jax.experimental.pallas import tpu as pltpu
from jax.sharding import PartitionSpec as P


def entering_2(array, axis, combine, identity):
    devices, here = (lax.axis_size(axis), lax.axis_index(axis))
    everything = jax.tree.map(
        lambda part, kind: lax.all_gather(part.astype(kind), axis),
        array,
        (jnp.bfloat16, jnp.bfloat16),
    )
    start = jax.tree.map(
        lambda part, zero: jnp.broadcast_to(jnp.asarray(zero, part.dtype), part.shape),
        array,
        identity,
    )

    def step(k, before):
        reached = k < here
        new = combine(
            before, jax.tree.map(lambda part, own: part[k].astype(own.dtype), everything, array)
        )
        return jax.tree.map(lambda a, b: jnp.where(reached, a, b), new, before)

    return lax.fori_loop(0, devices, step, start)


def block_local(masked, write_vecs, read_vecs, decays):
    blocks, length, span_width = masked.shape
    head_count = decays.shape[-1]
    head_width = span_width // head_count
    slots = jnp.arange(length)
    upto = (slots[:, None] >= slots[None, :]).astype(decays.dtype)
    running = jnp.einsum("ts,ksh->kht", upto, decays, preferred_element_type=jnp.float32)
    scores = jnp.einsum("ktn,ksn->kts", read_vecs, write_vecs, preferred_element_type=jnp.float32)
    target_slots = jnp.arange(length)
    causal = target_slots[:, None] >= target_slots[None, :]
    spread = jnp.where(causal, running[:, :, :, None] - running[:, :, None, :], jnp.float32(0.0))
    weights = jnp.where(causal, scores[:, None] * jnp.exp(spread), jnp.float32(0.0)).astype(
        jnp.bfloat16
    )
    values = masked.reshape(blocks, length, head_count, head_width)
    inside = jnp.einsum("khts,kshp->kthp", weights, values, preferred_element_type=jnp.float32)
    closing = running[:, :, -1]
    scaled = (
        write_vecs.astype(jnp.float32)[:, None] * jnp.exp(closing[:, :, None] - running)[..., None]
    ).astype(jnp.bfloat16)
    block_state = jnp.einsum("khsn,kshp->khnp", scaled, values, preferred_element_type=jnp.float32)
    return (inside, block_state, jnp.exp(closing), running)


def enter_states(damping, block_state, initial):

    def advance(carry_state, element):
        factor, fresh_term = element
        return (factor[:, None, None] * carry_state + fresh_term, carry_state)

    return lax.scan(advance, initial, (damping, block_state))


def combine_out(inside, entering, read_blocks, running):
    carried = jnp.einsum(
        "ktn,khnp->kthp", read_blocks.astype(jnp.float32), entering, precision=lax.Precision.HIGHEST
    )
    total = inside + carried * jnp.swapaxes(jnp.exp(running), 1, 2)[..., None]
    return total.reshape(total.shape[0] * total.shape[1], total.shape[2] * total.shape[3])


def to_blocks(array, block_len):
    return array.reshape(
        array.shape[:-2] + (array.shape[-2] // block_len, block_len, array.shape[-1])
    )


def column_chains(masked, write_vecs, read_vecs, decays, block_len):

    def one_column(masked_c, write_c, read_c, decay_c):
        read_blocks = to_blocks(read_c, block_len)
        inside, block_state, damping, running = block_local(
            to_blocks(masked_c, block_len),
            to_blocks(write_c, block_len),
            read_blocks,
            to_blocks(decay_c, block_len),
        )
        if read_blocks.shape[0] == 1:
            return inside.reshape(masked_c.shape)
        zero_state = jnp.zeros(block_state.shape[1:], jnp.float32)
        closing_state, entering = enter_states(damping, block_state, zero_state)
        return combine_out(inside, entering, read_blocks, running)

    results = jax.vmap(one_column, in_axes=1, out_axes=1)(masked, write_vecs, read_vecs, decays)
    return results.astype(jnp.bfloat16)


def row_terms(masked, write_vecs, read_vecs, decays, block_len):
    read_blocks = to_blocks(read_vecs, block_len)
    local_terms = jax.vmap(block_local)(
        to_blocks(masked, block_len),
        to_blocks(write_vecs, block_len),
        read_blocks,
        to_blocks(decays, block_len),
    )
    return (local_terms, read_blocks)


def row_finish(local_terms, read_blocks, incoming):
    inside, block_state, damping, running = local_terms
    closing_state, entering = jax.vmap(enter_states)(damping, block_state, incoming)
    return jax.vmap(combine_out)(inside, entering, read_blocks, running)


def link(earlier, later):
    return (earlier[0] * later[0], later[0][..., None, None] * earlier[1] + later[1])


MESH = pl.DeviceIdType.MESH
CHUNKS = 4
PIECES = 1


def fused_kernel(
    shape,
    mask_hbm,
    skip_hbm,
    x_hbm,
    write_hbm,
    read_hbm,
    row_hbm,
    col_hbm,
    out_ref,
    rest_ref,
    final_ref,
    restore_ref,
    mask_ref,
    skip_ref,
    x_ref,
    write_ref,
    read_ref,
    row_ref,
    col_ref,
    aux_out,
    aux_in,
    help_in,
    scores_out,
    scores_in,
    col_scores,
    decay_out,
    decay_in,
    pair_x,
    pair_write,
    pair_col,
    kept_write,
    sent,
    got,
    col_sent,
    col_got,
    total,
    grow,
    fade,
    load_sems,
    x_sems,
    aux_sems,
    help_sems,
    score_sems,
    decay_sems,
    pair_sems,
    there_sems,
    back_sems,
    late_sem,
):
    devices, tile_rows, tile_cols, heads = shape
    per = tile_cols // devices
    block = tile_rows * per
    patches = tile_rows * tile_cols
    chunks, _, width = sent.shape
    head_width = chunks * width // heads
    state = write_ref.shape[-1]
    f32, bf16 = jnp.float32, jnp.bfloat16
    me = lax.axis_index("row")
    own = pl.ds(pl.multiple_of(me * block, block), block)

    def dot(a, b):
        return jnp.dot(a, b, preferred_element_type=f32)

    quarter, half = devices // 4, devices // 2
    middle = patches // 2
    upper = me < half
    first = devices - quarter
    last = me >= first
    soon = jnp.where(last, devices - 1, first - 1)

    def peer(step):
        return lax.rem(me + 1 + step, devices)

    def soon_peer(step):
        across_first = jnp.where(
            step < quarter, half + lax.rem(me + step, quarter), lax.rem(me + 1 + step - quarter, half)
        )
        return jnp.where(upper, across_first, lax.rem(me + 1 + step, soon + 1))

    def far_peer(step):
        across_first = jnp.where(
            step < half, half + lax.rem(me + step, half), lax.rem(me + 1 + step - half, half)
        )
        return jnp.where(upper, across_first, peer(step))

    def late_peer(step):
        return first + lax.rem(me + step, quarter)

    barrier = pltpu.get_barrier_semaphore()

    def each(steps, act):
        def body(step, carry):
            act(step)
            return carry

        lax.fori_loop(0, steps, body, 0)

    def greet(other, semaphore=barrier):
        pl.semaphore_signal(semaphore, inc=1, device_id={"row": other}, device_id_type=MESH)

    @pl.when(last)
    def _():
        each(quarter - 1, lambda step: greet(first + lax.rem(me + 1 + step, quarter)))

    @pl.when(jnp.logical_not(last))
    def _():
        each(devices - 1, lambda step: greet(lax.rem(me - 1 - step + devices, devices)))

    loads = [
        pltpu.make_async_copy(source, target, load_sems.at[i])
        for i, (source, target) in enumerate(
            (
                (mask_hbm, mask_ref),
                (write_hbm, write_ref),
                (read_hbm, read_ref),
                (col_hbm, col_ref),
                (row_hbm, row_ref),
                (skip_hbm, skip_ref),
            )
        )
    ]
    x_loads = [
        pltpu.make_async_copy(
            x_hbm.at[:, pl.ds(c * width, width)], x_ref.at[:, pl.ds(c * width, width)], x_sems.at[c]
        )
        for c in range(chunks)
    ]
    for load in loads[:4] + x_loads + loads[4:]:
        load.start()

    def send(source, target, sems, other):
        pltpu.make_async_remote_copy(
            src_ref=source.at[pl.ds(pl.multiple_of(other * block, block), block)],
            dst_ref=target.at[own],
            send_sem=sems[0],
            recv_sem=sems[1],
            device_id={"row": other},
            device_id_type=MESH,
        ).start()

    tail = me >= devices - 2
    head = me < 2
    odd = (me & 1) == 1

    def scatter_soon(source, target, sems):
        each(soon, lambda step: send(source, target, sems, soon_peer(step)))

    def scatter_late(source, target, sems):
        each(quarter, lambda step: send(source, target, sems, late_peer(step)))

    def landing(c):
        return final_ref if c == chunks - 1 else col_got.at[c]

    def give_back(source, target, sems):
        def act(step):
            other = peer(step)

            @pl.when(other >= 2)
            def _():
                send(source, target, sems, other)

        each(devices - 1, act)

    def wait(buffer, sem, count=devices - 1):
        part = buffer.at[pl.ds(0, block * count)]
        pltpu.make_async_copy(part, part, sem).wait()

    def wait_either(buffer, sem, one_more):
        @pl.when(one_more)
        def _():
            wait(buffer, sem, devices - 2)

        @pl.when(jnp.logical_not(one_more))
        def _():
            wait(buffer, sem, devices - 3)

    pairs = [(x_ref, pair_x), (kept_write, pair_write), (col_ref, pair_col)]

    def shift(i, size):
        return lax.shift_right_logical(i, size.bit_length() - 1)

    down = lax.broadcasted_iota(jnp.int32, (patches, 1), 0)
    across = lax.broadcasted_iota(jnp.int32, (1, patches), 1)

    def home(i):
        row = shift(i, per) & (tile_rows - 1)
        return row * tile_cols + shift(i, block) * per + (i & (per - 1))

    def ones(where):
        return where.astype(f32).astype(bf16)

    from_home = home(down)
    order = ones(from_home == across)

    def turned(places, ref):
        lanes = lax.broadcasted_iota(jnp.int32, (1, tile_cols), 1)
        return sum(
            lax.dot_general(
                ones(places == lanes + r * tile_cols),
                ref[r],
                (((1,), (1,)), ((), ())),
                preferred_element_type=f32,
            )
            for r in range(tile_rows)
        ).astype(bf16)

    x_loads[0].wait()
    sent[0] = dot(order, x_ref[:, :width]).astype(bf16)

    @pl.when(last)
    def _():
        pl.semaphore_wait(barrier, devices - 1)
        each(first, lambda step: greet(first - 1 - lax.rem(me + step, first), late_sem))

    @pl.when(jnp.logical_not(last))
    def _():
        pl.semaphore_wait(barrier, first - 1)

    @pl.when(jnp.logical_not(tail))
    def _():
        scatter_soon(sent.at[0], got.at[0], (x_sems.at[0], there_sems.at[0]))

    for load in loads[:4]:
        load.wait()
    tile = [mask_ref[r].astype(f32) for r in range(tile_rows)]

    def keep(value):
        return jnp.concatenate(
            [value[r * tile_cols : (r + 1) * tile_cols] * tile[r] for r in range(tile_rows)]
        )

    kept_write[...] = keep(write_ref[...].astype(f32)).astype(bf16)
    aux_out[:, :state] = dot(order, kept_write[...]).astype(bf16)
    aux_out[:, state : 2 * state] = dot(order, read_ref[...]).astype(bf16)
    lanes = per * heads
    groups = patches // per
    lane_head = lax.broadcasted_iota(jnp.int32, (heads, lanes), 1) & (heads - 1)
    copies = ones(lax.broadcasted_iota(jnp.int32, (heads, lanes), 0) == lane_head)
    lane_col = shift(lax.broadcasted_iota(jnp.int32, (tile_cols, lanes), 1), heads)
    kept = (lax.broadcasted_iota(jnp.int32, (tile_cols, lanes), 0) & (per - 1)) == lane_col
    group = lax.broadcasted_iota(jnp.int32, (groups, tile_cols), 0)
    group_col = lax.broadcasted_iota(jnp.int32, (groups, tile_cols), 1)
    packed = jnp.zeros((groups, lanes), f32)
    for r in range(tile_rows):
        wide = lax.dot_general(
            col_ref[r], copies, (((0,), (0,)), ((), ())), preferred_element_type=f32
        )
        wide = jnp.where(kept, wide, 0.0).astype(bf16)
        packed += dot(ones(group == shift(group_col, per) * tile_rows + r), wide)
    decay_out[...] = packed.astype(bf16).reshape(decay_out.shape)

    def send_aux(other):
        def rows(index):
            return pl.ds(pl.multiple_of(index * block, block), block)

        def copy(source, target, send_sem, recv_sem):
            pltpu.make_async_remote_copy(
                src_ref=source,
                dst_ref=target,
                send_sem=send_sem,
                recv_sem=recv_sem,
                device_id={"row": other},
                device_id_type=MESH,
            ).start()

        above = other < half

        @pl.when(jnp.logical_or(above, jnp.logical_not(upper)))
        def _():
            copy(aux_out.at[rows(other)], aux_in.at[own], aux_sems.at[0], aux_sems.at[1])

        @pl.when(jnp.logical_and(above, upper))
        def _():
            copy(aux_out.at[rows(other + half)], help_in.at[own], help_sems.at[0], help_sems.at[1])

        @pl.when(jnp.logical_and(above, jnp.logical_not(upper)))
        def _():
            copy(
                aux_out.at[rows(other + half), pl.ds(state, state)],
                help_in.at[own, pl.ds(state, state)],
                help_sems.at[0],
                help_sems.at[2],
            )

        copy(decay_out.at[other], decay_in.at[me], decay_sems.at[0], decay_sems.at[1])

    each(soon, lambda step: send_aux(soon_peer(step)))
    aux_in[own, :] = aux_out[own, :]
    decay_in[me] = decay_out[me]

    @pl.when(upper)
    def _():
        twin = pl.ds(pl.multiple_of((me + half) * block, block), block)
        help_in[own, :] = aux_out[twin, :]


    def products(reads, writes):
        return lax.dot_general(
            reads, writes, (((1,), (1,)), ((), ())), preferred_element_type=f32
        )

    def causal(scores, allowed):
        return jnp.where(allowed, scores, 0.0).astype(bf16)

    same_col = (down & (per - 1)) == (across & (per - 1))
    earlier = (shift(down, 2 * block) > shift(across, 2 * block)) & same_col

    fold = ones(lax.broadcasted_iota(jnp.int32, (groups, 1), 0) == shift(across, per))
    slot = lax.broadcasted_iota(jnp.int32, (middle, middle), 0)
    slot = (slot & (per - 1)) * (middle // per) + shift(slot, per)
    swap = ones(slot == lax.broadcasted_iota(jnp.int32, (middle, middle), 1))

    two = groups // half
    span = middle // per
    lane_from = lax.broadcasted_iota(jnp.int32, (middle, middle), 0)
    lane_to = lax.broadcasted_iota(jnp.int32, (middle, middle), 1)
    free = span - span // 4
    aside = ones((lane_to == lane_from + free) & ((lane_from & (span - 1)) < span // 4))

    def help_below():
        part = help_in.at[pl.ds(0, block * (half - 1))]
        pltpu.make_async_copy(part, part, help_sems.at[1]).wait()
        part = help_in.at[pl.ds(0, block * half), pl.ds(0, state)]
        pltpu.make_async_copy(part, part, help_sems.at[2]).wait()
        known = causal(
            products(help_in[:, state:], help_in[:middle, :state]), earlier[:, :middle]
        )
        packed = dot(fold, dot(known, swap).astype(bf16))
        moved = dot(packed[two : 2 * two].astype(bf16), aside)
        scores_out[...] = jnp.concatenate(
            [packed[2 * two : 3 * two], packed[3 * two : 4 * two] + moved, packed[4 * two :]]
        ).astype(bf16)
        pltpu.make_async_remote_copy(
            src_ref=scores_out,
            dst_ref=scores_in,
            send_sem=score_sems.at[0],
            recv_sem=score_sems.at[1],
            device_id={"row": me + half},
            device_id_type=MESH,
        ).start()

    for c in range(chunks):
        if c:
            x_loads[c].wait()
            sent[c] = dot(order, x_ref[:, c * width : (c + 1) * width]).astype(bf16)
        got[c, block * (devices - 2) :, :] = jnp.zeros((2 * block, width), bf16)
        got[c, own, :] = sent[c, own, :]

        if c:

            @pl.when(jnp.logical_not(tail))
            def _():
                each(devices - 1, lambda step: send(sent.at[c], got.at[c], (x_sems.at[c], there_sems.at[c]), far_peer(step)))

        else:

            @pl.when(jnp.logical_not(last))
            def _():
                pl.semaphore_wait(late_sem, quarter)
                each(quarter, lambda step: send_aux(late_peer(step)))
                scatter_late(sent.at[c], got.at[c], (x_sems.at[c], there_sems.at[c]))

        if c == 2:

            @pl.when(upper)
            def _():
                help_below()

    @pl.when(jnp.logical_not(odd))
    def _():
        for i, (source, target) in enumerate(pairs):
            pltpu.make_async_remote_copy(
                src_ref=source,
                dst_ref=target,
                send_sem=pair_sems.at[i, 0],
                recv_sem=pair_sems.at[i, 1],
                device_id={"row": me + 1},
                device_id_type=MESH,
            ).start()

    def spread(c, count=heads):
        head = lax.broadcasted_iota(jnp.int32, (count, width), 0) & (heads - 1)
        lane = lax.broadcasted_iota(jnp.int32, (count, width), 1)
        return (head == shift(lane + c * width, head_width)).astype(f32)

    def running(below, decays, c):
        own_head = spread(c, decays.shape[1]).astype(bf16)
        return dot(below, dot(decays, own_head).astype(bf16))

    restore = keep((down == home(across)).astype(f32)).astype(bf16)
    in_row = (down >= across) & (shift(down, tile_cols) == shift(across, tile_cols))
    row_below = ones(in_row)
    for load in loads[4:]:
        load.wait()
    row_decays = turned(down, row_ref)
    own_scores = products(read_ref[...], write_ref[...])
    row_scores = causal(own_scores, in_row)
    in_home = (down >= across) & ((down & (tile_cols - 1)) == (across & (tile_cols - 1)))
    home_below = ones(in_home)
    home_decays = turned(down, col_ref)
    origin = shift(across, tile_cols)
    present = sum(jnp.where(origin == r, tile[r], 0.0) for r in range(tile_rows))
    home_scores = causal(own_scores * present, in_home)
    skip = jnp.broadcast_to(skip_ref[...], (8, heads))
    for c in range(chunks):
        cut = slice(c * width, (c + 1) * width)
        run = running(row_below, row_decays, c)
        faded = (x_ref[:, cut].astype(f32) * jnp.exp(-run)).astype(bf16)
        gain = jnp.dot(
            skip, spread(c), precision=lax.Precision.HIGHEST, preferred_element_type=f32
        )[:1]
        total[:, cut] = jnp.exp(run) * dot(row_scores, faded) + gain * x_ref[:, cut].astype(f32)

    col_below = ones((down >= across) & same_col)

    @pl.when(upper)
    def _():
        wait(aux_in, aux_sems.at[1])
        col_scores[...] = causal(products(aux_in[:, state:], aux_in[:, :state]), earlier)

    @pl.when(jnp.logical_not(upper))
    def _():
        wait(aux_in, aux_sems.at[1], half - 1)
        col_scores[:middle, middle:] = jnp.zeros((middle, middle), bf16)
        col_scores[middle:, middle:] = causal(
            products(aux_in[middle:, state:], aux_in[middle:, :state]), earlier[middle:, middle:]
        )
        pltpu.make_async_copy(scores_in, scores_in, score_sems.at[1]).wait()
        place = lax.broadcasted_iota(jnp.int32, (1, middle), 1)
        came = scores_in[...].astype(f32)
        shared = came[two : 2 * two]
        moved = lax.dot_general(
            shared.astype(bf16), aside, (((1,), (1,)), ((), ())), preferred_element_type=f32
        )
        stayed = jnp.where((place & (span - 1)) < free, shared, 0.0)
        packed = jnp.concatenate([jnp.zeros_like(moved), moved, came[:two], stayed, came[2 * two :]])
        wide = lax.dot_general(
            fold, packed.astype(bf16), (((0,), (0,)), ((), ())), preferred_element_type=f32
        )
        wide = jnp.where(shift(place, middle // per) == (down & (per - 1)), wide, 0.0)
        col_scores[:, :middle] = lax.dot_general(
            wide.astype(bf16), swap, (((1,), (1,)), ((), ())), preferred_element_type=f32
        ).astype(bf16)

    pieces = decay_in.at[pl.ds(0, devices - 1)]
    pltpu.make_async_copy(pieces, pieces, decay_sems.at[1]).wait()
    wide = lax.dot_general(
        fold,
        decay_in[...].reshape(groups, lanes),
        (((0,), (0,)), ((), ())),
        preferred_element_type=f32,
    )
    place = lax.broadcasted_iota(jnp.int32, (1, lanes), 1)
    col_decays = jnp.where(shift(place, heads) == (down & (per - 1)), wide, 0.0).astype(bf16)
    for c in range(chunks):
        run = running(col_below, col_decays, c)
        grow[c] = jnp.exp(run)
        fade[c] = jnp.exp(-run)

    for c in range(chunks):
        wait_either(got.at[c], there_sems.at[c], tail)
        faded = (got[c].astype(f32) * fade[c]).astype(bf16)
        col_sent[c] = (grow[c] * dot(col_scores[...], faded)).astype(bf16)
        give_back(col_sent.at[c], landing(c), (load_sems.at[c], back_sems.at[c]))
        landing(c)[own, :] = col_sent[c, own, :]

    for c in range(chunks):
        cut = slice(c * width, (c + 1) * width)
        run = running(home_below, home_decays, c)
        grow[c] = jnp.exp(run)
        faded = (x_ref[:, cut].astype(f32) * jnp.exp(-run)).astype(bf16)
        total[:, cut] += grow[c] * dot(home_scores, faded)

    @pl.when(odd)
    def _():
        for i, (source, target) in enumerate(pairs):
            pltpu.make_async_copy(target, target, pair_sems.at[i, 1]).wait()
        alike = (down & (tile_cols - 1)) == (across & (tile_cols - 1))
        pair_after = ones((shift(down, tile_cols) < shift(across, tile_cols)) & alike)
        pair_decays = turned(down, pair_col)
        pair_scores = causal(products(read_ref[...], pair_write[...]), alike)
        for c in range(chunks):
            cut = slice(c * width, (c + 1) * width)
            run = running(pair_after, pair_decays, c)
            faded = (pair_x[:, cut].astype(f32) * jnp.exp(run)).astype(bf16)
            total[:, cut] += grow[c] * dot(pair_scores, faded)

    @pl.when(jnp.logical_not(odd))
    def _():
        for i, (source, target) in enumerate(pairs):
            pltpu.make_async_copy(source, source, pair_sems.at[i, 0]).wait()

    pltpu.make_async_copy(pieces, pieces, decay_sems.at[0]).wait()

    @pl.when(upper)
    def _():
        wait(aux_out, aux_sems.at[0], half - 1)
        wait(aux_out, help_sems.at[0], half - 1)
        pltpu.make_async_copy(scores_out, scores_out, score_sems.at[0]).wait()

    @pl.when(jnp.logical_not(upper))
    def _():
        wait(aux_out, aux_sems.at[0])
        part = help_in.at[pl.ds(0, block * half), pl.ds(0, state)]
        pltpu.make_async_copy(part, part, help_sems.at[0]).wait()

    @pl.when(jnp.logical_not(tail))
    def _():
        for c in range(chunks):
            wait(sent.at[c], x_sems.at[c])

    total[...] = keep(total[...])
    rest_ref[...] = total[:, (chunks - 1) * width :]
    restore_ref[...] = restore
    for c in range(chunks):
        cut = slice(c * width, (c + 1) * width)

        if c:
            wait_either(col_sent.at[c - 1], load_sems.at[c - 1], head)

        @pl.when(head)
        def _():
            landing(c)[...] = jnp.zeros((patches, width), bf16)

        @pl.when(jnp.logical_not(head))
        def _():
            wait(landing(c), back_sems.at[c])

        if c < chunks - 1:
            out_ref[:, cut] = (total[:, cut] + dot(restore, col_got[c])).astype(bf16)

    wait_either(col_sent.at[chunks - 1], load_sems.at[chunks - 1], head)


def finish_kernel(done, rest, final, restore, out_hbm, last, sems):
    patches, width = final.shape
    ready = done.shape[1]
    rows = patches // PIECES
    copies = [pltpu.make_async_copy(done, out_hbm.at[:, pl.ds(0, ready)], sems.at[PIECES])]
    copies[0].start()
    for i in range(PIECES):
        part = pl.ds(i * rows, rows)
        back = jnp.dot(restore[part, :], final[...], preferred_element_type=jnp.float32)
        last[part, :] = (rest[part, :] + back).astype(jnp.bfloat16)
        copies.append(
            pltpu.make_async_copy(
                last.at[part], out_hbm.at[part, pl.ds(ready, width)], sems.at[i]
            )
        )
        copies[-1].start()
    for copy in copies:
        copy.wait()


def fused(features, write_vecs, read_vecs, row_decay, col_decay, tile_mask, skip_gain):
    tile_rows, tile_cols, span_width = features.shape
    heads, state = row_decay.shape[-1], write_vecs.shape[-1]
    patches = tile_rows * tile_cols
    devices = lax.axis_size("row")
    width = span_width // CHUNKS

    def flat(array):
        return array.reshape(patches, array.shape[-1])

    vmem = pl.BlockSpec(memory_space=pltpu.VMEM)
    piece = (CHUNKS, patches, width)
    aux = pltpu.VMEM((patches, 2 * state), jnp.bfloat16)
    per = tile_cols // devices
    scores = pltpu.VMEM((patches // per * 3 // 4, patches // 2), jnp.bfloat16)
    decays = pltpu.VMEM((devices, tile_rows, per * heads), jnp.bfloat16)
    result = pl.pallas_call(
        functools.partial(fused_kernel, (devices, tile_rows, tile_cols, heads)),
        out_shape=(
            pltpu.VMEM((patches, span_width - width), jnp.bfloat16),
            pltpu.VMEM((patches, width), jnp.float32),
            pltpu.VMEM((patches, width), jnp.bfloat16),
            pltpu.VMEM((patches, patches), jnp.bfloat16),
        ),
        in_specs=[pl.BlockSpec(memory_space=pl.ANY)] * 7,
        out_specs=(vmem,) * 4,
        scratch_shapes=[
            pltpu.SMEM((tile_rows,), jnp.int32),
            pltpu.VMEM((1, heads), jnp.float32),
            pltpu.VMEM((patches, span_width), jnp.bfloat16),
            pltpu.VMEM((patches, state), jnp.bfloat16),
            pltpu.VMEM((patches, state), jnp.bfloat16),
            pltpu.VMEM((tile_rows, heads, tile_cols), jnp.bfloat16),
            pltpu.VMEM((tile_rows, heads, tile_cols), jnp.bfloat16),
            aux,
            aux,
            aux,
            scores,
            scores,
            pltpu.VMEM((patches, patches), jnp.bfloat16),
            decays,
            decays,
            pltpu.VMEM((patches, span_width), jnp.bfloat16),
            pltpu.VMEM((patches, state), jnp.bfloat16),
            pltpu.VMEM((tile_rows, heads, tile_cols), jnp.bfloat16),
            pltpu.VMEM((patches, state), jnp.bfloat16),
            pltpu.VMEM(piece, jnp.bfloat16),
            pltpu.VMEM(piece, jnp.bfloat16),
            pltpu.VMEM(piece, jnp.bfloat16),
            pltpu.VMEM(piece, jnp.bfloat16),
            pltpu.VMEM((patches, span_width), jnp.float32),
            pltpu.VMEM(piece, jnp.float32),
            pltpu.VMEM(piece, jnp.float32),
            pltpu.SemaphoreType.DMA((6,)),
            pltpu.SemaphoreType.DMA((CHUNKS,)),
            pltpu.SemaphoreType.DMA((2,)),
            pltpu.SemaphoreType.DMA((3,)),
            pltpu.SemaphoreType.DMA((2,)),
            pltpu.SemaphoreType.DMA((2,)),
            pltpu.SemaphoreType.DMA((3, 2)),
            pltpu.SemaphoreType.DMA((CHUNKS,)),
            pltpu.SemaphoreType.DMA((CHUNKS,)),
            pltpu.SemaphoreType.REGULAR,
        ],
        compiler_params=pltpu.CompilerParams(
            collective_id=0, has_side_effects=True, vmem_limit_bytes=60 * 2**20
        ),
    )(
        tile_mask.reshape(-1),
        skip_gain.reshape(1, heads),
        flat(features),
        flat(write_vecs),
        flat(read_vecs),
        jnp.swapaxes(row_decay, 1, 2),
        jnp.swapaxes(col_decay, 1, 2),
    )
    stored = pl.pallas_call(
        finish_kernel,
        out_shape=jax.ShapeDtypeStruct((patches, span_width), jnp.bfloat16),
        in_specs=[vmem] * 4,
        out_specs=pl.BlockSpec(memory_space=pl.ANY),
        scratch_shapes=[
            pltpu.VMEM((patches, width), jnp.bfloat16),
            pltpu.SemaphoreType.DMA((PIECES + 1,)),
        ],
    )(*(pltpu.with_memory_space_constraint(part, pltpu.VMEM) for part in result))
    return stored.reshape(features.shape)


def fits_fused(features, row_decay, tile_mask):
    tile_rows, tile_cols, span_width = features.shape
    devices = lax.axis_size("row")
    return (
        lax.axis_size("col") == 1
        and tile_mask.shape[1] == 1
        and tile_rows * devices == tile_cols
        and devices == 16
        and tile_cols <= 64
        and (tile_rows * (tile_cols // devices)) % 16 == 0
        and span_width % (CHUNKS * 128) == 0
        and (tile_cols // devices) * row_decay.shape[-1] == 128
        and tile_rows * tile_cols % 256 == 0
        and all(
            size.bit_count() == 1
            for size in (tile_rows, tile_cols, devices, span_width // row_decay.shape[-1])
        )
    )


def per_device(features, write_vecs, read_vecs, row_decay, col_decay, tile_mask, skip_gain):
    tile_rows, tile_cols, span_width = features.shape
    if fits_fused(features, row_decay, tile_mask):
        return fused(features, write_vecs, read_vecs, row_decay, col_decay, tile_mask, skip_gain)
    head_count = row_decay.shape[-1]
    block_len = tile_cols // tile_mask.shape[1]
    patch_mask = jnp.repeat(tile_mask, block_len, axis=1)
    masked = jnp.where(patch_mask[..., None] > 0, features, jnp.zeros((), features.dtype))
    moved = (
        lax.all_to_all(masked, "row", split_axis=1, concat_axis=0, tiled=True),
        lax.all_to_all(write_vecs, "row", split_axis=1, concat_axis=0, tiled=True),
        lax.all_to_all(read_vecs, "row", split_axis=1, concat_axis=0, tiled=True),
        lax.all_to_all(col_decay, "row", split_axis=1, concat_axis=0, tiled=True),
    )
    result = column_chains(moved[0], moved[1], moved[2], moved[3], block_len)
    col_out = lax.all_to_all(result, "row", split_axis=0, concat_axis=1, tiled=True)
    local_terms, read_blocks = row_terms(masked, write_vecs, read_vecs, row_decay, block_len)
    if lax.axis_size("col") == 1 and tile_mask.shape[1] == 1:
        y_row = local_terms[0].reshape(features.shape)
    else:
        zero_states = jnp.zeros((tile_rows,) + local_terms[1].shape[2:], jnp.float32)
        closing_states, unused_states = jax.vmap(enter_states)(
            local_terms[2], local_terms[1], zero_states
        )
        device_decay = jnp.prod(local_terms[2], axis=1)
        identity = (jnp.ones_like(device_decay), jnp.zeros_like(closing_states))
        decay_before, state_before = entering_2((device_decay, closing_states), "col", link, identity)
        y_row = row_finish(local_terms, read_blocks, state_before)
    skip_vector = jnp.repeat(skip_gain, span_width // head_count)
    total = y_row + col_out.astype(jnp.float32) + skip_vector * features.astype(jnp.float32)
    return (patch_mask[..., None].astype(jnp.float32) * total).astype(jnp.bfloat16)


def solution(mesh):
    return jax.shard_map(
        per_device,
        mesh=mesh,
        in_specs=(
            P(("slides", "row"), "col", None),
            P(("slides", "row"), "col", None),
            P(("slides", "row"), "col", None),
            P(("slides", "row"), "col", None),
            P(("slides", "row"), "col", None),
            P(("slides", "row"), "col"),
            P(),
        ),
        out_specs=P(("slides", "row"), "col", None),
        check_vma=False,
    )
```

```python
import functools

import jax
import jax.numpy as jnp
from jax import lax
from jax.experimental import pallas as pl
from jax.experimental.pallas import tpu as pltpu
from jax.sharding import PartitionSpec as P


def entering_2(array, axis, combine, identity):
    devices, here = (lax.axis_size(axis), lax.axis_index(axis))
    everything = jax.tree.map(
        lambda part, kind: lax.all_gather(part.astype(kind), axis),
        array,
        (jnp.bfloat16, jnp.bfloat16),
    )
    start = jax.tree.map(
        lambda part, zero: jnp.broadcast_to(jnp.asarray(zero, part.dtype), part.shape),
        array,
        identity,
    )

    def step(k, before):
        reached = k < here
        new = combine(
            before, jax.tree.map(lambda part, own: part[k].astype(own.dtype), everything, array)
        )
        return jax.tree.map(lambda a, b: jnp.where(reached, a, b), new, before)

    return lax.fori_loop(0, devices, step, start)


def block_local(masked, write_vecs, read_vecs, decays):
    blocks, length, span_width = masked.shape
    head_count = decays.shape[-1]
    head_width = span_width // head_count
    slots = jnp.arange(length)
    upto = (slots[:, None] >= slots[None, :]).astype(decays.dtype)
    running = jnp.einsum("ts,ksh->kht", upto, decays, preferred_element_type=jnp.float32)
    scores = jnp.einsum("ktn,ksn->kts", read_vecs, write_vecs, preferred_element_type=jnp.float32)
    target_slots = jnp.arange(length)
    causal = target_slots[:, None] >= target_slots[None, :]
    spread = jnp.where(causal, running[:, :, :, None] - running[:, :, None, :], jnp.float32(0.0))
    weights = jnp.where(causal, scores[:, None] * jnp.exp(spread), jnp.float32(0.0)).astype(
        jnp.bfloat16
    )
    values = masked.reshape(blocks, length, head_count, head_width)
    inside = jnp.einsum("khts,kshp->kthp", weights, values, preferred_element_type=jnp.float32)
    closing = running[:, :, -1]
    scaled = (
        write_vecs.astype(jnp.float32)[:, None] * jnp.exp(closing[:, :, None] - running)[..., None]
    ).astype(jnp.bfloat16)
    block_state = jnp.einsum("khsn,kshp->khnp", scaled, values, preferred_element_type=jnp.float32)
    return (inside, block_state, jnp.exp(closing), running)


def enter_states(damping, block_state, initial):

    def advance(carry_state, element):
        factor, fresh_term = element
        return (factor[:, None, None] * carry_state + fresh_term, carry_state)

    return lax.scan(advance, initial, (damping, block_state))


def combine_out(inside, entering, read_blocks, running):
    carried = jnp.einsum(
        "ktn,khnp->kthp", read_blocks.astype(jnp.float32), entering, precision=lax.Precision.HIGHEST
    )
    total = inside + carried * jnp.swapaxes(jnp.exp(running), 1, 2)[..., None]
    return total.reshape(total.shape[0] * total.shape[1], total.shape[2] * total.shape[3])


def to_blocks(array, block_len):
    return array.reshape(
        array.shape[:-2] + (array.shape[-2] // block_len, block_len, array.shape[-1])
    )


def column_chains(masked, write_vecs, read_vecs, decays, block_len):

    def one_column(masked_c, write_c, read_c, decay_c):
        read_blocks = to_blocks(read_c, block_len)
        inside, block_state, damping, running = block_local(
            to_blocks(masked_c, block_len),
            to_blocks(write_c, block_len),
            read_blocks,
            to_blocks(decay_c, block_len),
        )
        if read_blocks.shape[0] == 1:
            return inside.reshape(masked_c.shape)
        zero_state = jnp.zeros(block_state.shape[1:], jnp.float32)
        closing_state, entering = enter_states(damping, block_state, zero_state)
        return combine_out(inside, entering, read_blocks, running)

    results = jax.vmap(one_column, in_axes=1, out_axes=1)(masked, write_vecs, read_vecs, decays)
    return results.astype(jnp.bfloat16)


def row_terms(masked, write_vecs, read_vecs, decays, block_len):
    read_blocks = to_blocks(read_vecs, block_len)
    local_terms = jax.vmap(block_local)(
        to_blocks(masked, block_len),
        to_blocks(write_vecs, block_len),
        read_blocks,
        to_blocks(decays, block_len),
    )
    return (local_terms, read_blocks)


def row_finish(local_terms, read_blocks, incoming):
    inside, block_state, damping, running = local_terms
    closing_state, entering = jax.vmap(enter_states)(damping, block_state, incoming)
    return jax.vmap(combine_out)(inside, entering, read_blocks, running)


def link(earlier, later):
    return (earlier[0] * later[0], later[0][..., None, None] * earlier[1] + later[1])


MESH = pl.DeviceIdType.MESH
CHUNKS = 4
PIECES = 1


def fused_kernel(
    shape,
    mask_hbm,
    skip_hbm,
    x_hbm,
    write_hbm,
    read_hbm,
    row_hbm,
    col_hbm,
    out_ref,
    rest_ref,
    final_ref,
    restore_ref,
    mask_ref,
    skip_ref,
    x_ref,
    write_ref,
    read_ref,
    row_ref,
    col_ref,
    aux_out,
    aux_in,
    help_in,
    scores_out,
    scores_in,
    col_scores,
    decay_out,
    decay_in,
    pair_x,
    pair_write,
    pair_col,
    kept_write,
    sent,
    got,
    col_sent,
    col_got,
    total,
    grow,
    fade,
    load_sems,
    x_sems,
    aux_sems,
    help_sems,
    score_sems,
    decay_sems,
    pair_sems,
    there_sems,
    back_sems,
    late_sem,
):
    devices, tile_rows, tile_cols, heads = shape
    per = tile_cols // devices
    block = tile_rows * per
    patches = tile_rows * tile_cols
    chunks, _, width = sent.shape
    head_width = chunks * width // heads
    state = write_ref.shape[-1]
    f32, bf16 = jnp.float32, jnp.bfloat16
    me = lax.axis_index("row")
    own = pl.ds(pl.multiple_of(me * block, block), block)

    def dot(a, b):
        return jnp.dot(a, b, preferred_element_type=f32)

    quarter, half = devices // 4, devices // 2
    middle = patches // 2
    upper = me < half
    first = devices - quarter
    last = me >= first
    soon = jnp.where(last, devices - 1, first - 1)

    def peer(step):
        return lax.rem(me + 1 + step, devices)

    def soon_peer(step):
        across_first = jnp.where(
            step < quarter, half + lax.rem(me + step, quarter), lax.rem(me + 1 + step - quarter, half)
        )
        return jnp.where(upper, across_first, lax.rem(me + 1 + step, soon + 1))

    def far_peer(step):
        place = lax.rem(me + step, half)
        place = lax.shift_right_logical(place, 1) + (place & 1) * quarter
        across_first = jnp.where(
            step < half, half + place, lax.rem(me + 1 + step - half, half)
        )
        return jnp.where(upper, across_first, peer(step))

    def late_peer(step):
        return first + lax.rem(me + step, quarter)

    barrier = pltpu.get_barrier_semaphore()

    def each(steps, act):
        def body(step, carry):
            act(step)
            return carry

        lax.fori_loop(0, steps, body, 0)

    def greet(other, semaphore=barrier):
        pl.semaphore_signal(semaphore, inc=1, device_id={"row": other}, device_id_type=MESH)

    @pl.when(last)
    def _():
        each(quarter - 1, lambda step: greet(first + lax.rem(me + 1 + step, quarter)))

    @pl.when(jnp.logical_not(last))
    def _():
        def act(step):
            other = lax.rem(me - lax.rem(me, quarter) - 1 - step + devices, devices)

            @pl.when(other != me)
            def _():
                greet(other)

        each(devices, act)

    loads = [
        pltpu.make_async_copy(source, target, load_sems.at[i])
        for i, (source, target) in enumerate(
            (
                (mask_hbm, mask_ref),
                (write_hbm, write_ref),
                (read_hbm, read_ref),
                (col_hbm, col_ref),
                (row_hbm, row_ref),
                (skip_hbm, skip_ref),
            )
        )
    ]
    x_loads = [
        pltpu.make_async_copy(
            x_hbm.at[:, pl.ds(c * width, width)], x_ref.at[:, pl.ds(c * width, width)], x_sems.at[c]
        )
        for c in range(chunks)
    ]
    for load in loads[:4] + x_loads + loads[4:]:
        load.start()

    def send(source, target, sems, other):
        pltpu.make_async_remote_copy(
            src_ref=source.at[pl.ds(pl.multiple_of(other * block, block), block)],
            dst_ref=target.at[own],
            send_sem=sems[0],
            recv_sem=sems[1],
            device_id={"row": other},
            device_id_type=MESH,
        ).start()

    tail = me >= devices - 2
    head = me < 2
    odd = (me & 1) == 1

    def scatter_soon(source, target, sems):
        each(soon, lambda step: send(source, target, sems, soon_peer(step)))

    def scatter_late(source, target, sems):
        each(quarter, lambda step: send(source, target, sems, late_peer(step)))

    def landing(c):
        return final_ref if c == chunks - 1 else col_got.at[c]

    def give_back(source, target, sems):
        def act(step):
            other = far_peer(step)

            @pl.when(other >= 2)
            def _():
                send(source, target, sems, other)

        each(devices - 1, act)

    def wait(buffer, sem, count=devices - 1):
        part = buffer.at[pl.ds(0, block * count)]
        pltpu.make_async_copy(part, part, sem).wait()

    def wait_either(buffer, sem, one_more):
        @pl.when(one_more)
        def _():
            wait(buffer, sem, devices - 2)

        @pl.when(jnp.logical_not(one_more))
        def _():
            wait(buffer, sem, devices - 3)

    pair_away = [load_sems.at[4], load_sems.at[5], pair_sems.at[3]]
    pairs = [(x_ref, pair_x), (kept_write, pair_write), (col_ref, pair_col)]

    def shift(i, size):
        return lax.shift_right_logical(i, size.bit_length() - 1)

    down = lax.broadcasted_iota(jnp.int32, (patches, 1), 0)
    across = lax.broadcasted_iota(jnp.int32, (1, patches), 1)

    def home(i):
        row = shift(i, per) & (tile_rows - 1)
        return row * tile_cols + shift(i, block) * per + (i & (per - 1))

    def ones(where):
        return where.astype(f32).astype(bf16)

    from_home = home(down)
    order = ones(from_home == across)

    def turned(places, ref):
        lanes = lax.broadcasted_iota(jnp.int32, (1, tile_cols), 1)
        return sum(
            lax.dot_general(
                ones(places == lanes + r * tile_cols),
                ref[r],
                (((1,), (1,)), ((), ())),
                preferred_element_type=f32,
            )
            for r in range(tile_rows)
        ).astype(bf16)

    x_loads[0].wait()
    sent[0] = dot(order, x_ref[:, :width]).astype(bf16)

    @pl.when(last)
    def _():
        pl.semaphore_wait(barrier, devices - 1)
        each(first, lambda step: greet(first - 1 - lax.rem(me + step, first), late_sem))

    @pl.when(jnp.logical_not(last))
    def _():
        pl.semaphore_wait(barrier, first - 1)

    @pl.when(jnp.logical_not(tail))
    def _():
        scatter_soon(sent.at[0], got.at[0], (x_sems.at[0], there_sems.at[0]))

    for load in loads[:4]:
        load.wait()
    tile = [mask_ref[r].astype(f32) for r in range(tile_rows)]

    def keep(value):
        return jnp.concatenate(
            [value[r * tile_cols : (r + 1) * tile_cols] * tile[r] for r in range(tile_rows)]
        )

    kept_write[...] = keep(write_ref[...].astype(f32)).astype(bf16)
    aux_out[:, :state] = dot(order, kept_write[...]).astype(bf16)
    aux_out[:, state : 2 * state] = dot(order, read_ref[...]).astype(bf16)
    lanes = per * heads
    groups = patches // per
    lane_head = lax.broadcasted_iota(jnp.int32, (heads, lanes), 1) & (heads - 1)
    copies = ones(lax.broadcasted_iota(jnp.int32, (heads, lanes), 0) == lane_head)
    lane_col = shift(lax.broadcasted_iota(jnp.int32, (tile_cols, lanes), 1), heads)
    kept = (lax.broadcasted_iota(jnp.int32, (tile_cols, lanes), 0) & (per - 1)) == lane_col
    group = lax.broadcasted_iota(jnp.int32, (groups, tile_cols), 0)
    group_col = lax.broadcasted_iota(jnp.int32, (groups, tile_cols), 1)
    packed = jnp.zeros((groups, lanes), f32)
    for r in range(tile_rows):
        wide = lax.dot_general(
            col_ref[r], copies, (((0,), (0,)), ((), ())), preferred_element_type=f32
        )
        wide = jnp.where(kept, wide, 0.0).astype(bf16)
        packed += dot(ones(group == shift(group_col, per) * tile_rows + r), wide)
    decay_out[...] = packed.astype(bf16).reshape(decay_out.shape)

    def send_aux(other):
        def rows(index):
            return pl.ds(pl.multiple_of(index * block, block), block)

        def copy(source, target, send_sem, recv_sem):
            pltpu.make_async_remote_copy(
                src_ref=source,
                dst_ref=target,
                send_sem=send_sem,
                recv_sem=recv_sem,
                device_id={"row": other},
                device_id_type=MESH,
            ).start()

        above = other < half

        @pl.when(jnp.logical_or(above, jnp.logical_not(upper)))
        def _():
            copy(aux_out.at[rows(other)], aux_in.at[own], aux_sems.at[0], aux_sems.at[1])

        @pl.when(jnp.logical_and(above, upper))
        def _():
            copy(aux_out.at[rows(other + half)], help_in.at[own], help_sems.at[0], help_sems.at[1])

        @pl.when(jnp.logical_and(above, jnp.logical_not(upper)))
        def _():
            copy(
                aux_out.at[rows(other + half), pl.ds(state, state)],
                help_in.at[own, pl.ds(state, state)],
                help_sems.at[0],
                help_sems.at[2],
            )

        copy(decay_out.at[other], decay_in.at[me], decay_sems.at[0], decay_sems.at[1])

    each(soon, lambda step: send_aux(soon_peer(step)))
    aux_in[own, :] = aux_out[own, :]
    decay_in[me] = decay_out[me]

    @pl.when(upper)
    def _():
        twin = pl.ds(pl.multiple_of((me + half) * block, block), block)
        help_in[own, :] = aux_out[twin, :]


    def products(reads, writes):
        return lax.dot_general(
            reads, writes, (((1,), (1,)), ((), ())), preferred_element_type=f32
        )

    def causal(scores, allowed):
        return jnp.where(allowed, scores, 0.0).astype(bf16)

    same_col = (down & (per - 1)) == (across & (per - 1))
    earlier = (shift(down, 2 * block) > shift(across, 2 * block)) & same_col

    fold = ones(lax.broadcasted_iota(jnp.int32, (groups, 1), 0) == shift(across, per))
    slot = lax.broadcasted_iota(jnp.int32, (middle, middle), 0)
    slot = (slot & (per - 1)) * (middle // per) + shift(slot, per)
    swap = ones(slot == lax.broadcasted_iota(jnp.int32, (middle, middle), 1))

    two = groups // half
    span = middle // per
    lane_from = lax.broadcasted_iota(jnp.int32, (middle, middle), 0)
    lane_to = lax.broadcasted_iota(jnp.int32, (middle, middle), 1)
    free = span - span // 4
    aside = ones((lane_to == lane_from + free) & ((lane_from & (span - 1)) < span // 4))

    def help_below():
        part = help_in.at[pl.ds(0, block * (half - 1))]
        pltpu.make_async_copy(part, part, help_sems.at[1]).wait()
        part = help_in.at[pl.ds(0, block * half), pl.ds(0, state)]
        pltpu.make_async_copy(part, part, help_sems.at[2]).wait()
        known = causal(
            products(help_in[:, state:], help_in[:middle, :state]), earlier[:, :middle]
        )
        packed = dot(fold, dot(known, swap).astype(bf16))
        moved = dot(packed[two : 2 * two].astype(bf16), aside)
        scores_out[...] = jnp.concatenate(
            [packed[2 * two : 3 * two], packed[3 * two : 4 * two] + moved, packed[4 * two :]]
        ).astype(bf16)
        pltpu.make_async_remote_copy(
            src_ref=scores_out,
            dst_ref=scores_in,
            send_sem=score_sems.at[0],
            recv_sem=score_sems.at[1],
            device_id={"row": me + half},
            device_id_type=MESH,
        ).start()

    for c in range(chunks):
        if c:
            x_loads[c].wait()
            sent[c] = dot(order, x_ref[:, c * width : (c + 1) * width]).astype(bf16)
        got[c, block * (devices - 2) :, :] = jnp.zeros((2 * block, width), bf16)
        got[c, own, :] = sent[c, own, :]

        if c:

            @pl.when(jnp.logical_not(tail))
            def _():
                each(devices - 1, lambda step: send(sent.at[c], got.at[c], (x_sems.at[c], there_sems.at[c]), far_peer(step)))

        else:

            @pl.when(jnp.logical_not(last))
            def _():
                pl.semaphore_wait(late_sem, quarter)
                each(quarter, lambda step: send_aux(late_peer(step)))
                scatter_late(sent.at[c], got.at[c], (x_sems.at[c], there_sems.at[c]))

        if c == 2:

            @pl.when(upper)
            def _():
                help_below()

    for load in loads[4:]:
        load.wait()

    @pl.when(jnp.logical_not(odd))
    def _():
        for i, (source, target) in enumerate(pairs):
            pltpu.make_async_remote_copy(
                src_ref=source,
                dst_ref=target,
                send_sem=pair_away[i],
                recv_sem=pair_sems.at[i],
                device_id={"row": me + 1},
                device_id_type=MESH,
            ).start()

    def spread(c, count=heads):
        head = lax.broadcasted_iota(jnp.int32, (count, width), 0) & (heads - 1)
        lane = lax.broadcasted_iota(jnp.int32, (count, width), 1)
        return (head == shift(lane + c * width, head_width)).astype(f32)

    def running(below, decays, c):
        own_head = spread(c, decays.shape[1]).astype(bf16)
        return dot(below, dot(decays, own_head).astype(bf16))

    restore = keep((down == home(across)).astype(f32)).astype(bf16)
    in_row = (down >= across) & (shift(down, tile_cols) == shift(across, tile_cols))
    row_below = ones(in_row)
    row_decays = turned(down, row_ref)
    own_scores = products(read_ref[...], write_ref[...])
    row_scores = causal(own_scores, in_row)
    in_home = (down >= across) & ((down & (tile_cols - 1)) == (across & (tile_cols - 1)))
    home_below = ones(in_home)
    home_decays = turned(down, col_ref)
    origin = shift(across, tile_cols)
    present = sum(jnp.where(origin == r, tile[r], 0.0) for r in range(tile_rows))
    home_scores = causal(own_scores * present, in_home)
    skip = jnp.broadcast_to(skip_ref[...], (8, heads))
    for c in range(chunks):
        cut = slice(c * width, (c + 1) * width)
        run = running(row_below, row_decays, c)
        faded = (x_ref[:, cut].astype(f32) * jnp.exp(-run)).astype(bf16)
        gain = jnp.dot(
            skip, spread(c), precision=lax.Precision.HIGHEST, preferred_element_type=f32
        )[:1]
        total[:, cut] = jnp.exp(run) * dot(row_scores, faded) + gain * x_ref[:, cut].astype(f32)

    col_below = ones((down >= across) & same_col)

    @pl.when(upper)
    def _():
        wait(aux_in, aux_sems.at[1])
        col_scores[...] = causal(products(aux_in[:, state:], aux_in[:, :state]), earlier)

    @pl.when(jnp.logical_not(upper))
    def _():
        wait(aux_in, aux_sems.at[1], half - 1)
        col_scores[:middle, middle:] = jnp.zeros((middle, middle), bf16)
        col_scores[middle:, middle:] = causal(
            products(aux_in[middle:, state:], aux_in[middle:, :state]), earlier[middle:, middle:]
        )
        pltpu.make_async_copy(scores_in, scores_in, score_sems.at[1]).wait()
        place = lax.broadcasted_iota(jnp.int32, (1, middle), 1)
        came = scores_in[...].astype(f32)
        shared = came[two : 2 * two]
        moved = lax.dot_general(
            shared.astype(bf16), aside, (((1,), (1,)), ((), ())), preferred_element_type=f32
        )
        stayed = jnp.where((place & (span - 1)) < free, shared, 0.0)
        packed = jnp.concatenate([jnp.zeros_like(moved), moved, came[:two], stayed, came[2 * two :]])
        wide = lax.dot_general(
            fold, packed.astype(bf16), (((0,), (0,)), ((), ())), preferred_element_type=f32
        )
        wide = jnp.where(shift(place, middle // per) == (down & (per - 1)), wide, 0.0)
        col_scores[:, :middle] = lax.dot_general(
            wide.astype(bf16), swap, (((1,), (1,)), ((), ())), preferred_element_type=f32
        ).astype(bf16)

    pieces = decay_in.at[pl.ds(0, devices - 1)]
    pltpu.make_async_copy(pieces, pieces, decay_sems.at[1]).wait()
    wide = lax.dot_general(
        fold,
        decay_in[...].reshape(groups, lanes),
        (((0,), (0,)), ((), ())),
        preferred_element_type=f32,
    )
    place = lax.broadcasted_iota(jnp.int32, (1, lanes), 1)
    col_decays = jnp.where(shift(place, heads) == (down & (per - 1)), wide, 0.0).astype(bf16)
    for c in range(chunks):
        run = running(col_below, col_decays, c)
        grow[c] = jnp.exp(run)
        fade[c] = jnp.exp(-run)

    for c in range(chunks):
        wait_either(got.at[c], there_sems.at[c], tail)
        faded = (got[c].astype(f32) * fade[c]).astype(bf16)
        col_sent[c] = (grow[c] * dot(col_scores[...], faded)).astype(bf16)
        give_back(col_sent.at[c], landing(c), (load_sems.at[c], back_sems.at[c]))
        landing(c)[own, :] = col_sent[c, own, :]

    for c in range(chunks):
        cut = slice(c * width, (c + 1) * width)
        run = running(home_below, home_decays, c)
        grow[c] = jnp.exp(run)
        faded = (x_ref[:, cut].astype(f32) * jnp.exp(-run)).astype(bf16)
        total[:, cut] += grow[c] * dot(home_scores, faded)

    @pl.when(odd)
    def _():
        for i, (source, target) in enumerate(pairs):
            pltpu.make_async_copy(target, target, pair_sems.at[i]).wait()
        alike = (down & (tile_cols - 1)) == (across & (tile_cols - 1))
        pair_after = ones((shift(down, tile_cols) < shift(across, tile_cols)) & alike)
        pair_decays = turned(down, pair_col)
        pair_scores = causal(products(read_ref[...], pair_write[...]), alike)
        for c in range(chunks):
            cut = slice(c * width, (c + 1) * width)
            run = running(pair_after, pair_decays, c)
            faded = (pair_x[:, cut].astype(f32) * jnp.exp(run)).astype(bf16)
            total[:, cut] += grow[c] * dot(pair_scores, faded)

    @pl.when(jnp.logical_not(odd))
    def _():
        for i, (source, target) in enumerate(pairs):
            pltpu.make_async_copy(source, source, pair_away[i]).wait()

    pltpu.make_async_copy(pieces, pieces, decay_sems.at[0]).wait()

    @pl.when(upper)
    def _():
        wait(aux_out, aux_sems.at[0], half - 1)
        wait(aux_out, help_sems.at[0], half - 1)
        pltpu.make_async_copy(scores_out, scores_out, score_sems.at[0]).wait()

    @pl.when(jnp.logical_not(upper))
    def _():
        wait(aux_out, aux_sems.at[0])
        part = help_in.at[pl.ds(0, block * half), pl.ds(0, state)]
        pltpu.make_async_copy(part, part, help_sems.at[0]).wait()

    @pl.when(jnp.logical_not(tail))
    def _():
        for c in range(chunks):
            wait(sent.at[c], x_sems.at[c])

    total[...] = keep(total[...])
    rest_ref[...] = total[:, (chunks - 1) * width :]
    restore_ref[...] = restore
    for c in range(chunks):
        cut = slice(c * width, (c + 1) * width)

        if c:
            wait_either(col_sent.at[c - 1], load_sems.at[c - 1], head)

        @pl.when(head)
        def _():
            landing(c)[...] = jnp.zeros((patches, width), bf16)

        @pl.when(jnp.logical_not(head))
        def _():
            wait(landing(c), back_sems.at[c])

        if c < chunks - 1:
            out_ref[:, cut] = (total[:, cut] + dot(restore, col_got[c])).astype(bf16)

    wait_either(col_sent.at[chunks - 1], load_sems.at[chunks - 1], head)


def finish_kernel(done, rest, final, restore, out_hbm, last, sems):
    patches, width = final.shape
    ready = done.shape[1]
    rows = patches // PIECES
    copies = [pltpu.make_async_copy(done, out_hbm.at[:, pl.ds(0, ready)], sems.at[PIECES])]
    copies[0].start()
    for i in range(PIECES):
        part = pl.ds(i * rows, rows)
        back = jnp.dot(restore[part, :], final[...], preferred_element_type=jnp.float32)
        last[part, :] = (rest[part, :] + back).astype(jnp.bfloat16)
        copies.append(
            pltpu.make_async_copy(
                last.at[part], out_hbm.at[part, pl.ds(ready, width)], sems.at[i]
            )
        )
        copies[-1].start()
    for copy in copies:
        copy.wait()


def fused(features, write_vecs, read_vecs, row_decay, col_decay, tile_mask, skip_gain):
    tile_rows, tile_cols, span_width = features.shape
    heads, state = row_decay.shape[-1], write_vecs.shape[-1]
    patches = tile_rows * tile_cols
    devices = lax.axis_size("row")
    width = span_width // CHUNKS

    def flat(array):
        return array.reshape(patches, array.shape[-1])

    vmem = pl.BlockSpec(memory_space=pltpu.VMEM)
    piece = (CHUNKS, patches, width)
    aux = pltpu.VMEM((patches, 2 * state), jnp.bfloat16)
    per = tile_cols // devices
    scores = pltpu.VMEM((patches // per * 3 // 4, patches // 2), jnp.bfloat16)
    decays = pltpu.VMEM((devices, tile_rows, per * heads), jnp.bfloat16)
    result = pl.pallas_call(
        functools.partial(fused_kernel, (devices, tile_rows, tile_cols, heads)),
        out_shape=(
            pltpu.VMEM((patches, span_width - width), jnp.bfloat16),
            pltpu.VMEM((patches, width), jnp.float32),
            pltpu.VMEM((patches, width), jnp.bfloat16),
            pltpu.VMEM((patches, patches), jnp.bfloat16),
        ),
        in_specs=[pl.BlockSpec(memory_space=pl.ANY)] * 7,
        out_specs=(vmem,) * 4,
        scratch_shapes=[
            pltpu.SMEM((tile_rows,), jnp.int32),
            pltpu.VMEM((1, heads), jnp.float32),
            pltpu.VMEM((patches, span_width), jnp.bfloat16),
            pltpu.VMEM((patches, state), jnp.bfloat16),
            pltpu.VMEM((patches, state), jnp.bfloat16),
            pltpu.VMEM((tile_rows, heads, tile_cols), jnp.bfloat16),
            pltpu.VMEM((tile_rows, heads, tile_cols), jnp.bfloat16),
            aux,
            aux,
            aux,
            scores,
            scores,
            pltpu.VMEM((patches, patches), jnp.bfloat16),
            decays,
            decays,
            pltpu.VMEM((patches, span_width), jnp.bfloat16),
            pltpu.VMEM((patches, state), jnp.bfloat16),
            pltpu.VMEM((tile_rows, heads, tile_cols), jnp.bfloat16),
            pltpu.VMEM((patches, state), jnp.bfloat16),
            pltpu.VMEM(piece, jnp.bfloat16),
            pltpu.VMEM(piece, jnp.bfloat16),
            pltpu.VMEM(piece, jnp.bfloat16),
            pltpu.VMEM(piece, jnp.bfloat16),
            pltpu.VMEM((patches, span_width), jnp.float32),
            pltpu.VMEM(piece, jnp.float32),
            pltpu.VMEM(piece, jnp.float32),
            pltpu.SemaphoreType.DMA((6,)),
            pltpu.SemaphoreType.DMA((CHUNKS,)),
            pltpu.SemaphoreType.DMA((2,)),
            pltpu.SemaphoreType.DMA((3,)),
            pltpu.SemaphoreType.DMA((2,)),
            pltpu.SemaphoreType.DMA((2,)),
            pltpu.SemaphoreType.DMA((4,)),
            pltpu.SemaphoreType.DMA((CHUNKS,)),
            pltpu.SemaphoreType.DMA((CHUNKS,)),
            pltpu.SemaphoreType.REGULAR,
        ],
        compiler_params=pltpu.CompilerParams(
            collective_id=0, has_side_effects=True, vmem_limit_bytes=60 * 2**20
        ),
    )(
        tile_mask.reshape(-1),
        skip_gain.reshape(1, heads),
        flat(features),
        flat(write_vecs),
        flat(read_vecs),
        jnp.swapaxes(row_decay, 1, 2),
        jnp.swapaxes(col_decay, 1, 2),
    )
    stored = pl.pallas_call(
        finish_kernel,
        out_shape=jax.ShapeDtypeStruct((patches, span_width), jnp.bfloat16),
        in_specs=[vmem] * 4,
        out_specs=pl.BlockSpec(memory_space=pl.ANY),
        scratch_shapes=[
            pltpu.VMEM((patches, width), jnp.bfloat16),
            pltpu.SemaphoreType.DMA((PIECES + 1,)),
        ],
    )(*(pltpu.with_memory_space_constraint(part, pltpu.VMEM) for part in result))
    return stored.reshape(features.shape)


def fits_fused(features, row_decay, tile_mask):
    tile_rows, tile_cols, span_width = features.shape
    devices = lax.axis_size("row")
    return (
        lax.axis_size("col") == 1
        and tile_mask.shape[1] == 1
        and tile_rows * devices == tile_cols
        and devices == 16
        and tile_cols <= 64
        and (tile_rows * (tile_cols // devices)) % 16 == 0
        and span_width % (CHUNKS * 128) == 0
        and (tile_cols // devices) * row_decay.shape[-1] == 128
        and tile_rows * tile_cols % 256 == 0
        and all(
            size.bit_count() == 1
            for size in (tile_rows, tile_cols, devices, span_width // row_decay.shape[-1])
        )
    )


def per_device(features, write_vecs, read_vecs, row_decay, col_decay, tile_mask, skip_gain):
    tile_rows, tile_cols, span_width = features.shape
    if fits_fused(features, row_decay, tile_mask):
        return fused(features, write_vecs, read_vecs, row_decay, col_decay, tile_mask, skip_gain)
    head_count = row_decay.shape[-1]
    block_len = tile_cols // tile_mask.shape[1]
    patch_mask = jnp.repeat(tile_mask, block_len, axis=1)
    masked = jnp.where(patch_mask[..., None] > 0, features, jnp.zeros((), features.dtype))
    moved = (
        lax.all_to_all(masked, "row", split_axis=1, concat_axis=0, tiled=True),
        lax.all_to_all(write_vecs, "row", split_axis=1, concat_axis=0, tiled=True),
        lax.all_to_all(read_vecs, "row", split_axis=1, concat_axis=0, tiled=True),
        lax.all_to_all(col_decay, "row", split_axis=1, concat_axis=0, tiled=True),
    )
    result = column_chains(moved[0], moved[1], moved[2], moved[3], block_len)
    col_out = lax.all_to_all(result, "row", split_axis=0, concat_axis=1, tiled=True)
    local_terms, read_blocks = row_terms(masked, write_vecs, read_vecs, row_decay, block_len)
    if lax.axis_size("col") == 1 and tile_mask.shape[1] == 1:
        y_row = local_terms[0].reshape(features.shape)
    else:
        zero_states = jnp.zeros((tile_rows,) + local_terms[1].shape[2:], jnp.float32)
        closing_states, unused_states = jax.vmap(enter_states)(
            local_terms[2], local_terms[1], zero_states
        )
        device_decay = jnp.prod(local_terms[2], axis=1)
        identity = (jnp.ones_like(device_decay), jnp.zeros_like(closing_states))
        decay_before, state_before = entering_2((device_decay, closing_states), "col", link, identity)
        y_row = row_finish(local_terms, read_blocks, state_before)
    skip_vector = jnp.repeat(skip_gain, span_width // head_count)
    total = y_row + col_out.astype(jnp.float32) + skip_vector * features.astype(jnp.float32)
    return (patch_mask[..., None].astype(jnp.float32) * total).astype(jnp.bfloat16)


def solution(mesh):
    return jax.shard_map(
        per_device,
        mesh=mesh,
        in_specs=(
            P(("slides", "row"), "col", None),
            P(("slides", "row"), "col", None),
            P(("slides", "row"), "col", None),
            P(("slides", "row"), "col", None),
            P(("slides", "row"), "col", None),
            P(("slides", "row"), "col"),
            P(),
        ),
        out_specs=P(("slides", "row"), "col", None),
        check_vma=False,
    )
```
